32 devices in a mesh: section: 2 (over core), req: 4 (over y, x), head: 4 (over z).
Axes of the slice: x: 2, y: 2, z: 4, core: 2. Of those that a mesh axis runs over, the one named last changes fastest.
Arguments:
- tokens: bfloat16 [64, 8192], P(None, 'req'), may hold values from -14 to 14
- attention_gain: bfloat16 [2, 8192], P('section', 'req'), may hold values from 0.099609375 to 1.8984375
- query_key_value_weight: bfloat16 [2, 8192, 8, 1280], P('section', 'req', 'head'), may hold values from -0.0625 to 0.0625
- head_output_weight: bfloat16 [2, 8, 1024, 8192], P('section', 'head', None, 'req'), may hold values from -0.0625 to 0.0625
- feedforward_gain: bfloat16 [2, 8192], P('section', 'req'), may hold values from 0.099609375 to 1.8984375
- gate_up: bfloat16 [2, 8192, 2, 14336], P('section', 'req', None, 'head'), may hold values from -0.0625 to 0.0625
- down_weight: bfloat16 [2, 14336, 8192], P('section', 'head', 'req'), may hold values from -0.046875 to 0.046875
- packed_cache: bfloat16 [2, 8192, 8, 256], P('section', 'req', 'head'), may hold values from -70 to 70
- long_cache: bfloat16 [2, 2, 32768, 8, 256], P('section', None, 'req', 'head'), may hold values from -70 to 70
- lengths: int32 [4, 16], P('req'), may hold values from 1 to 256, 2048 in all within a row
- long_split: int32 [2, 4], P(None, 'req'), may hold values from 1 to 8192, 16384 in all within a row
Outputs:
- layer_outputs: bfloat16 [2, 64, 8192], P('section', None, 'req')
The draws below stay inside these ranges and needn't reach their ends.
Inputs may be any that keep to these rules, and one draw needn't show every extreme that they name: Row g holds the lengths of the 16 requests of request group g in order; they sum to 2048, and the requests' keys fill that group's 2048 slots of packed_cache one request after another. `long_split`: entry (j, g) counts the live slots, the first ones, of group g's 8192 slots of long request j; each row sums to 16384.
All inputs are finite; a program needn't handle non-finite values.
Results may differ from the reference program's by a relative error of at most 0.04.
Values may be sent and summed in bfloat16 or wider, within the bound.
No kernel may reach another device: no remote copies, remote signals or barrier semaphores. Data moves between devices by JAX's collectives and lax.ppermute only.
A program may use at most 192 MiB of HBM per device.

```python
import math
import jax
import jax.numpy as jnp
import numpy as np
from jax import lax

MODEL_WIDTH = 8192
QUERY_HEADS = 64
KEY_VALUE_HEADS = 8
HEAD_SIZE = 128
FF = 14336
GROUP_REQUESTS = 16
LONG = 16384
GROUP_SLOTS = 2048
LONG_GROUP_SLOTS = 8192
REQUEST_COUNT = 64
N_REQ = 4


def cached_value_rows(key, shape):
    base = jnp.clip(jax.random.normal(key, shape, jnp.float32), -6.0, 6.0)
    values = jnp.concatenate([2.0 * base[..., :HEAD_SIZE], 3.0 * base[..., HEAD_SIZE:]], -1)
    return values.astype(jnp.bfloat16)


def draw_packed_cache(key, part):
    return cached_value_rows(jax.random.fold_in(key, 101), (2, N_REQ * GROUP_SLOTS, KEY_VALUE_HEADS, 2 * HEAD_SIZE))


def draw_long_cache(key, part):
    return cached_value_rows(jax.random.fold_in(key, 202), (2, 2, N_REQ * LONG_GROUP_SLOTS, KEY_VALUE_HEADS, 2 * HEAD_SIZE))


def draw_tokens(key, part):
    shape = (REQUEST_COUNT, MODEL_WIDTH)
    fraction = jnp.arange(MODEL_WIDTH).astype(jnp.float32) / (MODEL_WIDTH - 1)
    column_scale = jnp.exp(jnp.log(0.4) + fraction * jnp.log(5.0))
    base = jnp.clip(jax.random.normal(jax.random.fold_in(key, 303), shape, jnp.float32), -6.0, 6.0)
    return (base * column_scale[None, :]).astype(jnp.bfloat16)


def block_levels(own_key, shape, pieces, smallest, largest):
    gain = 1.0
    for dim, parts in pieces:
        steps = jax.random.uniform(jax.random.fold_in(jax.random.fold_in(own_key, 6), dim), (parts,), jnp.float32, smallest / len(pieces), largest / len(pieces))
        gain = gain * jnp.repeat(jnp.exp(steps), shape[dim] // parts).reshape((-1,) + (1,) * (len(shape) - 1 - dim))
    return gain


def profile(count, total, bound, slope):
    loads = [(1 << 20) // math.isqrt(standing ** slope) + 1 for standing in range(2, count + 1)]
    surplus, counts = total - bound - (count - 1), [1] * (count - 1)
    while surplus > 0:
        candidates = [i for i in range(count - 1) if counts[i] < bound]
        mass, remaining = sum([loads[i] for i in candidates]), surplus
        for i in candidates:
            addition = min(bound - counts[i], max(1, remaining * loads[i] // mass), surplus)
            counts[i] = counts[i] + addition
            surplus = surplus - addition
    return np.array([bound] + counts)


def ragged_sizes(stream_key, count, total, most, lean):
    if count == 2:
        one = jax.random.randint(stream_key, (), max(1, total - most), min(most, total - 1) + 1)
        return jnp.stack([one, total - one])
    sizes = jnp.asarray(profile(count, total, most, lean), jnp.int32)
    pairs = (count - 1) // 2
    source_of, sink = sizes[1:1 + 2 * pairs:2], sizes[2:2 + 2 * pairs:2]
    margin = jnp.minimum(source_of - 1, most - sink)
    shifted = jax.random.randint(jax.random.fold_in(stream_key, 1), (pairs,), 0, 1 << 20) % (margin + 1)
    sizes = sizes.at[1:1 + 2 * pairs:2].set(source_of - shifted).at[2:2 + 2 * pairs:2].set(sink + shifted)
    return sizes[jax.random.permutation(jax.random.fold_in(stream_key, 2), count)]


def centred(own_key, shape, scale, most, pieces=(), dtype=jnp.bfloat16):
    array = jax.random.normal(own_key, shape, jnp.float32) * scale
    if len(pieces) > 0:
        array = block_levels(own_key, shape, pieces, -0.22, 0.18) * array
    return jnp.clip(array, min=-most, max=most).astype(dtype)


def setup_inputs(seed: int = 0) -> dict:
    key_of = jax.random.split(jax.random.key(seed), 12)
    tokens = draw_tokens(jax.random.fold_in(key_of[11], 71), 0)
    attention_gain = jnp.clip(1.0 + 0.18 * jax.random.normal(key_of[1], (2, MODEL_WIDTH), jnp.float32), 0.099609375, 1.8984375).astype(jnp.bfloat16)
    query_key_value_weight = centred(key_of[2], (2, MODEL_WIDTH, KEY_VALUE_HEADS, (QUERY_HEADS // KEY_VALUE_HEADS + 2) * HEAD_SIZE), MODEL_WIDTH ** -0.5, 0.0625, ((0, 2), (1, 4), (2, 4)))
    head_output_weight = centred(key_of[3], (2, KEY_VALUE_HEADS, (QUERY_HEADS // KEY_VALUE_HEADS) * HEAD_SIZE, MODEL_WIDTH), (QUERY_HEADS * HEAD_SIZE) ** -0.5, 0.0625, ((0, 2), (1, 4), (3, 4)))
    feedforward_gain = jnp.clip(1.0 + 0.18 * jax.random.normal(key_of[4], (2, MODEL_WIDTH), jnp.float32), 0.099609375, 1.8984375).astype(jnp.bfloat16)
    gate_up = centred(key_of[5], (2, MODEL_WIDTH, 2, FF), MODEL_WIDTH ** -0.5, 0.0625, ((0, 2), (1, 4), (3, 4)))
    down_weight = centred(key_of[6], (2, FF, MODEL_WIDTH), FF ** -0.5, 0.046875, ((0, 2), (1, 4), (2, 4)))
    packed_cache = draw_packed_cache(jax.random.fold_in(key_of[11], 71), 0)
    long_cache = draw_long_cache(jax.random.fold_in(key_of[11], 71), 0)
    lengths = jax.vmap(lambda own: ragged_sizes(own, GROUP_REQUESTS, GROUP_SLOTS, 256, 2))(jax.random.split(key_of[9], N_REQ)).reshape((N_REQ, GROUP_REQUESTS)).astype(jnp.int32)
    long_split = jax.vmap(lambda own: ragged_sizes(own, N_REQ, LONG, LONG_GROUP_SLOTS, 1))(jax.random.split(key_of[10], 2)).reshape((2, N_REQ)).astype(jnp.int32)
    return dict(tokens=tokens, attention_gain=attention_gain, query_key_value_weight=query_key_value_weight, head_output_weight=head_output_weight, feedforward_gain=feedforward_gain, gate_up=gate_up, down_weight=down_weight, packed_cache=packed_cache, long_cache=long_cache, lengths=lengths, long_split=long_split)


EPSILON = 1e-05

def rotate(values, position):
    half_dim = values.shape[-1] // 2
    freq_ids = jnp.arange(half_dim).astype(jnp.float32)
    inverse = 1.0 / 10000.0 ** (freq_ids * 2.0 / values.shape[-1])
    angles = position.astype(jnp.float32)[:, None] * inverse[None, :]
    cosine = jnp.cos(angles)[:, None, None, :]
    sine_part = jnp.sin(angles)[:, None, None, :]
    lower_half = values[..., :half_dim]
    upper_half = values[..., half_dim:]
    return jnp.concatenate([lower_half * cosine - upper_half * sine_part, upper_half * cosine + lower_half * sine_part], -1)

def norm_rows(values, gain_row):
    floats = values.astype(jnp.float32)
    squares = lax.optimization_barrier(jnp.mean(floats * floats, axis=-1, keepdims=True))
    return (floats * lax.rsqrt(squares + EPSILON) * gain_row.astype(jnp.float32)).astype(jnp.bfloat16)

def decoder_layer(inputs, attention_gain, query_key_value_weight, head_output_weight, feedforward_gain, gate_up, down_weight, packed_cache, long_cache, lengths, long_split):
    requests_per_group = QUERY_HEADS // KEY_VALUE_HEADS
    score_scale = 1.0 / math.sqrt(HEAD_SIZE)
    normalized_input = norm_rows(inputs, attention_gain)
    projected_rows = jnp.dot(normalized_input, query_key_value_weight.reshape(MODEL_WIDTH, KEY_VALUE_HEADS * (requests_per_group + 2) * HEAD_SIZE), preferred_element_type=jnp.float32)
    projected_rows = projected_rows.reshape(REQUEST_COUNT, KEY_VALUE_HEADS, requests_per_group + 2, HEAD_SIZE)
    row_ids = jnp.arange(REQUEST_COUNT)
    long_row = (row_ids == 0) | (row_ids == N_REQ // 2 * GROUP_REQUESTS)
    position = lengths.reshape(REQUEST_COUNT) + jnp.where(long_row, LONG, 0).astype(jnp.int32)
    queries = rotate(projected_rows[:, :, :requests_per_group], position).astype(jnp.bfloat16)
    new_key = rotate(projected_rows[:, :, requests_per_group:requests_per_group + 1], position)[:, :, 0].astype(jnp.bfloat16)
    new_value = projected_rows[:, :, requests_per_group + 1].astype(jnp.bfloat16)
    far_keys = long_cache[..., :HEAD_SIZE].astype(jnp.float32)
    far_values = long_cache[..., HEAD_SIZE:].astype(jnp.float32)

    def attend(group_id):
        start_row = group_id * GROUP_REQUESTS
        group_queries = lax.dynamic_slice_in_dim(queries, start_row, GROUP_REQUESTS, 0).astype(jnp.float32)
        group_keys = lax.dynamic_slice_in_dim(new_key, start_row, GROUP_REQUESTS, 0).astype(jnp.float32)
        group_values = lax.dynamic_slice_in_dim(new_value, start_row, GROUP_REQUESTS, 0).astype(jnp.float32)
        group_lengths = lax.dynamic_index_in_dim(lengths, group_id, 0, keepdims=False)
        pack_part = lax.dynamic_slice_in_dim(packed_cache, group_id * GROUP_SLOTS, GROUP_SLOTS, 0).astype(jnp.float32)
        seg_ends = jnp.cumsum(group_lengths)
        slot_ids = jnp.arange(GROUP_SLOTS)
        slot_owner = lax.optimization_barrier(jnp.sum((slot_ids[:, None] >= seg_ends[None, :]).astype(jnp.int32), axis=1))
        in_segment = (slot_owner[None, :] == jnp.arange(GROUP_REQUESTS)[:, None])[:, None, None, :]
        scores = jnp.einsum('rkhd,pkd->rkhp', group_queries, pack_part[..., :HEAD_SIZE]) * score_scale
        own_score = jnp.einsum('rkhd,rkd->rkh', group_queries, group_keys) * score_scale
        long_id = jnp.where(group_id == 0, 0, 1)
        is_long = (group_id == 0) | (group_id == N_REQ // 2)
        split_row = lax.dynamic_index_in_dim(long_split, long_id, 0, keepdims=False)
        far_live = (jnp.arange(LONG_GROUP_SLOTS)[None, :] < split_row[:, None]).reshape(N_REQ * LONG_GROUP_SLOTS) & is_long
        far_key = lax.dynamic_index_in_dim(far_keys, long_id, 0, keepdims=False)
        far_value = lax.dynamic_index_in_dim(far_values, long_id, 0, keepdims=False)
        far_scores = jnp.einsum('khd,pkd->khp', group_queries[0], far_key) * score_scale
        far_live = far_live[None, None, :]
        row_max = jnp.maximum(lax.optimization_barrier(jnp.max(jnp.where(in_segment, scores, -jnp.inf), axis=-1)), own_score)
        far_max = lax.optimization_barrier(jnp.max(jnp.where(far_live, far_scores, -jnp.inf), axis=-1))
        row_max = row_max.at[0].set(jnp.maximum(row_max[0], far_max))
        weights = jnp.where(in_segment, jnp.exp(jnp.where(in_segment, scores - row_max[..., None], 0.0)), 0.0).astype(jnp.bfloat16)
        own_weights = jnp.exp(own_score - row_max).astype(jnp.bfloat16)
        far_weights = jnp.where(far_live, jnp.exp(jnp.where(far_live, far_scores - row_max[0][..., None], 0.0)), 0.0).astype(jnp.bfloat16)
        softmax_total = lax.optimization_barrier(jnp.sum(weights.astype(jnp.float32), axis=-1)) + own_weights.astype(jnp.float32)
        softmax_total = softmax_total.at[0].add(lax.optimization_barrier(jnp.sum(far_weights.astype(jnp.float32), axis=-1)))
        weighted_sum = jnp.einsum('rkhp,pkd->rkhd', weights.astype(jnp.float32), pack_part[..., HEAD_SIZE:])
        weighted_sum = weighted_sum + own_weights.astype(jnp.float32)[..., None] * group_values[:, :, None, :]
        weighted_sum = weighted_sum.at[0].add(jnp.einsum('khp,pkd->khd', far_weights.astype(jnp.float32), far_value))
        return (weighted_sum / softmax_total[..., None]).astype(jnp.bfloat16).reshape(GROUP_REQUESTS, KEY_VALUE_HEADS * requests_per_group * HEAD_SIZE)
    attended_heads = lax.map(attend, jnp.arange(N_REQ)).reshape(REQUEST_COUNT, QUERY_HEADS * HEAD_SIZE)
    attended = jnp.dot(attended_heads, head_output_weight.reshape(QUERY_HEADS * HEAD_SIZE, MODEL_WIDTH), preferred_element_type=jnp.float32)
    residual = (inputs.astype(jnp.float32) + attended).astype(jnp.bfloat16)
    normed_two = norm_rows(residual, feedforward_gain)
    gate_and_up = jnp.dot(normed_two, gate_up.reshape(MODEL_WIDTH, 2 * FF), preferred_element_type=jnp.float32)
    hidden = (jax.nn.silu(gate_and_up[:, :FF]) * gate_and_up[:, FF:]).astype(jnp.bfloat16)
    lowered = jnp.dot(hidden, down_weight, preferred_element_type=jnp.float32)
    return (residual.astype(jnp.float32) + lowered).astype(jnp.bfloat16)

def reference(tokens, attention_gain, query_key_value_weight, head_output_weight, feedforward_gain, gate_up, down_weight, packed_cache, long_cache, lengths, long_split):
    first_out = decoder_layer(tokens, attention_gain[0], query_key_value_weight[0], head_output_weight[0], feedforward_gain[0], gate_up[0], down_weight[0], packed_cache[0], long_cache[0], lengths, long_split)
    second_out = decoder_layer(first_out, attention_gain[1], query_key_value_weight[1], head_output_weight[1], feedforward_gain[1], gate_up[1], down_weight[1], packed_cache[1], long_cache[1], lengths, long_split)
    return jnp.stack([first_out, second_out])
```

```python
import functools
import math

import jax
import jax.numpy as jnp
from jax import lax
from jax.experimental import pallas as pl
from jax.experimental.pallas import tpu as pltpu
from jax.sharding import PartitionSpec as P

MODEL_WIDTH = 8192
QUERY_HEADS = 64
KEY_VALUE_HEADS = 8
HEAD_SIZE = 128
LONG = 16384
FF = 14336
MOST_SLOTS = 256
LANES = 128
COLUMNS = 256
FAR_SLOTS = 1024
LOWEST = -1e30


EPSILON = 1e-05


def merged(part, axis, combine):
    gathered = jax.tree.map(lambda a: lax.all_gather(a, axis), part)

    def take(source):
        return jax.tree.map(lambda a: lax.dynamic_index_in_dim(a, source, 0, False), gathered)

    return lax.fori_loop(
        1, lax.axis_size(axis), lambda source, state: combine(state, take(source)), take(0)
    )


def shifted(value, axis, by):
    peers = lax.axis_size(axis)
    pairs = [(i, i + by) for i in range(peers) if 0 <= i + by < peers]
    return lax.ppermute(value, axis, pairs)


def rotate(values, position):
    half_dim = values.shape[-1] // 2
    freq_ids = jnp.arange(half_dim).astype(jnp.float32)
    inverse = 1.0 / 10000.0 ** (freq_ids * 2.0 / values.shape[-1])
    angles = position.astype(jnp.float32)[:, None] * inverse[None, :]
    cosine = jnp.cos(angles)[:, None, None, :]
    sine_part = jnp.sin(angles)[:, None, None, :]
    lower_half = values[..., :half_dim]
    upper_half = values[..., half_dim:]
    return jnp.concatenate(
        [
            lower_half * cosine - upper_half * sine_part,
            upper_half * cosine + lower_half * sine_part,
        ],
        -1,
    )


def add_pair(earlier, second_part):
    return earlier + second_part


def combine_partial(earlier, second_part):
    peak = jnp.maximum(earlier[0], second_part[0])
    left_factor = jnp.exp(earlier[0] - peak)
    right_factor = jnp.exp(second_part[0] - peak)
    softmax_total = earlier[1] * left_factor + second_part[1] * right_factor
    weighted_sum = earlier[2] * left_factor[..., None] + second_part[2] * right_factor[..., None]
    return (peak, softmax_total, weighted_sum)


def over_requests(values, combiner):
    return merged(values, "req", combiner)


def rows_apply(values, row_fn):
    return row_fn(lax.all_gather(values, "req", axis=0, tiled=True), jnp.int32(0))


def rows_project(term_fn, row_count):
    return lax.psum_scatter(
        term_fn(jnp.int32(0), row_count * lax.axis_size("req")),
        "req",
        scatter_dimension=0,
        tiled=True,
    )


def head_total(values):
    return lax.psum(values, "head")


def keep_rows(piece_rows, start_row):
    return piece_rows


def norm_rows(values, gain_row):
    floats = values.astype(jnp.float32)
    squares = over_requests(jnp.sum(floats * floats, axis=-1), add_pair)
    return (
        floats * lax.rsqrt(squares / MODEL_WIDTH + EPSILON)[:, None] * gain_row.astype(jnp.float32)
    ).astype(jnp.bfloat16)


def decoder_layer(
    inputs,
    micro_batch,
    attention_gain,
    query_key_value_weight,
    head_output_weight,
    feedforward_gain,
    gate_up,
    down_weight,
    packed_cache,
    long_cache,
    lengths,
    long_split,
):
    req_count = lax.axis_size("req")
    group_index = lax.axis_index("req")
    blocks = inputs.shape[0] // req_count
    columns = query_key_value_weight.shape[1]
    kv_local = query_key_value_weight.shape[2]
    requests_per_group = QUERY_HEADS // KEY_VALUE_HEADS
    score_scale = 1.0 / math.sqrt(HEAD_SIZE)
    normalized_input = norm_rows(inputs, attention_gain[0])
    in_weights = query_key_value_weight[0].reshape(
        columns, kv_local * (requests_per_group + 2) * HEAD_SIZE
    )

    def qkv_term(start_row, row_count):
        return jnp.dot(normalized_input, in_weights, preferred_element_type=jnp.float32)

    projected_rows = rows_project(qkv_term, blocks).reshape(
        blocks, kv_local, requests_per_group + 2, HEAD_SIZE
    )
    local_rows = jnp.arange(blocks)
    row_lengths = lengths[0]
    owner_long = (group_index == 0) | (group_index == req_count // 2)
    long_row = (local_rows == 0) & (micro_batch == 0) & owner_long
    position = row_lengths + jnp.where(long_row, LONG, 0).astype(jnp.int32)
    queries = rotate(projected_rows[:, :, :requests_per_group], position).astype(jnp.bfloat16)
    new_key = rotate(projected_rows[:, :, requests_per_group : requests_per_group + 1], position)[
        :, :, 0
    ].astype(jnp.bfloat16)
    new_value = projected_rows[:, :, requests_per_group + 1].astype(jnp.bfloat16)
    gathered = rows_apply(
        queries[0:1].reshape(1, kv_local * requests_per_group * HEAD_SIZE), keep_rows
    )
    long_queries = jnp.stack([gathered[0], gathered[req_count // 2]]).reshape(
        2, kv_local, requests_per_group, HEAD_SIZE
    )
    far_cache = long_cache[0]
    far_live = (jnp.arange(far_cache.shape[1])[None, :] < long_split[:, 0][:, None])[
        :, None, None, :
    ]
    far_scores = (
        jnp.einsum(
            "jkhd,jpkd->jkhp",
            long_queries,
            far_cache[..., :HEAD_SIZE],
            preferred_element_type=jnp.float32,
        )
        * score_scale
    )
    far_max = jnp.max(jnp.where(far_live, far_scores, -jnp.inf), axis=-1)
    far_weights = jnp.where(
        far_live, jnp.exp(jnp.where(far_live, far_scores - far_max[..., None], 0.0)), 0.0
    ).astype(jnp.bfloat16)
    far_totals = jnp.sum(far_weights.astype(jnp.float32), axis=-1)
    far_summed = jnp.einsum(
        "jkhp,jpkd->jkhd",
        far_weights,
        far_cache[..., HEAD_SIZE:],
        preferred_element_type=jnp.float32,
    )
    far_max, far_totals, far_summed = over_requests(
        (far_max, far_totals, far_summed), combine_partial
    )
    far_index = jnp.where(group_index == 0, 0, 1)
    chosen_max = lax.dynamic_index_in_dim(far_max, far_index, 0, keepdims=False)
    chosen_totals = lax.dynamic_index_in_dim(far_totals, far_index, 0, keepdims=False)
    chosen_summed = lax.dynamic_index_in_dim(far_summed, far_index, 0, keepdims=False)
    pack_part = packed_cache[0]
    seg_ends = jnp.cumsum(lengths[0])
    slot_ids = jnp.arange(pack_part.shape[0])
    slot_owner = jnp.sum((slot_ids[:, None] >= seg_ends[None, :]).astype(jnp.int32), axis=1)
    request_ids = micro_batch * blocks + local_rows
    in_segment = (slot_owner[None, :] == request_ids[:, None])[:, None, None, :]
    scores = (
        jnp.einsum(
            "rkhd,pkd->rkhp",
            queries,
            pack_part[..., :HEAD_SIZE],
            preferred_element_type=jnp.float32,
        )
        * score_scale
    )
    own_score = (
        jnp.einsum("rkhd,rkd->rkh", queries, new_key, preferred_element_type=jnp.float32)
        * score_scale
    )
    row_max = jnp.maximum(jnp.max(jnp.where(in_segment, scores, -jnp.inf), axis=-1), own_score)
    long_mask = long_row[:, None, None]
    row_max = jnp.where(long_mask, jnp.maximum(row_max, chosen_max[None]), row_max)
    weights = jnp.where(
        in_segment, jnp.exp(jnp.where(in_segment, scores - row_max[..., None], 0.0)), 0.0
    ).astype(jnp.bfloat16)
    own_weights = jnp.exp(own_score - row_max).astype(jnp.bfloat16)
    far_factor = jnp.where(
        long_mask, jnp.exp(jnp.where(long_mask, chosen_max[None] - row_max, 0.0)), 0.0
    )
    softmax_total = (
        jnp.sum(weights.astype(jnp.float32), axis=-1)
        + own_weights.astype(jnp.float32)
        + far_factor * chosen_totals[None]
    )
    weighted_sum = jnp.einsum(
        "rkhp,pkd->rkhd", weights, pack_part[..., HEAD_SIZE:], preferred_element_type=jnp.float32
    )
    weighted_sum = (
        weighted_sum
        + own_weights.astype(jnp.float32)[..., None] * new_value.astype(jnp.float32)[:, :, None, :]
    )
    weighted_sum = weighted_sum + far_factor[..., None] * chosen_summed[None]
    attended_heads = (
        (weighted_sum / softmax_total[..., None])
        .astype(jnp.bfloat16)
        .reshape(blocks, kv_local * requests_per_group * HEAD_SIZE)
    )
    out_weights = head_output_weight[0].reshape(kv_local * requests_per_group * HEAD_SIZE, columns)

    def project_heads(piece_rows, start_row):
        return jnp.dot(piece_rows, out_weights, preferred_element_type=jnp.float32)

    attended = head_total(rows_apply(attended_heads, project_heads))
    residual = (inputs.astype(jnp.float32) + attended).astype(jnp.bfloat16)
    normed_two = norm_rows(residual, feedforward_gain[0])
    ff_weights = gate_up[0].reshape(columns, -1)

    def ff_term(start_row, row_count):
        return jnp.dot(normed_two, ff_weights, preferred_element_type=jnp.float32)

    gate_and_up = rows_project(ff_term, blocks)
    hidden_width = gate_and_up.shape[1] // 2
    hidden = (jax.nn.silu(gate_and_up[:, :hidden_width]) * gate_and_up[:, hidden_width:]).astype(
        jnp.bfloat16
    )
    lower_weights = down_weight[0]

    def project_hidden(piece_rows, start_row):
        return jnp.dot(piece_rows, lower_weights, preferred_element_type=jnp.float32)

    lowered = head_total(rows_apply(hidden, project_hidden))
    return (residual.astype(jnp.float32) + lowered).astype(jnp.bfloat16)


def local(
    tokens,
    attention_gain,
    query_key_value_weight,
    head_output_weight,
    feedforward_gain,
    gate_up,
    down_weight,
    packed_cache,
    long_cache,
    lengths,
    long_split,
):
    req_count = lax.axis_size("req")
    section_index = lax.axis_index("section")
    batch_count = 1
    per_group = tokens.shape[0] // req_count
    blocks = per_group // batch_count
    columns = tokens.shape[1]
    token_grid = tokens.reshape(req_count, per_group, columns)
    result = jnp.zeros_like(token_grid)
    incoming = jnp.zeros((req_count * blocks, columns), jnp.bfloat16)
    for phase_step in range(batch_count + 1):
        micro_batch = phase_step - section_index
        is_active = (micro_batch >= 0) & (micro_batch < batch_count)
        micro_batch = jnp.clip(micro_batch, 0, batch_count - 1)
        new_batch = token_grid.reshape(req_count * blocks, columns)
        inputs = jnp.where(section_index == 0, new_batch, incoming)
        output = decoder_layer(
            inputs,
            micro_batch,
            attention_gain,
            query_key_value_weight,
            head_output_weight,
            feedforward_gain,
            gate_up,
            down_weight,
            packed_cache,
            long_cache,
            lengths,
            long_split,
        )
        placed = output.reshape(req_count, blocks, columns)
        result = jnp.where(is_active, placed, result)
        if phase_step < batch_count:
            incoming = shifted(output, "section", 1)
    return result.reshape(1, req_count * per_group, columns)

def peer_ids(axis):
    return lax.axis_index(axis), lax.axis_size(axis)


def swap(value, axis, distance, section, target_section=None):
    size = lax.axis_size(axis)
    target_section = section if target_section is None else target_section
    pairs = [(section * size + i, target_section * size + (i ^ distance)) for i in range(size)]
    return lax.ppermute(value, ("section", axis), pairs)


def swap_all(values, axis, section):
    return [values[0]] + [swap(values[d], axis, d, section) for d in range(1, len(values))]


def spread(value, axis, section):
    return swap_all([value] * lax.axis_size(axis), axis, section)


def in_vmem(count):
    return [pl.BlockSpec(memory_space=pltpu.VMEM)] * count


def in_hbm(count):
    return [pl.BlockSpec(memory_space=pltpu.HBM)] * count


def in_smem(count):
    return [pl.BlockSpec(memory_space=pltpu.SMEM)] * count


def params(mebibytes):
    return pltpu.CompilerParams(vmem_limit_bytes=mebibytes * 2**20, has_side_effects=False)


def split_parts(value):
    high = value.astype(jnp.bfloat16)
    low = (value - high.astype(jnp.float32)).astype(jnp.bfloat16)
    return high, low


def sum_columns(values):
    floats = values.astype(jnp.float32)
    squares = jnp.sum(floats * floats, axis=-1, keepdims=True)
    high, low = split_parts(squares)
    lane = lax.broadcasted_iota(jnp.int32, (values.shape[0], LANES), 1)
    return jnp.where(
        lane == 0, high.astype(jnp.float32), jnp.where(lane == 1, low.astype(jnp.float32), 0.0)
    )


def row_scale(parts):
    total = sum(jnp.sum(part.astype(jnp.float32), axis=-1, keepdims=True) for part in parts)
    return lax.rsqrt(total / MODEL_WIDTH + EPSILON)


def expand_rows(scaled_ref, wide_ref):
    rows, columns = scaled_ref.shape
    chunk = 2 * LANES
    source = lax.broadcasted_iota(jnp.int32, (chunk, 2 * chunk), 0)
    target = lax.broadcasted_iota(jnp.int32, (chunk, 2 * chunk), 1)
    for half in range(2):
        select = jnp.where(target == 2 * source + half, 1.0, 0.0).astype(jnp.bfloat16)
        for c in range(columns // chunk):
            wide_ref[half * rows : (half + 1) * rows, 2 * c * chunk : 2 * (c + 1) * chunk] = jnp.dot(
                scaled_ref[:, c * chunk : (c + 1) * chunk],
                select,
                preferred_element_type=jnp.float32,
            ).astype(jnp.bfloat16)


def gather_columns(piece_refs, whole_ref, index):
    width = piece_refs[0].shape[1]
    for d, piece in enumerate(piece_refs):
        start = pl.multiple_of(lax.bitwise_xor(index, d) * width, LANES)
        whole_ref[:, pl.ds(start, width)] = piece[...]


def qkv_kernel(pieces, peers, *refs):
    piece_refs = refs[:pieces]
    gain_ref, weight_ref = refs[pieces : pieces + 2]
    outs = refs[pieces + 2 : pieces + 2 + peers]
    whole, scaled, wide, weights, total, sems = refs[pieces + 2 + peers :]
    group = lax.axis_index("req")
    rows = whole.shape[0]
    blocks = rows // peers
    width = weight_ref.shape[3]
    chunks = width // COLUMNS

    def copy(c):
        return pltpu.make_async_copy(
            weight_ref.at[0, :, :, pl.ds(c * COLUMNS, COLUMNS)], weights.at[c], sems.at[c]
        )

    for c in range(chunks):
        copy(c).start()
    gather_columns(piece_refs, whole, lax.axis_index("head"))
    scaled[...] = (
        whole[...].astype(jnp.float32) * gain_ref[...].astype(jnp.float32)
    ).astype(jnp.bfloat16)
    sums = sum_columns(whole[...])
    total[0:rows, width:] = sums
    total[rows:, width:] = sums
    expand_rows(scaled, wide)
    for c in range(chunks):
        copy(c).wait()
        total[:, c * COLUMNS : (c + 1) * COLUMNS] = jnp.dot(
            wide[...],
            weights[c].reshape(wide.shape[1], COLUMNS),
            preferred_element_type=jnp.float32,
        )
    far = peers // 2 * blocks
    filler = jnp.zeros((blocks - 4, total.shape[1]), jnp.float32)
    long_rows = jnp.concatenate(
        [
            total[0:1],
            total[far : far + 1],
            total[rows : rows + 1],
            total[rows + far : rows + far + 1],
            filler,
        ],
        0,
    ).astype(jnp.bfloat16)
    for d in range(peers):
        start = pl.multiple_of(lax.bitwise_xor(group, d) * blocks, blocks)
        outs[d][0:blocks] = total[pl.ds(start, blocks)].astype(jnp.bfloat16)
        outs[d][blocks : 2 * blocks] = total[pl.ds(rows + start, blocks)].astype(jnp.bfloat16)
        outs[d][2 * blocks :] = long_rows


def project_qkv(pieces, gain, weight, peers):
    rows = pieces[0].shape[0]
    depth, pair, width = weight.shape[1:]
    blocks = rows // peers
    return pl.pallas_call(
        functools.partial(qkv_kernel, len(pieces), peers),
        out_shape=[jax.ShapeDtypeStruct((3 * blocks, width + LANES), jnp.bfloat16)] * peers,
        in_specs=in_vmem(len(pieces) + 1) + in_hbm(1),
        out_specs=in_vmem(peers),
        scratch_shapes=[
            pltpu.VMEM((rows, depth), jnp.bfloat16),
            pltpu.VMEM((rows, depth), jnp.bfloat16),
            pltpu.VMEM((pair * rows, pair * depth), jnp.bfloat16),
            pltpu.VMEM((width // COLUMNS, depth, pair, COLUMNS), jnp.bfloat16),
            pltpu.VMEM((pair * rows, width + LANES), jnp.float32),
            pltpu.SemaphoreType.DMA((width // COLUMNS,)),
        ],
        compiler_params=params(24),
        name="project_qkv",
    )(*pieces, gain, weight)


def attention_kernel(peers, *refs):
    piece_refs = refs[:peers]
    cosine_ref, sine_ref, starts, lengths, split, packed_ref, long_ref = refs[peers : peers + 7]
    out_ref = refs[peers + 7]
    (rope, packed, far, queries, keys, values, scores, far_scores, merged_rows, packed_sem, far_sems) = (
        refs[peers + 8 :]
    )
    group = lax.axis_index("req")
    blocks = out_ref.shape[0] // 2
    heads = QUERY_HEADS // KEY_VALUE_HEADS
    pairs = 2 * heads
    window = scores.shape[2] // 2
    slots = packed.shape[0]
    far_chunks = far.shape[1] // FAR_SLOTS
    scale = 1.0 / math.sqrt(HEAD_SIZE)
    live = [split[0, 0], split[1, 0]]

    def far_copy(j, c):
        return pltpu.make_async_copy(
            long_ref.at[0, j, pl.ds(c * FAR_SLOTS, FAR_SLOTS)],
            far.at[j, pl.ds(c * FAR_SLOTS, FAR_SLOTS)],
            far_sems.at[j, c],
        )

    packed_copy = pltpu.make_async_copy(packed_ref.at[0], packed, packed_sem)
    packed_copy.start()
    for j in range(2):
        for c in range(far_chunks):

            @pl.when(c * FAR_SLOTS < live[j])
            def _():
                far_copy(j, c).start()

    width = cosine_ref.shape[1] * (heads + 2)
    scale_rows = row_scale([piece[:, width:] for piece in piece_refs])
    cosine, sine = cosine_ref[...], sine_ref[...]
    for b in range(heads + 2):
        lanes = slice(b * HEAD_SIZE, (b + 1) * HEAD_SIZE)
        block = sum(piece[:, lanes].astype(jnp.float32) for piece in piece_refs) * scale_rows
        if b <= heads:
            block = block * cosine + pltpu.roll(block, HEAD_SIZE // 2, 1) * sine
        block = block.astype(jnp.bfloat16).astype(jnp.float32)
        rope[:, lanes] = block
        for k in range(2):
            own_rows = block[k * blocks : (k + 1) * blocks]
            if b < heads:
                queries[:, k * heads + b, :] = own_rows
            else:
                for h in range(heads):
                    (keys if b == heads else values)[:, k * heads + h, :] = own_rows

    def same_head(columns):
        row = lax.broadcasted_iota(jnp.int32, (pairs, columns), 0)
        column = lax.broadcasted_iota(jnp.int32, (pairs, columns), 1)
        return (row // heads) == (column % 2), column // 2

    def contract(a, b):
        return lax.dot_general(a, b, (((1,), (1,)), ((), ())), preferred_element_type=jnp.float32)

    packed_copy.wait()
    matching, slot = same_head(2 * window)
    first_slots = []
    for r in range(blocks):
        first = jnp.minimum(starts[r], slots - window)
        first_slots.append(first)
        low = starts[r] - first
        segment = packed[pl.ds(first, window), :, 0:HEAD_SIZE].reshape(2 * window, HEAD_SIZE)
        own = contract(queries[r].astype(jnp.bfloat16), segment) * scale
        inside = matching & (slot >= low) & (slot < low + lengths[r])
        scores[r] = jnp.where(inside, own, LOWEST)
    own_score = jnp.sum(queries[...] * keys[...], axis=-1, keepdims=True) * scale
    row_max = jnp.maximum(jnp.max(scores[...], axis=-1, keepdims=True), own_score)
    weights = jnp.exp(scores[...] - row_max).astype(jnp.bfloat16)
    own_weight = jnp.exp(own_score - row_max).astype(jnp.bfloat16).astype(jnp.float32)
    totals = jnp.sum(weights.astype(jnp.float32), axis=-1, keepdims=True) + own_weight
    near_peak = row_max[0] + jnp.log(totals[0])
    for r in range(blocks):
        segment = packed[pl.ds(first_slots[r], window), :, HEAD_SIZE:].reshape(2 * window, HEAD_SIZE)
        summed = jnp.dot(weights[r], segment, preferred_element_type=jnp.float32)
        summed = summed + own_weight[r] * values[r]
        merged_rows[r] = summed / totals[r]

    matching, slot = same_head(2 * FAR_SLOTS)
    for j in range(2):
        long_rows = jnp.concatenate(
            [
                rope[2 * blocks + 2 * k + j : 2 * blocks + 2 * k + j + 1, h * HEAD_SIZE : (h + 1) * HEAD_SIZE]
                for k in range(2)
                for h in range(heads)
            ],
            0,
        ).astype(jnp.bfloat16)
        count = (live[j] + FAR_SLOTS - 1) // FAR_SLOTS

        def score(c, peak):
            far_copy(j, c).wait()
            chunk = far[j, pl.ds(c * FAR_SLOTS, FAR_SLOTS), :, 0:HEAD_SIZE].reshape(
                2 * FAR_SLOTS, HEAD_SIZE
            )
            found = contract(long_rows, chunk) * scale
            found = jnp.where(matching & (slot < live[j] - c * FAR_SLOTS), found, LOWEST)
            far_scores[c] = found
            return jnp.maximum(peak, jnp.max(found, axis=-1, keepdims=True))

        peak = lax.fori_loop(0, count, score, jnp.full((pairs, 1), LOWEST, jnp.float32))

        def weigh(c, state):
            total, summed = state
            weight = jnp.exp(far_scores[c] - peak).astype(jnp.bfloat16)
            chunk = far[j, pl.ds(c * FAR_SLOTS, FAR_SLOTS), :, HEAD_SIZE:].reshape(
                2 * FAR_SLOTS, HEAD_SIZE
            )
            total = total + jnp.sum(weight.astype(jnp.float32), axis=-1, keepdims=True)
            return total, summed + jnp.dot(weight, chunk, preferred_element_type=jnp.float32)

        total, summed = lax.fori_loop(
            0,
            count,
            weigh,
            (jnp.zeros((pairs, 1), jnp.float32), jnp.zeros((pairs, HEAD_SIZE), jnp.float32)),
        )
        far_peak = peak + jnp.log(total)
        result = summed / total
        owner = group == j * (peers // 2)
        top = jnp.maximum(far_peak, near_peak)
        far_part = jnp.exp(far_peak - top)
        near_part = jnp.exp(near_peak - top)
        both = far_part + near_part
        result = jnp.where(owner, (result * far_part + merged_rows[0] * near_part) / both, result)
        log_total = jnp.where(owner, top + jnp.log(both), far_peak)
        high, low = split_parts(log_total)
        merged_rows[blocks + j] = result
        merged_rows[blocks + 2 + j] = jnp.broadcast_to(high.astype(jnp.float32), result.shape)
        merged_rows[blocks + 4 + j] = jnp.broadcast_to(low.astype(jnp.float32), result.shape)
    merged_rows[blocks + 6 :] = jnp.zeros((blocks - 6, pairs, HEAD_SIZE), jnp.float32)
    for b in range(pairs):
        out_ref[:, b * HEAD_SIZE : (b + 1) * HEAD_SIZE] = merged_rows[:, b, :].astype(jnp.bfloat16)


def attend(pieces, cosine, sine, starts, lengths, split, packed_cache, long_cache):
    peers = len(pieces)
    blocks = pieces[0].shape[0] // 3
    heads = QUERY_HEADS // KEY_VALUE_HEADS
    pairs = 2 * heads
    slots = packed_cache.shape[1]
    far_slots = long_cache.shape[2]
    return pl.pallas_call(
        functools.partial(attention_kernel, peers),
        out_shape=jax.ShapeDtypeStruct((2 * blocks, pairs * HEAD_SIZE), jnp.bfloat16),
        in_specs=in_vmem(peers + 2) + in_smem(3) + in_hbm(2),
        out_specs=pl.BlockSpec(memory_space=pltpu.VMEM),
        scratch_shapes=[
            pltpu.VMEM((3 * blocks, (heads + 2) * HEAD_SIZE), jnp.float32),
            pltpu.VMEM((slots, 2, 2 * HEAD_SIZE), jnp.bfloat16),
            pltpu.VMEM((2, far_slots, 2, 2 * HEAD_SIZE), jnp.bfloat16),
            pltpu.VMEM((blocks, pairs, HEAD_SIZE), jnp.float32),
            pltpu.VMEM((blocks, pairs, HEAD_SIZE), jnp.float32),
            pltpu.VMEM((blocks, pairs, HEAD_SIZE), jnp.float32),
            pltpu.VMEM((blocks, pairs, 2 * MOST_SLOTS), jnp.float32),
            pltpu.VMEM((far_slots // FAR_SLOTS, pairs, 2 * FAR_SLOTS), jnp.float32),
            pltpu.VMEM((2 * blocks, pairs, HEAD_SIZE), jnp.float32),
            pltpu.SemaphoreType.DMA,
            pltpu.SemaphoreType.DMA((2, far_slots // FAR_SLOTS)),
        ],
        compiler_params=params(36),
        name="attend",
    )(*pieces, cosine, sine, starts, lengths, split, packed_cache, long_cache)


def column_copies(weight_at, weights, sems, order, width):
    per_peer = width // COLUMNS
    copies = []
    for place, peer in enumerate(order):
        for c in range(per_peer):
            slot = place * per_peer + c
            start = pl.multiple_of(peer * width + c * COLUMNS, LANES)
            copies.append(
                pltpu.make_async_copy(
                    weight_at.at[:, pl.ds(start, COLUMNS)], weights.at[slot], sems.at[slot]
                )
            )
    for copy in copies:
        copy.start()
    return copies


def head_sums(copies, rows_ref, weights, outs):
    per_peer = len(copies) // len(outs)
    for slot, copy in enumerate(copies):
        copy.wait()
        out = outs[len(outs) - 1 - slot // per_peer]
        c = slot % per_peer
        out[:, c * COLUMNS : (c + 1) * COLUMNS] = jnp.dot(
            rows_ref[...], weights[slot], preferred_element_type=jnp.float32
        ).astype(out.dtype)


def output_kernel(peers, head_peers, *refs):
    piece_refs = refs[:peers]
    weight_ref = refs[peers]
    outs = refs[peers + 1 : peers + 1 + head_peers]
    whole, weights, sems = refs[peers + 1 + head_peers :]
    group, place = lax.axis_index("req"), lax.axis_index("head")
    blocks = piece_refs[0].shape[0] // 2
    order = [lax.bitwise_xor(place, d) for d in reversed(range(head_peers))]
    copies = column_copies(weight_ref, weights, sems, order, outs[0].shape[1])
    for d, piece in enumerate(piece_refs):
        start = pl.multiple_of(lax.bitwise_xor(group, d) * blocks, blocks)
        whole[pl.ds(start, blocks)] = piece[0:blocks]
    extras = [piece[blocks:].astype(jnp.float32) for piece in piece_refs]
    for j in range(2):
        peaks = [e[2 + j : 3 + j] + e[4 + j : 5 + j] for e in extras]
        top = functools.reduce(jnp.maximum, peaks)
        parts = [jnp.exp(peak - top) for peak in peaks]
        merged_row = sum(e[j : j + 1] * part for e, part in zip(extras, parts)) / sum(parts)
        rows = slice(j * (peers // 2) * blocks, j * (peers // 2) * blocks + blocks)
        row = lax.broadcasted_iota(jnp.int32, (blocks, whole.shape[1]), 0)
        whole[rows] = jnp.where(
            row == 0, merged_row, whole[rows].astype(jnp.float32)
        ).astype(jnp.bfloat16)
    head_sums(copies, whole, weights, outs)


def project_output(pieces, weight, head_peers):
    peers = len(pieces)
    rows = peers * pieces[0].shape[0] // 2
    depth, width = weight.shape
    chunks = width // COLUMNS
    shape = (rows, width // head_peers)
    return pl.pallas_call(
        functools.partial(output_kernel, peers, head_peers),
        out_shape=[jax.ShapeDtypeStruct(shape, jnp.bfloat16)] * head_peers,
        in_specs=in_vmem(peers) + in_hbm(1),
        out_specs=in_vmem(head_peers),
        scratch_shapes=[
            pltpu.VMEM((rows, depth), jnp.bfloat16),
            pltpu.VMEM((chunks, depth, COLUMNS), jnp.bfloat16),
            pltpu.SemaphoreType.DMA((chunks,)),
        ],
        compiler_params=params(16),
        name="project_output",
    )(*pieces, weight)


def gate_up_kernel(pieces, peers, *refs):
    piece_refs = refs[:pieces]
    gain_ref, weight_ref = refs[pieces : pieces + 2]
    outs = refs[pieces + 2 : pieces + 2 + peers]
    whole, scaled, wide, weights, total, sems = refs[pieces + 2 + peers :]
    group = lax.axis_index("req")
    rows = whole.shape[0]
    chunks = weights.shape[0]

    def copy(c):
        return pltpu.make_async_copy(
            weight_ref.at[0, :, :, pl.ds(c * COLUMNS, COLUMNS)], weights.at[c], sems.at[c]
        )

    for c in range(chunks):
        copy(c).start()
    gather_columns(piece_refs, whole, lax.axis_index("head"))
    scaled[...] = (
        whole[...].astype(jnp.float32) * gain_ref[...].astype(jnp.float32)
    ).astype(jnp.bfloat16)
    sums = sum_columns(whole[...]).astype(jnp.bfloat16)
    expand_rows(scaled, wide)

    @pl.loop(0, chunks)
    def _(c):
        copy(c).wait()
        start = pl.multiple_of(c * COLUMNS, COLUMNS)
        total[:, pl.ds(start, COLUMNS)] = jnp.dot(
            wide[...],
            weights[c].reshape(wide.shape[1], COLUMNS),
            preferred_element_type=jnp.float32,
        ).astype(jnp.bfloat16)

    width = total.shape[1] // peers
    for d in range(peers):
        start = pl.multiple_of(lax.bitwise_xor(group, d) * width, LANES)
        outs[d][:, 0:width] = total[:, pl.ds(start, width)]
        outs[d][0:rows, width:] = sums
        outs[d][rows:, width:] = sums


def project_gate_up(pieces, gain, weight, peers):
    rows = pieces[0].shape[0]
    depth, pair, width = weight.shape[1:]
    chunks = width // COLUMNS
    return pl.pallas_call(
        functools.partial(gate_up_kernel, len(pieces), peers),
        out_shape=[jax.ShapeDtypeStruct((pair * rows, width // peers + LANES), jnp.bfloat16)] * peers,
        in_specs=in_vmem(len(pieces) + 1) + in_hbm(1),
        out_specs=in_vmem(peers),
        scratch_shapes=[
            pltpu.VMEM((rows, depth), jnp.bfloat16),
            pltpu.VMEM((rows, depth), jnp.bfloat16),
            pltpu.VMEM((pair * rows, pair * depth), jnp.bfloat16),
            pltpu.VMEM((chunks, depth, pair, COLUMNS), jnp.bfloat16),
            pltpu.VMEM((pair * rows, width), jnp.bfloat16),
            pltpu.SemaphoreType.DMA((chunks,)),
        ],
        compiler_params=params(44),
        name="project_gate_up",
    )(*pieces, gain, weight)


def hidden_kernel(peers, *refs):
    piece_refs, out_ref = refs[:peers], refs[peers]
    rows, width = out_ref.shape
    factor = row_scale([piece[0:rows, width:] for piece in piece_refs])

    def summed(rows_of):
        return sum(piece[rows_of, 0:width].astype(jnp.float32) for piece in piece_refs) * factor

    gate, up = summed(slice(0, rows)), summed(slice(rows, 2 * rows))
    out_ref[...] = (gate / (1.0 + jnp.exp(-gate)) * up).astype(jnp.bfloat16)


def gated_units(pieces):
    rows, width = pieces[0].shape[0] // 2, pieces[0].shape[1] - LANES
    return pl.pallas_call(
        functools.partial(hidden_kernel, len(pieces)),
        out_shape=jax.ShapeDtypeStruct((rows, width), jnp.bfloat16),
        in_specs=in_vmem(len(pieces)),
        out_specs=pl.BlockSpec(memory_space=pltpu.VMEM),
        compiler_params=params(8),
        name="gated_units",
    )(*pieces)


def down_kernel(peers, head_peers, *refs):
    piece_refs = refs[:peers]
    weight_ref = refs[peers]
    outs = refs[peers + 1 : peers + 1 + head_peers]
    whole, weights, sems = refs[peers + 1 + head_peers :]
    place = lax.axis_index("head")
    order = [lax.bitwise_xor(place, d) for d in reversed(range(head_peers))]
    copies = column_copies(weight_ref.at[0], weights, sems, order, outs[0].shape[1])
    gather_columns(piece_refs, whole, lax.axis_index("req"))
    head_sums(copies, whole, weights, outs)


def project_down(pieces, weight, head_peers):
    peers = len(pieces)
    rows = pieces[0].shape[0]
    depth, width = weight.shape[1:]
    chunks = width // COLUMNS
    shape = (rows, width // head_peers)
    return pl.pallas_call(
        functools.partial(down_kernel, peers, head_peers),
        out_shape=[jax.ShapeDtypeStruct(shape, jnp.bfloat16)] * head_peers,
        in_specs=in_vmem(peers) + in_hbm(1),
        out_specs=in_vmem(head_peers),
        scratch_shapes=[
            pltpu.VMEM((rows, depth), jnp.bfloat16),
            pltpu.VMEM((chunks, depth, COLUMNS), jnp.bfloat16),
            pltpu.SemaphoreType.DMA((chunks,)),
        ],
        compiler_params=params(24),
        name="project_down",
    )(*pieces, weight)


def add_terms(base, terms):
    return (
        base.astype(jnp.float32) + sum(term.astype(jnp.float32) for term in terms)
    ).astype(jnp.bfloat16)


def place_columns(pieces, index):
    stacked = jnp.stack(pieces)
    size = len(pieces)
    ordered = jnp.stack(
        [lax.dynamic_index_in_dim(stacked, lax.bitwise_xor(index, p), 0, False) for p in range(size)],
        1,
    )
    return ordered.reshape(pieces[0].shape[0], -1)


def fast_layer(section, base, pieces, attention_gain, query_key_value_weight, head_output_weight, feedforward_gain, gate_up, down_weight, packed_cache, long_cache, tables):
    req_count, head_count = lax.axis_size("req"), lax.axis_size("head")
    terms = project_qkv(pieces, attention_gain, query_key_value_weight, req_count)
    own = attend(swap_all(terms, "req", section), *tables, packed_cache, long_cache)
    out_weight = head_output_weight.reshape(-1, head_output_weight.shape[3])
    terms = project_output(spread(own, "req", section), out_weight, head_count)
    residual = add_terms(base, swap_all(terms, "head", section))
    terms = project_gate_up(spread(residual, "head", section), feedforward_gain, gate_up, req_count)
    hidden = gated_units(swap_all(terms, "req", section))
    terms = project_down(spread(hidden, "req", section), down_weight, head_count)
    return add_terms(residual, swap_all(terms, "head", section))


def rope_tables(lengths, long_split):
    req_count, group = lax.axis_size("req"), lax.axis_index("req")
    blocks = lengths.shape[1]
    first = lengths[:, :1]
    others = [lax.ppermute(first, "req", [(i, i ^ d) for i in range(req_count)]) for d in range(1, req_count)]
    firsts = jnp.concatenate([first] + others, 1)[0]
    far = [lax.dynamic_index_in_dim(firsts, lax.bitwise_xor(group, j * (req_count // 2)), 0, False) for j in range(2)]
    owner = (group == 0) | (group == req_count // 2)
    own = lengths[0] + jnp.where((jnp.arange(blocks) == 0) & owner, LONG, 0).astype(jnp.int32)
    long_positions = jnp.stack(far + far) + LONG
    position = jnp.concatenate([own, own, long_positions, jnp.zeros((blocks - 4,), jnp.int32)])
    half_dim = HEAD_SIZE // 2
    inverse = 1.0 / 10000.0 ** (jnp.arange(half_dim).astype(jnp.float32) * 2.0 / HEAD_SIZE)
    angles = position.astype(jnp.float32)[:, None] * inverse[None, :]
    cosine, sine = jnp.cos(angles), jnp.sin(angles)
    starts = jnp.cumsum(lengths[0]) - lengths[0]
    return (
        jnp.concatenate([cosine, cosine], 1),
        jnp.concatenate([-sine, sine], 1),
        starts,
        lengths[0],
        long_split,
    )


def fast_local(tokens, attention_gain, query_key_value_weight, head_output_weight, feedforward_gain, gate_up, down_weight, packed_cache, long_cache, lengths, long_split):
    section_index = lax.axis_index("section")
    place, head_count = lax.axis_index("head"), lax.axis_size("head")
    own_width = tokens.shape[1] // head_count
    layer_arrays = (
        attention_gain,
        query_key_value_weight,
        head_output_weight,
        feedforward_gain,
        gate_up,
        down_weight,
        packed_cache,
        long_cache,
        rope_tables(lengths, long_split),
    )
    base = lax.dynamic_slice_in_dim(tokens, place * own_width, own_width, 1)
    token_pieces = [
        lax.dynamic_slice_in_dim(tokens, lax.bitwise_xor(place, d) * own_width, own_width, 1)
        for d in range(head_count)
    ]
    first = fast_layer(0, base, token_pieces, *layer_arrays)
    crossed = [swap(first, "head", d, 0, 1) for d in range(head_count)]
    second = fast_layer(1, crossed[0], crossed, *layer_arrays)
    first_pieces = spread(first, "head", 0)
    second_pieces = spread(second, "head", 1)
    kept = [jnp.where(section_index == 0, a, b) for a, b in zip(first_pieces, second_pieces)]
    return place_columns(kept, place)[None]


def is_power_of_two(value):
    return value & (value - 1) == 0


def fits_fast(mesh):
    req_count, head_count = mesh.shape["req"], mesh.shape["head"]
    columns = MODEL_WIDTH // req_count
    return (
        mesh.shape["section"] == 2
        and is_power_of_two(req_count)
        and is_power_of_two(head_count)
        and KEY_VALUE_HEADS == 2 * head_count
        and columns % (head_count * COLUMNS) == 0
        and FF % (head_count * COLUMNS) == 0
        and FF % (head_count * req_count * LANES) == 0
    )


def solution(mesh):
    placed = (
        P(None, "req"),
        P("section", "req"),
        P("section", "req", "head", None),
        P("section", "head", None, "req"),
        P("section", "req"),
        P("section", "req", None, "head"),
        P("section", "head", "req"),
        P("section", "req", "head", None),
        P("section", None, "req", "head", None),
        P("req", None),
        P(None, "req"),
    )
    return jax.shard_map(
        fast_local if fits_fast(mesh) else local,
        mesh=mesh,
        in_specs=placed, out_specs=P("section", None, "req"), check_vma=False
    )
```

```python
import functools
import math

import jax
import jax.numpy as jnp
from jax import lax
from jax.experimental import pallas as pl
from jax.experimental.pallas import tpu as pltpu
from jax.sharding import PartitionSpec as P

MODEL_WIDTH = 8192
QUERY_HEADS = 64
KEY_VALUE_HEADS = 8
HEAD_SIZE = 128
LONG = 16384
FF = 14336
MOST_SLOTS = 256
LANES = 128
COLUMNS = 512
VMEM_MEBIBYTES = 54
FAR_SLOTS = 1024
LOWEST = -1e30


EPSILON = 1e-05


def merged(part, axis, combine):
    gathered = jax.tree.map(lambda a: lax.all_gather(a, axis), part)

    def take(source):
        return jax.tree.map(lambda a: lax.dynamic_index_in_dim(a, source, 0, False), gathered)

    return lax.fori_loop(
        1, lax.axis_size(axis), lambda source, state: combine(state, take(source)), take(0)
    )


def shifted(value, axis, by):
    peers = lax.axis_size(axis)
    pairs = [(i, i + by) for i in range(peers) if 0 <= i + by < peers]
    return lax.ppermute(value, axis, pairs)


def rotate(values, position):
    half_dim = values.shape[-1] // 2
    freq_ids = jnp.arange(half_dim).astype(jnp.float32)
    inverse = 1.0 / 10000.0 ** (freq_ids * 2.0 / values.shape[-1])
    angles = position.astype(jnp.float32)[:, None] * inverse[None, :]
    cosine = jnp.cos(angles)[:, None, None, :]
    sine_part = jnp.sin(angles)[:, None, None, :]
    lower_half = values[..., :half_dim]
    upper_half = values[..., half_dim:]
    return jnp.concatenate(
        [
            lower_half * cosine - upper_half * sine_part,
            upper_half * cosine + lower_half * sine_part,
        ],
        -1,
    )


def add_pair(earlier, second_part):
    return earlier + second_part


def combine_partial(earlier, second_part):
    peak = jnp.maximum(earlier[0], second_part[0])
    left_factor = jnp.exp(earlier[0] - peak)
    right_factor = jnp.exp(second_part[0] - peak)
    softmax_total = earlier[1] * left_factor + second_part[1] * right_factor
    weighted_sum = earlier[2] * left_factor[..., None] + second_part[2] * right_factor[..., None]
    return (peak, softmax_total, weighted_sum)


def over_requests(values, combiner):
    return merged(values, "req", combiner)


def rows_apply(values, row_fn):
    return row_fn(lax.all_gather(values, "req", axis=0, tiled=True), jnp.int32(0))


def rows_project(term_fn, row_count):
    return lax.psum_scatter(
        term_fn(jnp.int32(0), row_count * lax.axis_size("req")),
        "req",
        scatter_dimension=0,
        tiled=True,
    )


def head_total(values):
    return lax.psum(values, "head")


def keep_rows(piece_rows, start_row):
    return piece_rows


def norm_rows(values, gain_row):
    floats = values.astype(jnp.float32)
    squares = over_requests(jnp.sum(floats * floats, axis=-1), add_pair)
    return (
        floats * lax.rsqrt(squares / MODEL_WIDTH + EPSILON)[:, None] * gain_row.astype(jnp.float32)
    ).astype(jnp.bfloat16)


def decoder_layer(
    inputs,
    micro_batch,
    attention_gain,
    query_key_value_weight,
    head_output_weight,
    feedforward_gain,
    gate_up,
    down_weight,
    packed_cache,
    long_cache,
    lengths,
    long_split,
):
    req_count = lax.axis_size("req")
    group_index = lax.axis_index("req")
    blocks = inputs.shape[0] // req_count
    columns = query_key_value_weight.shape[1]
    kv_local = query_key_value_weight.shape[2]
    requests_per_group = QUERY_HEADS // KEY_VALUE_HEADS
    score_scale = 1.0 / math.sqrt(HEAD_SIZE)
    normalized_input = norm_rows(inputs, attention_gain[0])
    in_weights = query_key_value_weight[0].reshape(
        columns, kv_local * (requests_per_group + 2) * HEAD_SIZE
    )

    def qkv_term(start_row, row_count):
        return jnp.dot(normalized_input, in_weights, preferred_element_type=jnp.float32)

    projected_rows = rows_project(qkv_term, blocks).reshape(
        blocks, kv_local, requests_per_group + 2, HEAD_SIZE
    )
    local_rows = jnp.arange(blocks)
    row_lengths = lengths[0]
    owner_long = (group_index == 0) | (group_index == req_count // 2)
    long_row = (local_rows == 0) & (micro_batch == 0) & owner_long
    position = row_lengths + jnp.where(long_row, LONG, 0).astype(jnp.int32)
    queries = rotate(projected_rows[:, :, :requests_per_group], position).astype(jnp.bfloat16)
    new_key = rotate(projected_rows[:, :, requests_per_group : requests_per_group + 1], position)[
        :, :, 0
    ].astype(jnp.bfloat16)
    new_value = projected_rows[:, :, requests_per_group + 1].astype(jnp.bfloat16)
    gathered = rows_apply(
        queries[0:1].reshape(1, kv_local * requests_per_group * HEAD_SIZE), keep_rows
    )
    long_queries = jnp.stack([gathered[0], gathered[req_count // 2]]).reshape(
        2, kv_local, requests_per_group, HEAD_SIZE
    )
    far_cache = long_cache[0]
    far_live = (jnp.arange(far_cache.shape[1])[None, :] < long_split[:, 0][:, None])[
        :, None, None, :
    ]
    far_scores = (
        jnp.einsum(
            "jkhd,jpkd->jkhp",
            long_queries,
            far_cache[..., :HEAD_SIZE],
            preferred_element_type=jnp.float32,
        )
        * score_scale
    )
    far_max = jnp.max(jnp.where(far_live, far_scores, -jnp.inf), axis=-1)
    far_weights = jnp.where(
        far_live, jnp.exp(jnp.where(far_live, far_scores - far_max[..., None], 0.0)), 0.0
    ).astype(jnp.bfloat16)
    far_totals = jnp.sum(far_weights.astype(jnp.float32), axis=-1)
    far_summed = jnp.einsum(
        "jkhp,jpkd->jkhd",
        far_weights,
        far_cache[..., HEAD_SIZE:],
        preferred_element_type=jnp.float32,
    )
    far_max, far_totals, far_summed = over_requests(
        (far_max, far_totals, far_summed), combine_partial
    )
    far_index = jnp.where(group_index == 0, 0, 1)
    chosen_max = lax.dynamic_index_in_dim(far_max, far_index, 0, keepdims=False)
    chosen_totals = lax.dynamic_index_in_dim(far_totals, far_index, 0, keepdims=False)
    chosen_summed = lax.dynamic_index_in_dim(far_summed, far_index, 0, keepdims=False)
    pack_part = packed_cache[0]
    seg_ends = jnp.cumsum(lengths[0])
    slot_ids = jnp.arange(pack_part.shape[0])
    slot_owner = jnp.sum((slot_ids[:, None] >= seg_ends[None, :]).astype(jnp.int32), axis=1)
    request_ids = micro_batch * blocks + local_rows
    in_segment = (slot_owner[None, :] == request_ids[:, None])[:, None, None, :]
    scores = (
        jnp.einsum(
            "rkhd,pkd->rkhp",
            queries,
            pack_part[..., :HEAD_SIZE],
            preferred_element_type=jnp.float32,
        )
        * score_scale
    )
    own_score = (
        jnp.einsum("rkhd,rkd->rkh", queries, new_key, preferred_element_type=jnp.float32)
        * score_scale
    )
    row_max = jnp.maximum(jnp.max(jnp.where(in_segment, scores, -jnp.inf), axis=-1), own_score)
    long_mask = long_row[:, None, None]
    row_max = jnp.where(long_mask, jnp.maximum(row_max, chosen_max[None]), row_max)
    weights = jnp.where(
        in_segment, jnp.exp(jnp.where(in_segment, scores - row_max[..., None], 0.0)), 0.0
    ).astype(jnp.bfloat16)
    own_weights = jnp.exp(own_score - row_max).astype(jnp.bfloat16)
    far_factor = jnp.where(
        long_mask, jnp.exp(jnp.where(long_mask, chosen_max[None] - row_max, 0.0)), 0.0
    )
    softmax_total = (
        jnp.sum(weights.astype(jnp.float32), axis=-1)
        + own_weights.astype(jnp.float32)
        + far_factor * chosen_totals[None]
    )
    weighted_sum = jnp.einsum(
        "rkhp,pkd->rkhd", weights, pack_part[..., HEAD_SIZE:], preferred_element_type=jnp.float32
    )
    weighted_sum = (
        weighted_sum
        + own_weights.astype(jnp.float32)[..., None] * new_value.astype(jnp.float32)[:, :, None, :]
    )
    weighted_sum = weighted_sum + far_factor[..., None] * chosen_summed[None]
    attended_heads = (
        (weighted_sum / softmax_total[..., None])
        .astype(jnp.bfloat16)
        .reshape(blocks, kv_local * requests_per_group * HEAD_SIZE)
    )
    out_weights = head_output_weight[0].reshape(kv_local * requests_per_group * HEAD_SIZE, columns)

    def project_heads(piece_rows, start_row):
        return jnp.dot(piece_rows, out_weights, preferred_element_type=jnp.float32)

    attended = head_total(rows_apply(attended_heads, project_heads))
    residual = (inputs.astype(jnp.float32) + attended).astype(jnp.bfloat16)
    normed_two = norm_rows(residual, feedforward_gain[0])
    ff_weights = gate_up[0].reshape(columns, -1)

    def ff_term(start_row, row_count):
        return jnp.dot(normed_two, ff_weights, preferred_element_type=jnp.float32)

    gate_and_up = rows_project(ff_term, blocks)
    hidden_width = gate_and_up.shape[1] // 2
    hidden = (jax.nn.silu(gate_and_up[:, :hidden_width]) * gate_and_up[:, hidden_width:]).astype(
        jnp.bfloat16
    )
    lower_weights = down_weight[0]

    def project_hidden(piece_rows, start_row):
        return jnp.dot(piece_rows, lower_weights, preferred_element_type=jnp.float32)

    lowered = head_total(rows_apply(hidden, project_hidden))
    return (residual.astype(jnp.float32) + lowered).astype(jnp.bfloat16)


def local(
    tokens,
    attention_gain,
    query_key_value_weight,
    head_output_weight,
    feedforward_gain,
    gate_up,
    down_weight,
    packed_cache,
    long_cache,
    lengths,
    long_split,
):
    req_count = lax.axis_size("req")
    section_index = lax.axis_index("section")
    batch_count = 1
    per_group = tokens.shape[0] // req_count
    blocks = per_group // batch_count
    columns = tokens.shape[1]
    token_grid = tokens.reshape(req_count, per_group, columns)
    result = jnp.zeros_like(token_grid)
    incoming = jnp.zeros((req_count * blocks, columns), jnp.bfloat16)
    for phase_step in range(batch_count + 1):
        micro_batch = phase_step - section_index
        is_active = (micro_batch >= 0) & (micro_batch < batch_count)
        micro_batch = jnp.clip(micro_batch, 0, batch_count - 1)
        new_batch = token_grid.reshape(req_count * blocks, columns)
        inputs = jnp.where(section_index == 0, new_batch, incoming)
        output = decoder_layer(
            inputs,
            micro_batch,
            attention_gain,
            query_key_value_weight,
            head_output_weight,
            feedforward_gain,
            gate_up,
            down_weight,
            packed_cache,
            long_cache,
            lengths,
            long_split,
        )
        placed = output.reshape(req_count, blocks, columns)
        result = jnp.where(is_active, placed, result)
        if phase_step < batch_count:
            incoming = shifted(output, "section", 1)
    return result.reshape(1, req_count * per_group, columns)

def swap(value, axis, distance, section, target_section=None):
    size = lax.axis_size(axis)
    target_section = section if target_section is None else target_section
    pairs = [(section * size + i, target_section * size + (i ^ distance)) for i in range(size)]
    return lax.ppermute(value, ("section", axis), pairs)


def gather_doubling(value, axis, section):
    held, distance = value[None], 1
    while distance < lax.axis_size(axis):
        held = jnp.concatenate([held, swap(held, axis, distance, section)])
        distance *= 2
    return held


def sum_doubling(value, axis, section):
    distance = 1
    while distance < lax.axis_size(axis):
        other = swap(value, axis, distance, section)
        total = value.astype(jnp.float32) + other.astype(jnp.float32)
        distance *= 2
        value = total.astype(jnp.bfloat16)
    return total


def exchange(values, axis):
    return lax.all_to_all(values, axis, 0, 0)


def in_vmem(count):
    return [pl.BlockSpec(memory_space=pltpu.VMEM)] * count


def in_hbm(count):
    return [pl.BlockSpec(memory_space=pltpu.HBM)] * count


def in_smem(count):
    return [pl.BlockSpec(memory_space=pltpu.SMEM)] * count


def params():
    return pltpu.CompilerParams(vmem_limit_bytes=VMEM_MEBIBYTES * 2**20)


def column_chunks(width):
    return [(start, min(COLUMNS, width - start)) for start in range(0, width, COLUMNS)]


def split_parts(value):
    high = value.astype(jnp.bfloat16)
    low = (value - high.astype(jnp.float32)).astype(jnp.bfloat16)
    return high, low


def sum_columns(values):
    floats = values.astype(jnp.float32)
    squares = jnp.sum(floats * floats, axis=-1, keepdims=True)
    high, low = split_parts(squares)
    lane = lax.broadcasted_iota(jnp.int32, (values.shape[0], LANES), 1)
    return jnp.where(
        lane == 0, high.astype(jnp.float32), jnp.where(lane == 1, low.astype(jnp.float32), 0.0)
    )


def row_scale(parts):
    total = sum(jnp.sum(part.astype(jnp.float32), axis=-1, keepdims=True) for part in parts)
    return lax.rsqrt(total / MODEL_WIDTH + EPSILON)


def expand_rows(scaled, wide_ref):
    rows, columns = scaled.shape
    chunk = 2 * LANES
    source = lax.broadcasted_iota(jnp.int32, (chunk, 2 * chunk), 0)
    target = lax.broadcasted_iota(jnp.int32, (chunk, 2 * chunk), 1)
    count = columns // chunk
    stacked = jnp.concatenate([scaled[:, c * chunk : (c + 1) * chunk] for c in range(count)], 0)
    for half in range(2):
        select = jnp.where(target == 2 * source + half, 1.0, 0.0).astype(jnp.bfloat16)
        spread = jnp.dot(stacked, select, preferred_element_type=jnp.float32).astype(jnp.bfloat16)
        for c in range(count):
            wide_ref[half * rows : (half + 1) * rows, 2 * c * chunk : 2 * (c + 1) * chunk] = spread[
                c * rows : (c + 1) * rows
            ]


def scale_columns(values, gain):
    return (values.astype(jnp.float32) * gain.astype(jnp.float32)).astype(jnp.bfloat16)


def start_pair_copies(weight_ref, weights, sems):
    copies = []
    for c, (start, width) in enumerate(column_chunks(weight_ref.shape[3])):
        copies.append(
            pltpu.make_async_copy(
                weight_ref.at[0, :, :, pl.ds(start, width)],
                weights.at[c, :, :, pl.ds(0, width)],
                sems.at[c],
            )
        )
    for copy in copies:
        copy.start()
    return copies


def qkv_kernel(peers, inputs_ref, gain_ref, table_ref, weight_ref, out_ref, wide, weights, sems):
    rows, depth = inputs_ref.shape
    blocks = rows // peers
    width = weight_ref.shape[3]
    far = peers // 2 * blocks
    copies = start_pair_copies(weight_ref, weights, sems)
    expand_rows(scale_columns(inputs_ref[...], gain_ref[...]), wide)

    def write(result, start, size, tail):
        lanes = pl.ds(start, size)
        long_rows = [result[r : r + 1] for r in (0, far, rows, rows + far)]
        extra = jnp.concatenate(long_rows + tail, 0).astype(jnp.bfloat16)
        for p in range(peers):
            for k in range(2):
                first = k * rows + p * blocks
                out_ref[p, k * blocks : (k + 1) * blocks, lanes] = result[
                    first : first + blocks
                ].astype(jnp.bfloat16)
            out_ref[p, 2 * blocks :, lanes] = extra

    sums = sum_columns(inputs_ref[...])
    high, low = split_parts(table_ref[0:1])
    write(
        jnp.concatenate([sums, sums], 0),
        width,
        LANES,
        [high.astype(jnp.float32), low.astype(jnp.float32), jnp.zeros((blocks - 6, LANES), jnp.float32)],
    )
    for c, (start, size) in enumerate(column_chunks(width)):
        copies[c].wait()
        result = jnp.dot(
            wide[...],
            weights[c, :, :, 0:size].reshape(2 * depth, size),
            preferred_element_type=jnp.float32,
        )
        write(result, start, size, [jnp.zeros((blocks - 4, size), jnp.float32)])


def project_qkv(inputs, gain, table, weight, peers):
    rows = inputs.shape[0]
    depth, pair, width = weight.shape[1:]
    chunks = len(column_chunks(width))
    return pl.pallas_call(
        functools.partial(qkv_kernel, peers),
        out_shape=jax.ShapeDtypeStruct((peers, 3 * rows // peers, width + LANES), jnp.bfloat16),
        in_specs=in_vmem(3) + in_hbm(1),
        out_specs=pl.BlockSpec(memory_space=pltpu.VMEM),
        scratch_shapes=[
            pltpu.VMEM((pair * rows, pair * depth), jnp.bfloat16),
            pltpu.VMEM((chunks, depth, pair, COLUMNS), jnp.bfloat16),
            pltpu.SemaphoreType.DMA((chunks,)),
        ],
        compiler_params=params(),
        name="project_qkv",
    )(inputs, gain, table, weight)


def attention_kernel(peers, *refs):
    pieces_ref, table_ref, starts, lengths, split, packed_ref, long_ref, out_ref = refs[:8]
    piece_refs = [pieces_ref.at[p] for p in range(peers)]
    (rope, packed, far, queries, keys, values, scores, far_scores, merged_rows, packed_sem, far_sems) = (
        refs[8:]
    )
    group = lax.axis_index("req")
    blocks = out_ref.shape[0] // 2
    heads = QUERY_HEADS // KEY_VALUE_HEADS
    pairs = 2 * heads
    window = scores.shape[2] // 2
    slots = packed.shape[0]
    far_chunks = far.shape[1] // FAR_SLOTS
    scale = 1.0 / math.sqrt(HEAD_SIZE)
    live = [split[0, 0], split[1, 0]]

    def far_copy(j, c):
        return pltpu.make_async_copy(
            long_ref.at[0, j, pl.ds(c * FAR_SLOTS, FAR_SLOTS)],
            far.at[j, pl.ds(c * FAR_SLOTS, FAR_SLOTS)],
            far_sems.at[j, c],
        )

    packed_copy = pltpu.make_async_copy(packed_ref.at[0], packed, packed_sem)
    packed_copy.start()
    for j in range(2):
        for c in range(far_chunks):

            @pl.when(c * FAR_SLOTS < live[j])
            def _():
                far_copy(j, c).start()

    width = HEAD_SIZE * (heads + 2)
    scale_rows = row_scale([piece[:, width:] for piece in piece_refs])
    far_tables = [
        sum(
            pieces_ref[j * (peers // 2), 2 * blocks :, width:][row : row + 1].astype(jnp.float32)
            for row in (4, 5)
        )
        for j in range(2)
    ]
    own_table = table_ref[...]
    table = jnp.concatenate(
        [own_table, own_table] + far_tables * 2 + [jnp.zeros((blocks - 4, HEAD_SIZE), jnp.float32)], 0
    )
    turned = pltpu.roll(table, HEAD_SIZE // 2, 1)
    lower = lax.broadcasted_iota(jnp.int32, table.shape, 1) < HEAD_SIZE // 2
    cosine = jnp.where(lower, table, turned)
    sine = jnp.where(lower, -turned, table)
    for b in range(heads + 2):
        lanes = slice(b * HEAD_SIZE, (b + 1) * HEAD_SIZE)
        block = sum(piece[:, lanes].astype(jnp.float32) for piece in piece_refs) * scale_rows
        if b <= heads:
            block = block * cosine + pltpu.roll(block, HEAD_SIZE // 2, 1) * sine
        block = block.astype(jnp.bfloat16).astype(jnp.float32)
        rope[:, lanes] = block
        for k in range(2):
            own_rows = block[k * blocks : (k + 1) * blocks]
            if b < heads:
                queries[:, k * heads + b, :] = own_rows
            else:
                for h in range(heads):
                    (keys if b == heads else values)[:, k * heads + h, :] = own_rows

    def same_head(columns):
        row = lax.broadcasted_iota(jnp.int32, (pairs, columns), 0)
        column = lax.broadcasted_iota(jnp.int32, (pairs, columns), 1)
        return (row // heads) == (column % 2), column // 2

    def contract(a, b):
        return lax.dot_general(a, b, (((1,), (1,)), ((), ())), preferred_element_type=jnp.float32)

    packed_copy.wait()
    matching, slot = same_head(2 * window)
    first_slots = []
    for r in range(blocks):
        first = jnp.minimum(starts[r], slots - window)
        first_slots.append(first)
        low = starts[r] - first
        segment = packed[pl.ds(first, window), :, 0:HEAD_SIZE].reshape(2 * window, HEAD_SIZE)
        own = contract(queries[r].astype(jnp.bfloat16), segment) * scale
        inside = matching & (slot >= low) & (slot < low + lengths[r])
        scores[r] = jnp.where(inside, own, LOWEST)
    own_score = jnp.sum(queries[...] * keys[...], axis=-1, keepdims=True) * scale
    row_max = jnp.maximum(jnp.max(scores[...], axis=-1, keepdims=True), own_score)
    weights = jnp.exp(scores[...] - row_max).astype(jnp.bfloat16)
    own_weight = jnp.exp(own_score - row_max).astype(jnp.bfloat16).astype(jnp.float32)
    totals = jnp.sum(weights.astype(jnp.float32), axis=-1, keepdims=True) + own_weight
    near_peak = row_max[0] + jnp.log(totals[0])
    for r in range(blocks):
        segment = packed[pl.ds(first_slots[r], window), :, HEAD_SIZE:].reshape(2 * window, HEAD_SIZE)
        summed = jnp.dot(weights[r], segment, preferred_element_type=jnp.float32)
        summed = summed + own_weight[r] * values[r]
        merged_rows[r] = summed / totals[r]

    matching, slot = same_head(2 * FAR_SLOTS)
    for j in range(2):
        long_rows = jnp.concatenate(
            [
                rope[2 * blocks + 2 * k + j : 2 * blocks + 2 * k + j + 1, h * HEAD_SIZE : (h + 1) * HEAD_SIZE]
                for k in range(2)
                for h in range(heads)
            ],
            0,
        ).astype(jnp.bfloat16)
        count = (live[j] + FAR_SLOTS - 1) // FAR_SLOTS

        def score(c, peak):
            far_copy(j, c).wait()
            chunk = far[j, pl.ds(c * FAR_SLOTS, FAR_SLOTS), :, 0:HEAD_SIZE].reshape(
                2 * FAR_SLOTS, HEAD_SIZE
            )
            found = contract(long_rows, chunk) * scale
            found = jnp.where(matching & (slot < live[j] - c * FAR_SLOTS), found, LOWEST)
            far_scores[c] = found
            return jnp.maximum(peak, jnp.max(found, axis=-1, keepdims=True))

        peak = lax.fori_loop(0, count, score, jnp.full((pairs, 1), LOWEST, jnp.float32))

        def weigh(c, state):
            total, summed = state
            weight = jnp.exp(far_scores[c] - peak).astype(jnp.bfloat16)
            chunk = far[j, pl.ds(c * FAR_SLOTS, FAR_SLOTS), :, HEAD_SIZE:].reshape(
                2 * FAR_SLOTS, HEAD_SIZE
            )
            total = total + jnp.sum(weight.astype(jnp.float32), axis=-1, keepdims=True)
            return total, summed + jnp.dot(weight, chunk, preferred_element_type=jnp.float32)

        total, summed = lax.fori_loop(
            0,
            count,
            weigh,
            (jnp.zeros((pairs, 1), jnp.float32), jnp.zeros((pairs, HEAD_SIZE), jnp.float32)),
        )
        far_peak = peak + jnp.log(total)
        result = summed / total
        owner = group == j * (peers // 2)
        top = jnp.maximum(far_peak, near_peak)
        far_part = jnp.exp(far_peak - top)
        near_part = jnp.exp(near_peak - top)
        both = far_part + near_part
        result = jnp.where(owner, (result * far_part + merged_rows[0] * near_part) / both, result)
        log_total = jnp.where(owner, top + jnp.log(both), far_peak)
        high, low = split_parts(log_total)
        merged_rows[blocks + j] = result
        merged_rows[blocks + 2 + j] = jnp.broadcast_to(high.astype(jnp.float32), result.shape)
        merged_rows[blocks + 4 + j] = jnp.broadcast_to(low.astype(jnp.float32), result.shape)
    merged_rows[blocks + 6 :] = jnp.zeros((blocks - 6, pairs, HEAD_SIZE), jnp.float32)
    for b in range(pairs):
        out_ref[:, b * HEAD_SIZE : (b + 1) * HEAD_SIZE] = merged_rows[:, b, :].astype(jnp.bfloat16)


def attend(pieces, table, starts, lengths, split, packed_cache, long_cache):
    peers = pieces.shape[0]
    blocks = pieces.shape[1] // 3
    heads = QUERY_HEADS // KEY_VALUE_HEADS
    pairs = 2 * heads
    slots = packed_cache.shape[1]
    far_slots = long_cache.shape[2]
    return pl.pallas_call(
        functools.partial(attention_kernel, peers),
        out_shape=jax.ShapeDtypeStruct((2 * blocks, pairs * HEAD_SIZE), jnp.bfloat16),
        in_specs=in_vmem(2) + in_smem(3) + in_hbm(2),
        out_specs=pl.BlockSpec(memory_space=pltpu.VMEM),
        scratch_shapes=[
            pltpu.VMEM((3 * blocks, (heads + 2) * HEAD_SIZE), jnp.float32),
            pltpu.VMEM((slots, 2, 2 * HEAD_SIZE), jnp.bfloat16),
            pltpu.VMEM((2, far_slots, 2, 2 * HEAD_SIZE), jnp.bfloat16),
            pltpu.VMEM((blocks, pairs, HEAD_SIZE), jnp.float32),
            pltpu.VMEM((blocks, pairs, HEAD_SIZE), jnp.float32),
            pltpu.VMEM((blocks, pairs, HEAD_SIZE), jnp.float32),
            pltpu.VMEM((blocks, pairs, 2 * MOST_SLOTS), jnp.float32),
            pltpu.VMEM((far_slots // FAR_SLOTS, pairs, 2 * FAR_SLOTS), jnp.float32),
            pltpu.VMEM((2 * blocks, pairs, HEAD_SIZE), jnp.float32),
            pltpu.SemaphoreType.DMA,
            pltpu.SemaphoreType.DMA((2, far_slots // FAR_SLOTS)),
        ],
        compiler_params=params(),
        name="attend",
    )(pieces, table, starts, lengths, split, packed_cache, long_cache)


def start_column_copies(weight_at, weights, sems):
    copies = []
    for c, (start, width) in enumerate(column_chunks(weight_at.shape[1])):
        copies.append(
            pltpu.make_async_copy(weight_at.at[:, pl.ds(start, width)], weights.at[c], sems.at[c])
        )
    for copy in copies:
        copy.start()
    return copies


def multiply_columns(rows_ref, weights, copies, out_ref):
    for c, copy in enumerate(copies):
        copy.wait()
        out_ref[:, c * COLUMNS : (c + 1) * COLUMNS] = jnp.dot(
            rows_ref[...], weights[c], preferred_element_type=jnp.float32
        ).astype(out_ref.dtype)


def output_kernel(pieces_ref, weight_ref, out_ref, whole, weights, sems):
    peers = pieces_ref.shape[0]
    group = lax.axis_index("req")
    blocks = pieces_ref.shape[1] // 2
    copies = start_column_copies(weight_ref, weights, sems)
    for d in range(peers):
        start = pl.multiple_of(lax.bitwise_xor(group, d) * blocks, blocks)
        whole[pl.ds(start, blocks)] = pieces_ref[d, 0:blocks]
    extras = [pieces_ref[d, blocks:].astype(jnp.float32) for d in range(peers)]
    for j in range(2):
        peaks = [e[2 + j : 3 + j] + e[4 + j : 5 + j] for e in extras]
        top = functools.reduce(jnp.maximum, peaks)
        parts = [jnp.exp(peak - top) for peak in peaks]
        merged_row = sum(e[j : j + 1] * part for e, part in zip(extras, parts)) / sum(parts)
        rows = slice(j * (peers // 2) * blocks, j * (peers // 2) * blocks + blocks)
        row = lax.broadcasted_iota(jnp.int32, (blocks, whole.shape[1]), 0)
        whole[rows] = jnp.where(
            row == 0, merged_row, whole[rows].astype(jnp.float32)
        ).astype(jnp.bfloat16)
    multiply_columns(whole, weights, copies, out_ref)


def project_columns(kernel, pieces, weight, rows, depth, width, name):
    chunks = len(column_chunks(width))
    return pl.pallas_call(
        kernel,
        out_shape=jax.ShapeDtypeStruct((rows, width), jnp.bfloat16),
        in_specs=in_vmem(1) + in_hbm(1),
        out_specs=pl.BlockSpec(memory_space=pltpu.VMEM),
        scratch_shapes=[
            pltpu.VMEM((rows, depth), jnp.bfloat16),
            pltpu.VMEM((chunks, depth, COLUMNS), jnp.bfloat16),
            pltpu.SemaphoreType.DMA((chunks,)),
        ],
        compiler_params=params(),
        name=name,
    )(pieces, weight)


def project_output(pieces, weight):
    rows = pieces.shape[0] * pieces.shape[1] // 2
    return project_columns(output_kernel, pieces, weight, rows, *weight.shape, "project_output")


def down_kernel(pieces_ref, weight_ref, out_ref, whole, weights, sems):
    peers, _, width = pieces_ref.shape
    group = lax.axis_index("req")
    copies = start_column_copies(weight_ref.at[0], weights, sems)
    for d in range(peers):
        start = pl.multiple_of(lax.bitwise_xor(group, d) * width, LANES)
        whole[:, pl.ds(start, width)] = pieces_ref[d]
    multiply_columns(whole, weights, copies, out_ref)


def project_down(pieces, weight):
    return project_columns(down_kernel, pieces, weight, pieces.shape[1], *weight.shape[1:], "project_down")


def gate_up_kernel(peers, inputs_ref, gain_ref, weight_ref, out_ref, wide, weights, total, sems):
    rows, depth = inputs_ref.shape
    copies = start_pair_copies(weight_ref, weights, sems)
    expand_rows(scale_columns(inputs_ref[...], gain_ref[...]), wide)
    sums = sum_columns(inputs_ref[...]).astype(jnp.bfloat16)
    width = total.shape[1] // peers
    for p in range(peers):
        out_ref[p, 0:rows, width:] = sums
        out_ref[p, rows:, width:] = sums
    done = 0
    for c, copy in enumerate(copies):
        copy.wait()
        total[:, c * COLUMNS : (c + 1) * COLUMNS] = jnp.dot(
            wide[...],
            weights[c].reshape(2 * depth, COLUMNS),
            preferred_element_type=jnp.float32,
        ).astype(jnp.bfloat16)
        while done < peers and (done + 1) * width <= (c + 1) * COLUMNS:
            out_ref[done, :, 0:width] = total[:, done * width : (done + 1) * width]
            done += 1


def project_gate_up(inputs, gain, weight, peers):
    rows = inputs.shape[0]
    depth, pair, width = weight.shape[1:]
    chunks = len(column_chunks(width))
    return pl.pallas_call(
        functools.partial(gate_up_kernel, peers),
        out_shape=jax.ShapeDtypeStruct((peers, pair * rows, width // peers + LANES), jnp.bfloat16),
        in_specs=in_vmem(2) + in_hbm(1),
        out_specs=pl.BlockSpec(memory_space=pltpu.VMEM),
        scratch_shapes=[
            pltpu.VMEM((pair * rows, pair * depth), jnp.bfloat16),
            pltpu.VMEM((chunks, depth, pair, COLUMNS), jnp.bfloat16),
            pltpu.VMEM((pair * rows, width), jnp.bfloat16),
            pltpu.SemaphoreType.DMA((chunks,)),
        ],
        compiler_params=params(),
        name="project_gate_up",
    )(inputs, gain, weight)


def hidden_kernel(pieces_ref, out_ref):
    peers = pieces_ref.shape[0]
    rows, width = out_ref.shape
    factor = row_scale([pieces_ref[p, 0:rows, width:] for p in range(peers)])

    def summed(first):
        return sum(
            pieces_ref[p, first : first + rows, 0:width].astype(jnp.float32) for p in range(peers)
        ) * factor

    gate, up = summed(0), summed(rows)
    out_ref[...] = (gate / (1.0 + jnp.exp(-gate)) * up).astype(jnp.bfloat16)


def gated_units(pieces):
    rows, width = pieces.shape[1] // 2, pieces.shape[2] - LANES
    return pl.pallas_call(
        hidden_kernel,
        out_shape=jax.ShapeDtypeStruct((rows, width), jnp.bfloat16),
        in_specs=in_vmem(1),
        out_specs=pl.BlockSpec(memory_space=pltpu.VMEM),
        compiler_params=params(),
        name="gated_units",
    )(pieces)


def fast_layer(section, inputs, attention_gain, query_key_value_weight, head_output_weight, feedforward_gain, gate_up, down_weight, packed_cache, long_cache, table, *segments):
    req_count = lax.axis_size("req")
    terms = project_qkv(inputs, attention_gain, table, query_key_value_weight, req_count)
    own = attend(exchange(terms, "req"), table, *segments, packed_cache, long_cache)
    out_weight = head_output_weight.reshape(-1, head_output_weight.shape[3])
    attended = project_output(gather_doubling(own, "req", section), out_weight)
    attended = sum_doubling(attended, "head", section)
    residual = (inputs.astype(jnp.float32) + attended).astype(jnp.bfloat16)
    terms = project_gate_up(residual, feedforward_gain, gate_up, req_count)
    hidden = gated_units(exchange(terms, "req"))
    lowered = project_down(gather_doubling(hidden, "req", section), down_weight)
    lowered = sum_doubling(lowered, "head", section)
    return (residual.astype(jnp.float32) + lowered).astype(jnp.bfloat16)


def rope_table(lengths):
    req_count, group = lax.axis_size("req"), lax.axis_index("req")
    owner = (group == 0) | (group == req_count // 2)
    long_row = (jnp.arange(lengths.shape[1]) == 0) & owner
    position = lengths[0] + jnp.where(long_row, LONG, 0).astype(jnp.int32)
    half_dim = HEAD_SIZE // 2
    inverse = 1.0 / 10000.0 ** (jnp.arange(half_dim).astype(jnp.float32) * 2.0 / HEAD_SIZE)
    angles = position.astype(jnp.float32)[:, None] * inverse[None, :]
    return jnp.concatenate([jnp.cos(angles), jnp.sin(angles)], 1)


def fast_local(tokens, attention_gain, query_key_value_weight, head_output_weight, feedforward_gain, gate_up, down_weight, packed_cache, long_cache, lengths, long_split):
    layer_arrays = (
        attention_gain,
        query_key_value_weight,
        head_output_weight,
        feedforward_gain,
        gate_up,
        down_weight,
        packed_cache,
        long_cache,
        rope_table(lengths),
        jnp.cumsum(lengths[0]) - lengths[0],
        lengths[0],
        long_split,
    )
    first = fast_layer(0, tokens, *layer_arrays)
    second = fast_layer(1, swap(first, "head", 0, 0, 1), *layer_arrays)
    return jnp.where(lax.axis_index("section") == 0, first, second)[None]


def is_power_of_two(value):
    return value & (value - 1) == 0


def fits_fast(mesh):
    req_count, head_count = mesh.shape["req"], mesh.shape["head"]
    columns = MODEL_WIDTH // req_count
    return (
        mesh.shape["section"] == 2
        and is_power_of_two(req_count)
        and is_power_of_two(head_count)
        and KEY_VALUE_HEADS == 2 * head_count
        and columns % COLUMNS == 0
        and FF % (head_count * COLUMNS) == 0
        and FF % (head_count * req_count * LANES) == 0
    )


def solution(mesh):
    placed = (
        P(None, "req"),
        P("section", "req"),
        P("section", "req", "head", None),
        P("section", "head", None, "req"),
        P("section", "req"),
        P("section", "req", None, "head"),
        P("section", "head", "req"),
        P("section", "req", "head", None),
        P("section", None, "req", "head", None),
        P("req", None),
        P(None, "req"),
    )
    return jax.shard_map(
        fast_local if fits_fast(mesh) else local,
        mesh=mesh,
        in_specs=placed, out_specs=P("section", None, "req"), check_vma=False
    )
```

```python
import functools
import math

import jax
import jax.numpy as jnp
from jax import lax
from jax.experimental import pallas as pl
from jax.experimental.pallas import tpu as pltpu
from jax.sharding import PartitionSpec as P

MODEL_WIDTH = 8192
QUERY_HEADS = 64
KEY_VALUE_HEADS = 8
HEAD_SIZE = 128
LONG = 16384
FF = 14336
MOST_SLOTS = 256
LANES = 128
COLUMNS = 512
VMEM_MEBIBYTES = 50
FAR_SLOTS = 2048
LOWEST = -1e30


EPSILON = 1e-05


def merged(part, axis, combine):
    gathered = jax.tree.map(lambda a: lax.all_gather(a, axis), part)

    def take(source):
        return jax.tree.map(lambda a: lax.dynamic_index_in_dim(a, source, 0, False), gathered)

    return lax.fori_loop(
        1, lax.axis_size(axis), lambda source, state: combine(state, take(source)), take(0)
    )


def shifted(value, axis, by):
    peers = lax.axis_size(axis)
    pairs = [(i, i + by) for i in range(peers) if 0 <= i + by < peers]
    return lax.ppermute(value, axis, pairs)


def rotate(values, position):
    half_dim = values.shape[-1] // 2
    freq_ids = jnp.arange(half_dim).astype(jnp.float32)
    inverse = 1.0 / 10000.0 ** (freq_ids * 2.0 / values.shape[-1])
    angles = position.astype(jnp.float32)[:, None] * inverse[None, :]
    cosine = jnp.cos(angles)[:, None, None, :]
    sine_part = jnp.sin(angles)[:, None, None, :]
    lower_half = values[..., :half_dim]
    upper_half = values[..., half_dim:]
    return jnp.concatenate(
        [
            lower_half * cosine - upper_half * sine_part,
            upper_half * cosine + lower_half * sine_part,
        ],
        -1,
    )


def add_pair(earlier, second_part):
    return earlier + second_part


def combine_partial(earlier, second_part):
    peak = jnp.maximum(earlier[0], second_part[0])
    left_factor = jnp.exp(earlier[0] - peak)
    right_factor = jnp.exp(second_part[0] - peak)
    softmax_total = earlier[1] * left_factor + second_part[1] * right_factor
    weighted_sum = earlier[2] * left_factor[..., None] + second_part[2] * right_factor[..., None]
    return (peak, softmax_total, weighted_sum)


def over_requests(values, combiner):
    return merged(values, "req", combiner)


def rows_apply(values, row_fn):
    return row_fn(lax.all_gather(values, "req", axis=0, tiled=True), jnp.int32(0))


def rows_project(term_fn, row_count):
    return lax.psum_scatter(
        term_fn(jnp.int32(0), row_count * lax.axis_size("req")),
        "req",
        scatter_dimension=0,
        tiled=True,
    )


def head_total(values):
    return lax.psum(values, "head")


def keep_rows(piece_rows, start_row):
    return piece_rows


def norm_rows(values, gain_row):
    floats = values.astype(jnp.float32)
    squares = over_requests(jnp.sum(floats * floats, axis=-1), add_pair)
    return (
        floats * lax.rsqrt(squares / MODEL_WIDTH + EPSILON)[:, None] * gain_row.astype(jnp.float32)
    ).astype(jnp.bfloat16)


def decoder_layer(
    inputs,
    micro_batch,
    attention_gain,
    query_key_value_weight,
    head_output_weight,
    feedforward_gain,
    gate_up,
    down_weight,
    packed_cache,
    long_cache,
    lengths,
    long_split,
):
    req_count = lax.axis_size("req")
    group_index = lax.axis_index("req")
    blocks = inputs.shape[0] // req_count
    columns = query_key_value_weight.shape[1]
    kv_local = query_key_value_weight.shape[2]
    requests_per_group = QUERY_HEADS // KEY_VALUE_HEADS
    score_scale = 1.0 / math.sqrt(HEAD_SIZE)
    normalized_input = norm_rows(inputs, attention_gain[0])
    in_weights = query_key_value_weight[0].reshape(
        columns, kv_local * (requests_per_group + 2) * HEAD_SIZE
    )

    def qkv_term(start_row, row_count):
        return jnp.dot(normalized_input, in_weights, preferred_element_type=jnp.float32)

    projected_rows = rows_project(qkv_term, blocks).reshape(
        blocks, kv_local, requests_per_group + 2, HEAD_SIZE
    )
    local_rows = jnp.arange(blocks)
    row_lengths = lengths[0]
    owner_long = (group_index == 0) | (group_index == req_count // 2)
    long_row = (local_rows == 0) & (micro_batch == 0) & owner_long
    position = row_lengths + jnp.where(long_row, LONG, 0).astype(jnp.int32)
    queries = rotate(projected_rows[:, :, :requests_per_group], position).astype(jnp.bfloat16)
    new_key = rotate(projected_rows[:, :, requests_per_group : requests_per_group + 1], position)[
        :, :, 0
    ].astype(jnp.bfloat16)
    new_value = projected_rows[:, :, requests_per_group + 1].astype(jnp.bfloat16)
    gathered = rows_apply(
        queries[0:1].reshape(1, kv_local * requests_per_group * HEAD_SIZE), keep_rows
    )
    long_queries = jnp.stack([gathered[0], gathered[req_count // 2]]).reshape(
        2, kv_local, requests_per_group, HEAD_SIZE
    )
    far_cache = long_cache[0]
    far_live = (jnp.arange(far_cache.shape[1])[None, :] < long_split[:, 0][:, None])[
        :, None, None, :
    ]
    far_scores = (
        jnp.einsum(
            "jkhd,jpkd->jkhp",
            long_queries,
            far_cache[..., :HEAD_SIZE],
            preferred_element_type=jnp.float32,
        )
        * score_scale
    )
    far_max = jnp.max(jnp.where(far_live, far_scores, -jnp.inf), axis=-1)
    far_weights = jnp.where(
        far_live, jnp.exp(jnp.where(far_live, far_scores - far_max[..., None], 0.0)), 0.0
    ).astype(jnp.bfloat16)
    far_totals = jnp.sum(far_weights.astype(jnp.float32), axis=-1)
    far_summed = jnp.einsum(
        "jkhp,jpkd->jkhd",
        far_weights,
        far_cache[..., HEAD_SIZE:],
        preferred_element_type=jnp.float32,
    )
    far_max, far_totals, far_summed = over_requests(
        (far_max, far_totals, far_summed), combine_partial
    )
    far_index = jnp.where(group_index == 0, 0, 1)
    chosen_max = lax.dynamic_index_in_dim(far_max, far_index, 0, keepdims=False)
    chosen_totals = lax.dynamic_index_in_dim(far_totals, far_index, 0, keepdims=False)
    chosen_summed = lax.dynamic_index_in_dim(far_summed, far_index, 0, keepdims=False)
    pack_part = packed_cache[0]
    seg_ends = jnp.cumsum(lengths[0])
    slot_ids = jnp.arange(pack_part.shape[0])
    slot_owner = jnp.sum((slot_ids[:, None] >= seg_ends[None, :]).astype(jnp.int32), axis=1)
    request_ids = micro_batch * blocks + local_rows
    in_segment = (slot_owner[None, :] == request_ids[:, None])[:, None, None, :]
    scores = (
        jnp.einsum(
            "rkhd,pkd->rkhp",
            queries,
            pack_part[..., :HEAD_SIZE],
            preferred_element_type=jnp.float32,
        )
        * score_scale
    )
    own_score = (
        jnp.einsum("rkhd,rkd->rkh", queries, new_key, preferred_element_type=jnp.float32)
        * score_scale
    )
    row_max = jnp.maximum(jnp.max(jnp.where(in_segment, scores, -jnp.inf), axis=-1), own_score)
    long_mask = long_row[:, None, None]
    row_max = jnp.where(long_mask, jnp.maximum(row_max, chosen_max[None]), row_max)
    weights = jnp.where(
        in_segment, jnp.exp(jnp.where(in_segment, scores - row_max[..., None], 0.0)), 0.0
    ).astype(jnp.bfloat16)
    own_weights = jnp.exp(own_score - row_max).astype(jnp.bfloat16)
    far_factor = jnp.where(
        long_mask, jnp.exp(jnp.where(long_mask, chosen_max[None] - row_max, 0.0)), 0.0
    )
    softmax_total = (
        jnp.sum(weights.astype(jnp.float32), axis=-1)
        + own_weights.astype(jnp.float32)
        + far_factor * chosen_totals[None]
    )
    weighted_sum = jnp.einsum(
        "rkhp,pkd->rkhd", weights, pack_part[..., HEAD_SIZE:], preferred_element_type=jnp.float32
    )
    weighted_sum = (
        weighted_sum
        + own_weights.astype(jnp.float32)[..., None] * new_value.astype(jnp.float32)[:, :, None, :]
    )
    weighted_sum = weighted_sum + far_factor[..., None] * chosen_summed[None]
    attended_heads = (
        (weighted_sum / softmax_total[..., None])
        .astype(jnp.bfloat16)
        .reshape(blocks, kv_local * requests_per_group * HEAD_SIZE)
    )
    out_weights = head_output_weight[0].reshape(kv_local * requests_per_group * HEAD_SIZE, columns)

    def project_heads(piece_rows, start_row):
        return jnp.dot(piece_rows, out_weights, preferred_element_type=jnp.float32)

    attended = head_total(rows_apply(attended_heads, project_heads))
    residual = (inputs.astype(jnp.float32) + attended).astype(jnp.bfloat16)
    normed_two = norm_rows(residual, feedforward_gain[0])
    ff_weights = gate_up[0].reshape(columns, -1)

    def ff_term(start_row, row_count):
        return jnp.dot(normed_two, ff_weights, preferred_element_type=jnp.float32)

    gate_and_up = rows_project(ff_term, blocks)
    hidden_width = gate_and_up.shape[1] // 2
    hidden = (jax.nn.silu(gate_and_up[:, :hidden_width]) * gate_and_up[:, hidden_width:]).astype(
        jnp.bfloat16
    )
    lower_weights = down_weight[0]

    def project_hidden(piece_rows, start_row):
        return jnp.dot(piece_rows, lower_weights, preferred_element_type=jnp.float32)

    lowered = head_total(rows_apply(hidden, project_hidden))
    return (residual.astype(jnp.float32) + lowered).astype(jnp.bfloat16)


def local(
    tokens,
    attention_gain,
    query_key_value_weight,
    head_output_weight,
    feedforward_gain,
    gate_up,
    down_weight,
    packed_cache,
    long_cache,
    lengths,
    long_split,
):
    req_count = lax.axis_size("req")
    section_index = lax.axis_index("section")
    batch_count = 1
    per_group = tokens.shape[0] // req_count
    blocks = per_group // batch_count
    columns = tokens.shape[1]
    token_grid = tokens.reshape(req_count, per_group, columns)
    result = jnp.zeros_like(token_grid)
    incoming = jnp.zeros((req_count * blocks, columns), jnp.bfloat16)
    for phase_step in range(batch_count + 1):
        micro_batch = phase_step - section_index
        is_active = (micro_batch >= 0) & (micro_batch < batch_count)
        micro_batch = jnp.clip(micro_batch, 0, batch_count - 1)
        new_batch = token_grid.reshape(req_count * blocks, columns)
        inputs = jnp.where(section_index == 0, new_batch, incoming)
        output = decoder_layer(
            inputs,
            micro_batch,
            attention_gain,
            query_key_value_weight,
            head_output_weight,
            feedforward_gain,
            gate_up,
            down_weight,
            packed_cache,
            long_cache,
            lengths,
            long_split,
        )
        placed = output.reshape(req_count, blocks, columns)
        result = jnp.where(is_active, placed, result)
        if phase_step < batch_count:
            incoming = shifted(output, "section", 1)
    return result.reshape(1, req_count * per_group, columns)

def swap(value, axis, distance, section, target_section=None):
    size = lax.axis_size(axis)
    target_section = section if target_section is None else target_section
    pairs = [(section * size + i, target_section * size + (i ^ distance)) for i in range(size)]
    return lax.ppermute(value, ("section", axis), pairs)


def swap_all(values, axis, section):
    received = {d: swap(values[d], axis, d, section) for d in reversed(range(1, len(values)))}
    return [values[0]] + [received[d] for d in range(1, len(values))]


def spread(value, axis, section):
    return swap_all([value] * lax.axis_size(axis), axis, section)


def sum_doubling(values, axis, section):
    distance = lax.axis_size(axis) // 2
    while distance >= 1:
        others = [swap(value, axis, distance, section) for value in values]
        totals = [a.astype(jnp.float32) + b.astype(jnp.float32) for a, b in zip(values, others)]
        values = [total.astype(jnp.bfloat16) for total in totals]
        distance //= 2
    return jnp.concatenate(totals, 1)


def in_vmem(count):
    return [pl.BlockSpec(memory_space=pltpu.VMEM)] * count


def in_hbm(count):
    return [pl.BlockSpec(memory_space=pltpu.HBM)] * count


def in_smem(count):
    return [pl.BlockSpec(memory_space=pltpu.SMEM)] * count


def params():
    return pltpu.CompilerParams(vmem_limit_bytes=VMEM_MEBIBYTES * 2**20)


def column_chunks(width):
    edge = COLUMNS // 2
    starts = [0] + list(range(edge, width - edge, COLUMNS)) + [width - edge]
    return [(a, b - a) for a, b in zip(starts, starts[1:] + [width]) if b > a]


def split_parts(value):
    high = value.astype(jnp.bfloat16)
    low = (value - high.astype(jnp.float32)).astype(jnp.bfloat16)
    return high, low


def sum_columns(values):
    floats = values.astype(jnp.float32)
    squares = jnp.sum(floats * floats, axis=-1, keepdims=True)
    high, low = split_parts(squares)
    lane = lax.broadcasted_iota(jnp.int32, (values.shape[0], LANES), 1)
    return jnp.where(
        lane == 0, high.astype(jnp.float32), jnp.where(lane == 1, low.astype(jnp.float32), 0.0)
    )


def row_scale(parts):
    total = sum(jnp.sum(part.astype(jnp.float32), axis=-1, keepdims=True) for part in parts)
    return lax.rsqrt(total / MODEL_WIDTH + EPSILON)


def expand_rows(scaled, wide_ref):
    rows, columns = scaled.shape
    chunk = 2 * LANES
    source = lax.broadcasted_iota(jnp.int32, (chunk, 2 * chunk), 0)
    target = lax.broadcasted_iota(jnp.int32, (chunk, 2 * chunk), 1)
    count = columns // chunk
    stacked = jnp.concatenate([scaled[:, c * chunk : (c + 1) * chunk] for c in range(count)], 0)
    for half in range(2):
        select = jnp.where(target == 2 * source + half, 1.0, 0.0).astype(jnp.bfloat16)
        spread = jnp.dot(stacked, select, preferred_element_type=jnp.float32).astype(jnp.bfloat16)
        for c in range(count):
            wide_ref[half * rows : (half + 1) * rows, 2 * c * chunk : 2 * (c + 1) * chunk] = spread[
                c * rows : (c + 1) * rows
            ]


def scale_columns(values, gain):
    return (values.astype(jnp.float32) * gain.astype(jnp.float32)).astype(jnp.bfloat16)


def start_pair_copies(weight_ref, weights, sems):
    copies = []
    for c, (start, width) in enumerate(column_chunks(weight_ref.shape[3])):
        copies.append(
            pltpu.make_async_copy(
                weight_ref.at[0, :, :, pl.ds(start, width)],
                weights.at[:, :, pl.ds(start, width)],
                sems.at[c],
            )
        )
    for copy in copies:
        copy.start()
    return copies


def qkv_kernel(peers, inputs_ref, gain_ref, table_ref, weight_ref, *refs):
    outs, (wide, weights, sums_ref, sems) = refs[:peers], refs[peers:]
    group = lax.axis_index("req")
    rows, depth = inputs_ref.shape
    blocks = rows // peers
    width = weight_ref.shape[3]
    far = peers // 2 * blocks
    copies = start_pair_copies(weight_ref, weights, sems)
    expand_rows(scale_columns(inputs_ref[...], gain_ref[...]), wide)

    def write(result_ref, start, size, tail):
        lanes = pl.ds(start, size)
        long_rows = [result_ref[r : r + 1, lanes] for r in (0, far, rows, rows + far)]
        extra = jnp.concatenate(long_rows + tail, 0).astype(jnp.bfloat16)
        for d in range(peers):
            peer = pl.multiple_of(lax.bitwise_xor(group, d) * blocks, blocks)
            for k in range(2):
                outs[d][k * blocks : (k + 1) * blocks, lanes] = result_ref[
                    pl.ds(k * rows + peer, blocks), lanes
                ].astype(jnp.bfloat16)
            outs[d][2 * blocks :, lanes] = extra

    sums = sum_columns(inputs_ref[...])
    sums_ref[0:rows, width:] = sums
    sums_ref[rows:, width:] = sums
    high, low = split_parts(table_ref[0:1])
    write(
        sums_ref,
        width,
        LANES,
        [high.astype(jnp.float32), low.astype(jnp.float32), jnp.zeros((blocks - 6, LANES), jnp.float32)],
    )
    for c, (start, size) in enumerate(column_chunks(width)):
        copies[c].wait()
        sums_ref[:, start : start + size] = jnp.dot(
            wide[...],
            weights[:, :, start : start + size].reshape(2 * depth, size),
            preferred_element_type=jnp.float32,
        )
        write(sums_ref, start, size, [jnp.zeros((blocks - 4, size), jnp.float32)])


def project_qkv(inputs, gain, table, weight, peers):
    rows = inputs.shape[0]
    depth, pair, width = weight.shape[1:]
    chunks = len(column_chunks(width))
    return pl.pallas_call(
        functools.partial(qkv_kernel, peers),
        out_shape=[jax.ShapeDtypeStruct((3 * rows // peers, width + LANES), jnp.bfloat16)] * peers,
        in_specs=in_vmem(3) + in_hbm(1),
        out_specs=in_vmem(peers),
        scratch_shapes=[
            pltpu.VMEM((pair * rows, pair * depth), jnp.bfloat16),
            pltpu.VMEM((depth, pair, width), jnp.bfloat16),
            pltpu.VMEM((pair * rows, width + LANES), jnp.float32),
            pltpu.SemaphoreType.DMA((chunks,)),
        ],
        compiler_params=params(),
        name="project_qkv",
    )(inputs, gain, table, weight)


def fold_lanes(values, combine):
    blocks = [values[:, i : i + LANES] for i in range(0, values.shape[1], LANES)]
    while len(blocks) > 1:
        pairs = [combine(a, b) for a, b in zip(blocks[::2], blocks[1::2])]
        blocks = pairs + blocks[2 * len(pairs) :]
    return blocks[0]


def attention_kernel(peers, *refs):
    piece_refs, refs = refs[:peers], refs[peers:]
    table_ref, starts, lengths, split, packed_ref, long_ref, out_ref = refs[:7]
    (rope, packed, far, queries, keys, values, scores, far_scores, far_state, merged_rows) = refs[7:17]
    packed_sem, far_sems = refs[17:]
    group = lax.axis_index("req")
    blocks = out_ref.shape[0] // 2
    heads = QUERY_HEADS // KEY_VALUE_HEADS
    pairs = 2 * heads
    window = scores.shape[2] // 2
    slots = packed.shape[0]
    far_chunks = far.shape[1] // FAR_SLOTS
    scale = 1.0 / math.sqrt(HEAD_SIZE)
    live = [split[0, 0], split[1, 0]]

    def far_copy(j, c):
        return pltpu.make_async_copy(
            long_ref.at[0, j, pl.ds(c * FAR_SLOTS, FAR_SLOTS)],
            far.at[j, pl.ds(c * FAR_SLOTS, FAR_SLOTS)],
            far_sems.at[j, c],
        )

    packed_copy = pltpu.make_async_copy(packed_ref.at[0], packed, packed_sem)
    packed_copy.start()
    for j in range(2):
        for c in range(far_chunks):

            @pl.when(c * FAR_SLOTS < live[j])
            def _():
                far_copy(j, c).start()

    width = HEAD_SIZE * (heads + 2)
    scale_rows = row_scale([piece[:, width:] for piece in piece_refs])
    tables = [piece[2 * blocks :, width:].astype(jnp.float32) for piece in piece_refs]
    tables = [t[4:5] + t[5:6] for t in tables]
    far_tables = [
        sum(
            jnp.where(lax.bitwise_xor(group, d) == j * (peers // 2), t, 0.0)
            for d, t in enumerate(tables)
        )
        for j in range(2)
    ]
    own_table = table_ref[...]
    table = jnp.concatenate(
        [own_table, own_table] + far_tables * 2 + [jnp.zeros((blocks - 4, HEAD_SIZE), jnp.float32)], 0
    )
    turned = pltpu.roll(table, HEAD_SIZE // 2, 1)
    lower = lax.broadcasted_iota(jnp.int32, table.shape, 1) < HEAD_SIZE // 2
    cosine = jnp.where(lower, table, turned)
    sine = jnp.where(lower, -turned, table)
    for b in range(heads + 2):
        lanes = slice(b * HEAD_SIZE, (b + 1) * HEAD_SIZE)
        block = sum(piece[:, lanes].astype(jnp.float32) for piece in piece_refs) * scale_rows
        if b <= heads:
            block = block * cosine + pltpu.roll(block, HEAD_SIZE // 2, 1) * sine
        block = block.astype(jnp.bfloat16).astype(jnp.float32)
        rope[:, lanes] = block
        for k in range(2):
            own_rows = block[k * blocks : (k + 1) * blocks]
            if b < heads:
                queries[:, k * heads + b, :] = own_rows
            else:
                for h in range(heads):
                    (keys if b == heads else values)[:, k * heads + h, :] = own_rows

    def same_head(columns):
        row = lax.broadcasted_iota(jnp.int32, (pairs, columns), 0)
        column = lax.broadcasted_iota(jnp.int32, (pairs, columns), 1)
        return (row // heads) == (column % 2), column // 2

    def contract(a, b):
        return lax.dot_general(a, b, (((1,), (1,)), ((), ())), preferred_element_type=jnp.float32)

    packed_copy.wait()
    matching, slot = same_head(2 * window)
    first_slots = []
    for r in range(blocks):
        first = jnp.minimum(starts[r], slots - window)
        first_slots.append(first)
        low = starts[r] - first
        segment = packed[pl.ds(first, window), :, 0:HEAD_SIZE].reshape(2 * window, HEAD_SIZE)
        own = contract(queries[r].astype(jnp.bfloat16), segment) * scale
        inside = matching & (slot >= low) & (slot < low + lengths[r])
        scores[r] = jnp.where(inside, own, LOWEST)
    own_score = jnp.sum(queries[...] * keys[...], axis=-1, keepdims=True) * scale
    row_max = jnp.maximum(jnp.max(scores[...], axis=-1, keepdims=True), own_score)
    weights = jnp.exp(scores[...] - row_max).astype(jnp.bfloat16)
    own_weight = jnp.exp(own_score - row_max).astype(jnp.bfloat16).astype(jnp.float32)
    totals = jnp.sum(weights.astype(jnp.float32), axis=-1, keepdims=True) + own_weight
    near_peak = row_max[0] + jnp.log(totals[0])
    for r in range(blocks):
        segment = packed[pl.ds(first_slots[r], window), :, HEAD_SIZE:].reshape(2 * window, HEAD_SIZE)
        summed = jnp.dot(weights[r], segment, preferred_element_type=jnp.float32)
        summed = summed + own_weight[r] * values[r]
        merged_rows[r] = summed / totals[r]

    matching, slot = same_head(2 * FAR_SLOTS)
    for j in range(2):
        long_rows = jnp.concatenate(
            [
                rope[2 * blocks + 2 * k + j : 2 * blocks + 2 * k + j + 1, h * HEAD_SIZE : (h + 1) * HEAD_SIZE]
                for k in range(2)
                for h in range(heads)
            ],
            0,
        ).astype(jnp.bfloat16)
        far_state[0] = jnp.full((pairs, LANES), LOWEST, jnp.float32)
        far_state[1] = jnp.zeros((pairs, LANES), jnp.float32)
        far_state[2] = jnp.zeros((pairs, HEAD_SIZE), jnp.float32)

        def rows_of(c, first):
            part = far[j, c * FAR_SLOTS : (c + 1) * FAR_SLOTS, :, first : first + HEAD_SIZE]
            return part.reshape(2 * FAR_SLOTS, HEAD_SIZE)

        for c in range(far_chunks):

            @pl.when(c * FAR_SLOTS < live[j])
            def _():
                far_copy(j, c).wait()
                found = contract(long_rows, rows_of(c, 0)) * scale
                found = jnp.where(matching & (slot < live[j] - c * FAR_SLOTS), found, LOWEST)
                far_scores[c] = found
                far_state[0] = jnp.maximum(far_state[0], fold_lanes(found, jnp.maximum))

        peak = jnp.max(far_state[0], axis=-1, keepdims=True)
        for c in range(far_chunks):

            @pl.when(c * FAR_SLOTS < live[j])
            def _():
                weight = jnp.exp(far_scores[c] - peak).astype(jnp.bfloat16)
                far_state[1] = far_state[1] + fold_lanes(weight.astype(jnp.float32), jnp.add)
                far_state[2] = far_state[2] + jnp.dot(
                    weight, rows_of(c, HEAD_SIZE), preferred_element_type=jnp.float32
                )

        total = jnp.sum(far_state[1], axis=-1, keepdims=True)
        summed = far_state[2]
        far_peak = peak + jnp.log(total)
        result = summed / total
        owner = group == j * (peers // 2)
        top = jnp.maximum(far_peak, near_peak)
        far_part = jnp.exp(far_peak - top)
        near_part = jnp.exp(near_peak - top)
        both = far_part + near_part
        result = jnp.where(owner, (result * far_part + merged_rows[0] * near_part) / both, result)
        log_total = jnp.where(owner, top + jnp.log(both), far_peak)
        high, low = split_parts(log_total)
        merged_rows[blocks + j] = result
        merged_rows[blocks + 2 + j] = jnp.broadcast_to(high.astype(jnp.float32), result.shape)
        merged_rows[blocks + 4 + j] = jnp.broadcast_to(low.astype(jnp.float32), result.shape)
    merged_rows[blocks + 6 :] = jnp.zeros((blocks - 6, pairs, HEAD_SIZE), jnp.float32)
    for b in range(pairs):
        out_ref[:, b * HEAD_SIZE : (b + 1) * HEAD_SIZE] = merged_rows[:, b, :].astype(jnp.bfloat16)


def attend(pieces, table, starts, lengths, split, packed_cache, long_cache):
    peers = len(pieces)
    blocks = pieces[0].shape[0] // 3
    heads = QUERY_HEADS // KEY_VALUE_HEADS
    pairs = 2 * heads
    slots = packed_cache.shape[1]
    far_slots = long_cache.shape[2]
    return pl.pallas_call(
        functools.partial(attention_kernel, peers),
        out_shape=jax.ShapeDtypeStruct((2 * blocks, pairs * HEAD_SIZE), jnp.bfloat16),
        in_specs=in_vmem(peers + 1) + in_smem(3) + in_hbm(2),
        out_specs=pl.BlockSpec(memory_space=pltpu.VMEM),
        scratch_shapes=[
            pltpu.VMEM((3 * blocks, (heads + 2) * HEAD_SIZE), jnp.float32),
            pltpu.VMEM((slots, 2, 2 * HEAD_SIZE), jnp.bfloat16),
            pltpu.VMEM((2, far_slots, 2, 2 * HEAD_SIZE), jnp.bfloat16),
            pltpu.VMEM((blocks, pairs, HEAD_SIZE), jnp.float32),
            pltpu.VMEM((blocks, pairs, HEAD_SIZE), jnp.float32),
            pltpu.VMEM((blocks, pairs, HEAD_SIZE), jnp.float32),
            pltpu.VMEM((blocks, pairs, 2 * MOST_SLOTS), jnp.float32),
            pltpu.VMEM((far_slots // FAR_SLOTS, pairs, 2 * FAR_SLOTS), jnp.float32),
            pltpu.VMEM((3, pairs, LANES), jnp.float32),
            pltpu.VMEM((2 * blocks, pairs, HEAD_SIZE), jnp.float32),
            pltpu.SemaphoreType.DMA,
            pltpu.SemaphoreType.DMA((2, far_slots // FAR_SLOTS)),
        ],
        compiler_params=params(),
        name="attend",
    )(*pieces, table, starts, lengths, split, packed_cache, long_cache)


def start_column_copies(weight_at, weights, sems):
    copies = []
    for c, (start, width) in enumerate(column_chunks(weight_at.shape[1])):
        lanes = pl.ds(start, width)
        copies.append(
            pltpu.make_async_copy(weight_at.at[:, lanes], weights.at[:, lanes], sems.at[c])
        )
    for copy in copies:
        copy.start()
    return copies


def multiply_columns(rows_ref, weights, copies, outs):
    half = weights.shape[1] // len(outs)
    for copy, (start, width) in zip(copies, column_chunks(weights.shape[1])):
        copy.wait()
        result = jnp.dot(
            rows_ref[...], weights[:, start : start + width], preferred_element_type=jnp.float32
        ).astype(jnp.bfloat16)
        for h, out in enumerate(outs):
            first, last = max(start, h * half), min(start + width, (h + 1) * half)
            if first < last:
                out[:, first - h * half : last - h * half] = result[:, first - start : last - start]


def output_kernel(peers, *refs):
    piece_refs, refs = refs[:peers], refs[peers:]
    weight_ref, outs, (whole, weights, sems) = refs[0], refs[1:3], refs[3:]
    group = lax.axis_index("req")
    blocks = piece_refs[0].shape[0] // 2
    copies = start_column_copies(weight_ref, weights, sems)
    for d, piece in enumerate(piece_refs):
        start = pl.multiple_of(lax.bitwise_xor(group, d) * blocks, blocks)
        whole[pl.ds(start, blocks)] = piece[0:blocks]
    extras = [piece[blocks:].astype(jnp.float32) for piece in piece_refs]
    for j in range(2):
        peaks = [e[2 + j : 3 + j] + e[4 + j : 5 + j] for e in extras]
        top = functools.reduce(jnp.maximum, peaks)
        parts = [jnp.exp(peak - top) for peak in peaks]
        merged_row = sum(e[j : j + 1] * part for e, part in zip(extras, parts)) / sum(parts)
        rows = slice(j * (peers // 2) * blocks, j * (peers // 2) * blocks + blocks)
        row = lax.broadcasted_iota(jnp.int32, (blocks, whole.shape[1]), 0)
        whole[rows] = jnp.where(
            row == 0, merged_row, whole[rows].astype(jnp.float32)
        ).astype(jnp.bfloat16)
    multiply_columns(whole, weights, copies, outs)


def down_kernel(peers, *refs):
    piece_refs, refs = refs[:peers], refs[peers:]
    weight_ref, outs, (whole, weights, sems) = refs[0], refs[1:3], refs[3:]
    group = lax.axis_index("req")
    copies = start_column_copies(weight_ref.at[0], weights, sems)
    for d, piece in enumerate(piece_refs):
        width = piece.shape[1]
        start = pl.multiple_of(lax.bitwise_xor(group, d) * width, LANES)
        whole[:, pl.ds(start, width)] = piece[...]
    multiply_columns(whole, weights, copies, outs)


def project_columns(kernel, pieces, weight, rows, name):
    depth, width = weight.shape[-2:]
    chunks = len(column_chunks(width))
    return pl.pallas_call(
        functools.partial(kernel, len(pieces)),
        out_shape=[jax.ShapeDtypeStruct((rows, width // 2), jnp.bfloat16)] * 2,
        in_specs=in_vmem(len(pieces)) + in_hbm(1),
        out_specs=in_vmem(2),
        scratch_shapes=[
            pltpu.VMEM((rows, depth), jnp.bfloat16),
            pltpu.VMEM((depth, width), jnp.bfloat16),
            pltpu.SemaphoreType.DMA((chunks,)),
        ],
        compiler_params=params(),
        name=name,
    )(*pieces, weight)


def project_output(pieces, weight):
    rows = len(pieces) * pieces[0].shape[0] // 2
    return project_columns(output_kernel, pieces, weight, rows, "project_output")


def project_down(pieces, weight):
    return project_columns(down_kernel, pieces, weight, pieces[0].shape[0], "project_down")


def gate_up_kernel(peers, inputs_ref, gain_ref, weight_ref, *refs):
    outs, (wide, weights, total, sems) = refs[:peers], refs[peers:]
    group = lax.axis_index("req")
    rows, depth = inputs_ref.shape
    copies = start_pair_copies(weight_ref, weights, sems)
    expand_rows(scale_columns(inputs_ref[...], gain_ref[...]), wide)
    sums = sum_columns(inputs_ref[...]).astype(jnp.bfloat16)
    for copy, (start, size) in zip(copies, column_chunks(total.shape[1])):
        copy.wait()
        total[:, start : start + size] = jnp.dot(
            wide[...],
            weights[:, :, start : start + size].reshape(2 * depth, size),
            preferred_element_type=jnp.float32,
        ).astype(jnp.bfloat16)
    width = total.shape[1] // peers
    for d in range(peers):
        start = pl.multiple_of(lax.bitwise_xor(group, d) * width, LANES)
        outs[d][:, 0:width] = total[:, pl.ds(start, width)]
        outs[d][0:rows, width:] = sums
        outs[d][rows:, width:] = sums


def project_gate_up(inputs, gain, weight, peers):
    rows = inputs.shape[0]
    depth, pair, width = weight.shape[1:]
    chunks = len(column_chunks(width))
    return pl.pallas_call(
        functools.partial(gate_up_kernel, peers),
        out_shape=[jax.ShapeDtypeStruct((pair * rows, width // peers + LANES), jnp.bfloat16)] * peers,
        in_specs=in_vmem(2) + in_hbm(1),
        out_specs=in_vmem(peers),
        scratch_shapes=[
            pltpu.VMEM((pair * rows, pair * depth), jnp.bfloat16),
            pltpu.VMEM((depth, pair, width), jnp.bfloat16),
            pltpu.VMEM((pair * rows, width), jnp.bfloat16),
            pltpu.SemaphoreType.DMA((chunks,)),
        ],
        compiler_params=params(),
        name="project_gate_up",
    )(inputs, gain, weight)


def hidden_kernel(peers, *refs):
    piece_refs, out_ref = refs[:peers], refs[peers]
    rows, width = out_ref.shape
    factor = row_scale([piece[0:rows, width:] for piece in piece_refs])

    def summed(first):
        return sum(piece[first : first + rows, 0:width].astype(jnp.float32) for piece in piece_refs) * factor

    gate, up = summed(0), summed(rows)
    out_ref[...] = (gate / (1.0 + jnp.exp(-gate)) * up).astype(jnp.bfloat16)


def gated_units(pieces):
    rows, width = pieces[0].shape[0] // 2, pieces[0].shape[1] - LANES
    return pl.pallas_call(
        functools.partial(hidden_kernel, len(pieces)),
        out_shape=jax.ShapeDtypeStruct((rows, width), jnp.bfloat16),
        in_specs=in_vmem(len(pieces)),
        out_specs=pl.BlockSpec(memory_space=pltpu.VMEM),
        compiler_params=pltpu.CompilerParams(vmem_limit_bytes=16 * 2**20),
        name="gated_units",
    )(*pieces)


def fast_layer(section, inputs, attention_gain, query_key_value_weight, head_output_weight, feedforward_gain, gate_up, down_weight, packed_cache, long_cache, table, *segments):
    req_count = lax.axis_size("req")
    terms = project_qkv(inputs, attention_gain, table, query_key_value_weight, req_count)
    own = attend(swap_all(terms, "req", section), table, *segments, packed_cache, long_cache)
    out_weight = head_output_weight.reshape(-1, head_output_weight.shape[3])
    attended = project_output(spread(own, "req", section), out_weight)
    attended = sum_doubling(attended, "head", section)
    residual = (inputs.astype(jnp.float32) + attended).astype(jnp.bfloat16)
    terms = project_gate_up(residual, feedforward_gain, gate_up, req_count)
    hidden = gated_units(swap_all(terms, "req", section))
    lowered = project_down(spread(hidden, "req", section), down_weight)
    lowered = sum_doubling(lowered, "head", section)
    return (residual.astype(jnp.float32) + lowered).astype(jnp.bfloat16)


def rope_table(lengths):
    req_count, group = lax.axis_size("req"), lax.axis_index("req")
    owner = (group == 0) | (group == req_count // 2)
    long_row = (jnp.arange(lengths.shape[1]) == 0) & owner
    position = lengths[0] + jnp.where(long_row, LONG, 0).astype(jnp.int32)
    half_dim = HEAD_SIZE // 2
    inverse = 1.0 / 10000.0 ** (jnp.arange(half_dim).astype(jnp.float32) * 2.0 / HEAD_SIZE)
    angles = position.astype(jnp.float32)[:, None] * inverse[None, :]
    return jnp.concatenate([jnp.cos(angles), jnp.sin(angles)], 1)


def fast_local(tokens, attention_gain, query_key_value_weight, head_output_weight, feedforward_gain, gate_up, down_weight, packed_cache, long_cache, lengths, long_split):
    layer_arrays = (
        attention_gain,
        query_key_value_weight,
        head_output_weight,
        feedforward_gain,
        gate_up,
        down_weight,
        packed_cache,
        long_cache,
        rope_table(lengths),
        jnp.cumsum(lengths[0]) - lengths[0],
        lengths[0],
        long_split,
    )
    first = fast_layer(0, tokens, *layer_arrays)
    second = fast_layer(1, swap(first, "head", 0, 0, 1), *layer_arrays)
    return jnp.where(lax.axis_index("section") == 0, first, second)[None]


def is_power_of_two(value):
    return value & (value - 1) == 0


def fits_fast(mesh):
    req_count, head_count = mesh.shape["req"], mesh.shape["head"]
    columns = MODEL_WIDTH // req_count
    return (
        mesh.shape["section"] == 2
        and is_power_of_two(req_count)
        and is_power_of_two(head_count)
        and KEY_VALUE_HEADS == 2 * head_count
        and columns % COLUMNS == 0
        and FF % (head_count * COLUMNS) == 0
        and FF % (head_count * req_count * LANES) == 0
    )


def solution(mesh):
    placed = (
        P(None, "req"),
        P("section", "req"),
        P("section", "req", "head", None),
        P("section", "head", None, "req"),
        P("section", "req"),
        P("section", "req", None, "head"),
        P("section", "head", "req"),
        P("section", "req", "head", None),
        P("section", None, "req", "head", None),
        P("req", None),
        P(None, "req"),
    )
    return jax.shard_map(
        fast_local if fits_fast(mesh) else local,
        mesh=mesh,
        in_specs=placed, out_specs=P("section", None, "req"), check_vma=False
    )
```

```python
import functools
import math

import jax
import jax.numpy as jnp
from jax import lax
from jax.experimental import pallas as pl
from jax.experimental.pallas import tpu as pltpu
from jax.sharding import PartitionSpec as P

MODEL_WIDTH = 8192
QUERY_HEADS = 64
KEY_VALUE_HEADS = 8
HEAD_SIZE = 128
LONG = 16384
FF = 14336
MOST_SLOTS = 256
LANES = 128
COLUMNS = 512
VMEM_MEBIBYTES = 50
FAR_SLOTS = 2048
LOWEST = -1e30


EPSILON = 1e-05


def merged(part, axis, combine):
    gathered = jax.tree.map(lambda a: lax.all_gather(a, axis), part)

    def take(source):
        return jax.tree.map(lambda a: lax.dynamic_index_in_dim(a, source, 0, False), gathered)

    return lax.fori_loop(
        1, lax.axis_size(axis), lambda source, state: combine(state, take(source)), take(0)
    )


def shifted(value, axis, by):
    peers = lax.axis_size(axis)
    pairs = [(i, i + by) for i in range(peers) if 0 <= i + by < peers]
    return lax.ppermute(value, axis, pairs)


def rotate(values, position):
    half_dim = values.shape[-1] // 2
    freq_ids = jnp.arange(half_dim).astype(jnp.float32)
    inverse = 1.0 / 10000.0 ** (freq_ids * 2.0 / values.shape[-1])
    angles = position.astype(jnp.float32)[:, None] * inverse[None, :]
    cosine = jnp.cos(angles)[:, None, None, :]
    sine_part = jnp.sin(angles)[:, None, None, :]
    lower_half = values[..., :half_dim]
    upper_half = values[..., half_dim:]
    return jnp.concatenate(
        [
            lower_half * cosine - upper_half * sine_part,
            upper_half * cosine + lower_half * sine_part,
        ],
        -1,
    )


def add_pair(earlier, second_part):
    return earlier + second_part


def combine_partial(earlier, second_part):
    peak = jnp.maximum(earlier[0], second_part[0])
    left_factor = jnp.exp(earlier[0] - peak)
    right_factor = jnp.exp(second_part[0] - peak)
    softmax_total = earlier[1] * left_factor + second_part[1] * right_factor
    weighted_sum = earlier[2] * left_factor[..., None] + second_part[2] * right_factor[..., None]
    return (peak, softmax_total, weighted_sum)


def over_requests(values, combiner):
    return merged(values, "req", combiner)


def rows_apply(values, row_fn):
    return row_fn(lax.all_gather(values, "req", axis=0, tiled=True), jnp.int32(0))


def rows_project(term_fn, row_count):
    return lax.psum_scatter(
        term_fn(jnp.int32(0), row_count * lax.axis_size("req")),
        "req",
        scatter_dimension=0,
        tiled=True,
    )


def head_total(values):
    return lax.psum(values, "head")


def keep_rows(piece_rows, start_row):
    return piece_rows


def norm_rows(values, gain_row):
    floats = values.astype(jnp.float32)
    squares = over_requests(jnp.sum(floats * floats, axis=-1), add_pair)
    return (
        floats * lax.rsqrt(squares / MODEL_WIDTH + EPSILON)[:, None] * gain_row.astype(jnp.float32)
    ).astype(jnp.bfloat16)


def decoder_layer(
    inputs,
    micro_batch,
    attention_gain,
    query_key_value_weight,
    head_output_weight,
    feedforward_gain,
    gate_up,
    down_weight,
    packed_cache,
    long_cache,
    lengths,
    long_split,
):
    req_count = lax.axis_size("req")
    group_index = lax.axis_index("req")
    blocks = inputs.shape[0] // req_count
    columns = query_key_value_weight.shape[1]
    kv_local = query_key_value_weight.shape[2]
    requests_per_group = QUERY_HEADS // KEY_VALUE_HEADS
    score_scale = 1.0 / math.sqrt(HEAD_SIZE)
    normalized_input = norm_rows(inputs, attention_gain[0])
    in_weights = query_key_value_weight[0].reshape(
        columns, kv_local * (requests_per_group + 2) * HEAD_SIZE
    )

    def qkv_term(start_row, row_count):
        return jnp.dot(normalized_input, in_weights, preferred_element_type=jnp.float32)

    projected_rows = rows_project(qkv_term, blocks).reshape(
        blocks, kv_local, requests_per_group + 2, HEAD_SIZE
    )
    local_rows = jnp.arange(blocks)
    row_lengths = lengths[0]
    owner_long = (group_index == 0) | (group_index == req_count // 2)
    long_row = (local_rows == 0) & (micro_batch == 0) & owner_long
    position = row_lengths + jnp.where(long_row, LONG, 0).astype(jnp.int32)
    queries = rotate(projected_rows[:, :, :requests_per_group], position).astype(jnp.bfloat16)
    new_key = rotate(projected_rows[:, :, requests_per_group : requests_per_group + 1], position)[
        :, :, 0
    ].astype(jnp.bfloat16)
    new_value = projected_rows[:, :, requests_per_group + 1].astype(jnp.bfloat16)
    gathered = rows_apply(
        queries[0:1].reshape(1, kv_local * requests_per_group * HEAD_SIZE), keep_rows
    )
    long_queries = jnp.stack([gathered[0], gathered[req_count // 2]]).reshape(
        2, kv_local, requests_per_group, HEAD_SIZE
    )
    far_cache = long_cache[0]
    far_live = (jnp.arange(far_cache.shape[1])[None, :] < long_split[:, 0][:, None])[
        :, None, None, :
    ]
    far_scores = (
        jnp.einsum(
            "jkhd,jpkd->jkhp",
            long_queries,
            far_cache[..., :HEAD_SIZE],
            preferred_element_type=jnp.float32,
        )
        * score_scale
    )
    far_max = jnp.max(jnp.where(far_live, far_scores, -jnp.inf), axis=-1)
    far_weights = jnp.where(
        far_live, jnp.exp(jnp.where(far_live, far_scores - far_max[..., None], 0.0)), 0.0
    ).astype(jnp.bfloat16)
    far_totals = jnp.sum(far_weights.astype(jnp.float32), axis=-1)
    far_summed = jnp.einsum(
        "jkhp,jpkd->jkhd",
        far_weights,
        far_cache[..., HEAD_SIZE:],
        preferred_element_type=jnp.float32,
    )
    far_max, far_totals, far_summed = over_requests(
        (far_max, far_totals, far_summed), combine_partial
    )
    far_index = jnp.where(group_index == 0, 0, 1)
    chosen_max = lax.dynamic_index_in_dim(far_max, far_index, 0, keepdims=False)
    chosen_totals = lax.dynamic_index_in_dim(far_totals, far_index, 0, keepdims=False)
    chosen_summed = lax.dynamic_index_in_dim(far_summed, far_index, 0, keepdims=False)
    pack_part = packed_cache[0]
    seg_ends = jnp.cumsum(lengths[0])
    slot_ids = jnp.arange(pack_part.shape[0])
    slot_owner = jnp.sum((slot_ids[:, None] >= seg_ends[None, :]).astype(jnp.int32), axis=1)
    request_ids = micro_batch * blocks + local_rows
    in_segment = (slot_owner[None, :] == request_ids[:, None])[:, None, None, :]
    scores = (
        jnp.einsum(
            "rkhd,pkd->rkhp",
            queries,
            pack_part[..., :HEAD_SIZE],
            preferred_element_type=jnp.float32,
        )
        * score_scale
    )
    own_score = (
        jnp.einsum("rkhd,rkd->rkh", queries, new_key, preferred_element_type=jnp.float32)
        * score_scale
    )
    row_max = jnp.maximum(jnp.max(jnp.where(in_segment, scores, -jnp.inf), axis=-1), own_score)
    long_mask = long_row[:, None, None]
    row_max = jnp.where(long_mask, jnp.maximum(row_max, chosen_max[None]), row_max)
    weights = jnp.where(
        in_segment, jnp.exp(jnp.where(in_segment, scores - row_max[..., None], 0.0)), 0.0
    ).astype(jnp.bfloat16)
    own_weights = jnp.exp(own_score - row_max).astype(jnp.bfloat16)
    far_factor = jnp.where(
        long_mask, jnp.exp(jnp.where(long_mask, chosen_max[None] - row_max, 0.0)), 0.0
    )
    softmax_total = (
        jnp.sum(weights.astype(jnp.float32), axis=-1)
        + own_weights.astype(jnp.float32)
        + far_factor * chosen_totals[None]
    )
    weighted_sum = jnp.einsum(
        "rkhp,pkd->rkhd", weights, pack_part[..., HEAD_SIZE:], preferred_element_type=jnp.float32
    )
    weighted_sum = (
        weighted_sum
        + own_weights.astype(jnp.float32)[..., None] * new_value.astype(jnp.float32)[:, :, None, :]
    )
    weighted_sum = weighted_sum + far_factor[..., None] * chosen_summed[None]
    attended_heads = (
        (weighted_sum / softmax_total[..., None])
        .astype(jnp.bfloat16)
        .reshape(blocks, kv_local * requests_per_group * HEAD_SIZE)
    )
    out_weights = head_output_weight[0].reshape(kv_local * requests_per_group * HEAD_SIZE, columns)

    def project_heads(piece_rows, start_row):
        return jnp.dot(piece_rows, out_weights, preferred_element_type=jnp.float32)

    attended = head_total(rows_apply(attended_heads, project_heads))
    residual = (inputs.astype(jnp.float32) + attended).astype(jnp.bfloat16)
    normed_two = norm_rows(residual, feedforward_gain[0])
    ff_weights = gate_up[0].reshape(columns, -1)

    def ff_term(start_row, row_count):
        return jnp.dot(normed_two, ff_weights, preferred_element_type=jnp.float32)

    gate_and_up = rows_project(ff_term, blocks)
    hidden_width = gate_and_up.shape[1] // 2
    hidden = (jax.nn.silu(gate_and_up[:, :hidden_width]) * gate_and_up[:, hidden_width:]).astype(
        jnp.bfloat16
    )
    lower_weights = down_weight[0]

    def project_hidden(piece_rows, start_row):
        return jnp.dot(piece_rows, lower_weights, preferred_element_type=jnp.float32)

    lowered = head_total(rows_apply(hidden, project_hidden))
    return (residual.astype(jnp.float32) + lowered).astype(jnp.bfloat16)


def local(
    tokens,
    attention_gain,
    query_key_value_weight,
    head_output_weight,
    feedforward_gain,
    gate_up,
    down_weight,
    packed_cache,
    long_cache,
    lengths,
    long_split,
):
    req_count = lax.axis_size("req")
    section_index = lax.axis_index("section")
    batch_count = 1
    per_group = tokens.shape[0] // req_count
    blocks = per_group // batch_count
    columns = tokens.shape[1]
    token_grid = tokens.reshape(req_count, per_group, columns)
    result = jnp.zeros_like(token_grid)
    incoming = jnp.zeros((req_count * blocks, columns), jnp.bfloat16)
    for phase_step in range(batch_count + 1):
        micro_batch = phase_step - section_index
        is_active = (micro_batch >= 0) & (micro_batch < batch_count)
        micro_batch = jnp.clip(micro_batch, 0, batch_count - 1)
        new_batch = token_grid.reshape(req_count * blocks, columns)
        inputs = jnp.where(section_index == 0, new_batch, incoming)
        output = decoder_layer(
            inputs,
            micro_batch,
            attention_gain,
            query_key_value_weight,
            head_output_weight,
            feedforward_gain,
            gate_up,
            down_weight,
            packed_cache,
            long_cache,
            lengths,
            long_split,
        )
        placed = output.reshape(req_count, blocks, columns)
        result = jnp.where(is_active, placed, result)
        if phase_step < batch_count:
            incoming = shifted(output, "section", 1)
    return result.reshape(1, req_count * per_group, columns)

def swap(value, axis, distance, section, target_section=None):
    size = lax.axis_size(axis)
    target_section = section if target_section is None else target_section
    pairs = [(section * size + i, target_section * size + (i ^ distance)) for i in range(size)]
    return lax.ppermute(value, ("section", axis), pairs)


def swap_all(values, axis, section):
    received = {d: swap(values[d], axis, d, section) for d in reversed(range(1, len(values)))}
    return [values[0]] + [received[d] for d in range(1, len(values))]


def spread(value, axis, section):
    return swap_all([value] * lax.axis_size(axis), axis, section)


def sum_doubling(value, axis, section):
    distance = 2
    total = value.astype(jnp.float32)
    while distance < lax.axis_size(axis):
        other = swap(value, axis, distance, section)
        total = value.astype(jnp.float32) + other.astype(jnp.float32)
        value = total.astype(jnp.bfloat16)
        distance *= 2
    return total


def finish_sum(sent, kept, axis, section):
    pair = kept.astype(jnp.float32) + swap(sent, axis, 1, section).astype(jnp.float32)
    return sum_doubling(pair.astype(jnp.bfloat16), axis, section)


def half_start(other, half):
    index = lax.bitwise_and(lax.axis_index("head"), 1)
    return (1 - index if other else index) * half


def in_vmem(count):
    return [pl.BlockSpec(memory_space=pltpu.VMEM)] * count


def in_hbm(count):
    return [pl.BlockSpec(memory_space=pltpu.HBM)] * count


def in_smem(count):
    return [pl.BlockSpec(memory_space=pltpu.SMEM)] * count


def params():
    return pltpu.CompilerParams(vmem_limit_bytes=VMEM_MEBIBYTES * 2**20)


def column_chunks(width):
    edge = COLUMNS // 2
    starts = [0] + list(range(edge, width - edge, COLUMNS)) + [width - edge]
    return [(a, b - a) for a, b in zip(starts, starts[1:] + [width]) if b > a]


def split_parts(value):
    high = value.astype(jnp.bfloat16)
    low = (value - high.astype(jnp.float32)).astype(jnp.bfloat16)
    return high, low


def sum_squares(values):
    floats = values.astype(jnp.float32)
    return jnp.sum(floats * floats, axis=-1, keepdims=True)


def in_lanes(columns):
    rows = columns[0].shape[0]
    lane = lax.broadcasted_iota(jnp.int32, (rows, LANES), 1)
    block = jnp.zeros((rows, LANES), jnp.float32)
    for i, column in enumerate(columns):
        high, low = split_parts(column)
        block = jnp.where(lane == 2 * i, high.astype(jnp.float32), block)
        block = jnp.where(lane == 2 * i + 1, low.astype(jnp.float32), block)
    return block


def from_lanes(block, i):
    return block[:, 2 * i : 2 * i + 1] + block[:, 2 * i + 1 : 2 * i + 2]


def row_scale(squares):
    return lax.rsqrt(squares / MODEL_WIDTH + EPSILON)


def expand_rows(scaled, wide_ref):
    rows, columns = scaled.shape
    chunk = 2 * LANES
    source = lax.broadcasted_iota(jnp.int32, (chunk, 2 * chunk), 0)
    target = lax.broadcasted_iota(jnp.int32, (chunk, 2 * chunk), 1)
    count = columns // chunk
    stacked = jnp.concatenate([scaled[:, c * chunk : (c + 1) * chunk] for c in range(count)], 0)
    for half in range(2):
        select = jnp.where(target == 2 * source + half, 1.0, 0.0).astype(jnp.bfloat16)
        spread = jnp.dot(stacked, select, preferred_element_type=jnp.float32).astype(jnp.bfloat16)
        for c in range(count):
            wide_ref[half * rows : (half + 1) * rows, 2 * c * chunk : 2 * (c + 1) * chunk] = spread[
                c * rows : (c + 1) * rows
            ]


def scale_columns(values, gain):
    return (values.astype(jnp.float32) * gain.astype(jnp.float32)).astype(jnp.bfloat16)


def multiply_halves(others, add, refs):
    count = len(others)
    input_refs, refs = refs[:count], refs[count:]
    (gain_ref, weight_ref), refs = refs[:2], refs[2:]
    if add:
        (partial_ref, squares_ref), refs = refs[:2], refs[2:]
    rest, (wide, weights, total, sems) = refs[:-4], refs[-4:]
    half = input_refs[0].shape[1]
    starts = [pl.multiple_of(half_start(other, half), half) for other in others]
    chunks = column_chunks(total.shape[1])
    copies = [
        [
            pltpu.make_async_copy(
                weight_ref.at[0, pl.ds(first, half), :, pl.ds(start, width)],
                weights.at[pl.ds(p * half, half), :, pl.ds(start, width)],
                sems.at[p, c],
            )
            for p, first in enumerate(starts)
        ]
        for c, (start, width) in enumerate(chunks)
    ]
    for parts in copies:
        for copy in parts:
            copy.start()
    scaled = [
        scale_columns(ref[...], gain_ref[:, pl.ds(first, half)])
        for ref, first in zip(input_refs, starts)
    ]
    expand_rows(jnp.concatenate(scaled, 1), wide)
    squares = sum(sum_squares(ref[...]) for ref in input_refs)
    if add:
        squares = squares + squares_ref[:, 0:1]

    def fill():
        for parts, (start, width) in zip(copies, chunks):
            for copy in parts:
                copy.wait()
            lanes = slice(start, start + width)
            result = jnp.dot(
                wide[...],
                weights[:, :, lanes].reshape(wide.shape[1], width),
                preferred_element_type=jnp.float32,
            )
            total[:, lanes] = result + partial_ref[:, lanes] if add else result

    return rest, squares, total, fill


def partial_kernel(others, *refs):
    (partial_out, squares_out), squares, total, fill = multiply_halves(others, False, refs)
    squares_out[...] = jnp.broadcast_to(squares, squares_out.shape)
    fill()
    partial_out[...] = total[...]


def qkv_kernel(peers, others, add, *refs):
    (table_ref, *outs), squares, total, fill = multiply_halves(others, add, refs)
    group = lax.axis_index("req")
    rows = squares.shape[0]
    blocks = rows // peers
    far = peers // 2 * blocks
    width = total.shape[1]
    long_squares = [jnp.broadcast_to(squares[r : r + 1], squares.shape) for r in (0, far)]
    sums = in_lanes([squares] + long_squares)
    high, low = split_parts(table_ref[0:1])
    table = jnp.concatenate(
        [high.astype(jnp.float32), low.astype(jnp.float32), jnp.zeros((blocks - 2, LANES), jnp.float32)], 0
    ).astype(jnp.bfloat16)
    fill()
    heads = QUERY_HEADS // KEY_VALUE_HEADS
    long_queries = [
        jnp.concatenate(
            [
                total[k * rows + r : k * rows + r + 1, h * HEAD_SIZE : (h + 1) * HEAD_SIZE]
                for k in range(2)
                for h in range(heads)
            ],
            0,
        ).astype(jnp.bfloat16)
        for r in (0, far)
    ]
    for d, out in enumerate(outs):
        peer = pl.multiple_of(lax.bitwise_xor(group, d) * blocks, blocks)
        for k in range(2):
            out[:, k * width : (k + 1) * width] = total[pl.ds(k * rows + peer, blocks)].astype(
                jnp.bfloat16
            )
        out[:, 2 * width + LANES : 2 * width + 2 * LANES] = table
        for j in range(2):
            first = 2 * width + (2 + j) * LANES
            out[:, first : first + LANES] = long_queries[j]
    total[0:rows, 0:LANES] = sums
    for d, out in enumerate(outs):
        peer = pl.multiple_of(lax.bitwise_xor(group, d) * blocks, blocks)
        out[:, 2 * width : 2 * width + LANES] = total[pl.ds(peer, blocks), 0:LANES].astype(jnp.bfloat16)


def gate_up_kernel(peers, others, add, *refs):
    outs, squares, total, fill = multiply_halves(others, add, refs)
    group = lax.axis_index("req")
    rows = squares.shape[0]
    width = total.shape[1] // peers
    sums = in_lanes([squares]).astype(jnp.bfloat16)
    fill()
    for d, out in enumerate(outs):
        start = pl.multiple_of(lax.bitwise_xor(group, d) * width, LANES)
        out[:, 0:width] = total[:, pl.ds(start, width)].astype(jnp.bfloat16)
        out[0:rows, width:] = sums
        out[rows:, width:] = sums


def project_pairs(kernel, others, inputs, gain, weight, partial, extra, out_shapes, name):
    rows, half = inputs[0].shape
    pair, width = weight.shape[2:]
    depth = len(inputs) * half
    operands = [*inputs, gain, weight, *partial, *extra]
    specs = in_vmem(len(inputs) + 1) + in_hbm(1) + in_vmem(len(partial) + len(extra))
    return pl.pallas_call(
        kernel,
        out_shape=out_shapes,
        in_specs=specs,
        out_specs=in_vmem(len(out_shapes)),
        scratch_shapes=[
            pltpu.VMEM((pair * rows, pair * depth), jnp.bfloat16),
            pltpu.VMEM((depth, pair, width), jnp.bfloat16),
            pltpu.VMEM((pair * rows, width), jnp.float32),
            pltpu.SemaphoreType.DMA((len(inputs), len(column_chunks(width)))),
        ],
        compiler_params=params(),
        name=name,
    )(*operands)


def project_early(own, gain, weight, name):
    rows = own.shape[0]
    shapes = [
        jax.ShapeDtypeStruct((2 * rows, weight.shape[3]), jnp.float32),
        jax.ShapeDtypeStruct((rows, LANES), jnp.float32),
    ]
    kernel = functools.partial(partial_kernel, (False,))
    return project_pairs(kernel, (False,), [own], gain, weight, [], [], shapes, name)


def project_qkv(own, other, gain, weight, table, peers, early):
    blocks = own.shape[0] // peers
    shapes = [jax.ShapeDtypeStruct((blocks, 2 * weight.shape[3] + 4 * LANES), jnp.bfloat16)] * peers
    partial = project_early(own, gain, weight, "project_qkv_early") if early else []
    others = (True,) if early else (False, True)
    inputs = [other] if early else [own, other]
    kernel = functools.partial(qkv_kernel, peers, others, early)
    return project_pairs(kernel, others, inputs, gain, weight, partial, [table], shapes, "project_qkv")


def project_gate_up(own, other, gain, weight, peers):
    rows, width = own.shape[0], weight.shape[3] // peers + LANES
    shapes = [jax.ShapeDtypeStruct((2 * rows, width), jnp.bfloat16)] * peers
    partial = project_early(own, gain, weight, "project_gate_up_early")
    kernel = functools.partial(gate_up_kernel, peers, (True,), True)
    return project_pairs(kernel, (True,), [other], gain, weight, partial, [], shapes, "project_gate_up")


def fold_lanes(values, combine):
    blocks = [values[:, i : i + LANES] for i in range(0, values.shape[1], LANES)]
    while len(blocks) > 1:
        pairs = [combine(a, b) for a, b in zip(blocks[::2], blocks[1::2])]
        blocks = pairs + blocks[2 * len(pairs) :]
    return blocks[0]


def attention_kernel(peers, *refs):
    piece_refs, refs = refs[:peers], refs[peers:]
    table_ref, starts, lengths, split, packed_ref, long_ref, out_ref = refs[:7]
    (packed, far, queries, keys, values, scores, far_scores, far_state, merged_rows) = refs[7:16]
    packed_sem, far_sems = refs[16:]
    group = lax.axis_index("req")
    blocks = out_ref.shape[0]
    heads = QUERY_HEADS // KEY_VALUE_HEADS
    pairs = 2 * heads
    window = scores.shape[2] // 2
    slots = packed.shape[0]
    far_chunks = far.shape[1] // FAR_SLOTS
    scale = 1.0 / math.sqrt(HEAD_SIZE)
    live = [split[0, 0], split[1, 0]]

    def far_copy(j, c):
        return pltpu.make_async_copy(
            long_ref.at[0, j, pl.ds(c * FAR_SLOTS, FAR_SLOTS)],
            far.at[j, pl.ds(c * FAR_SLOTS, FAR_SLOTS)],
            far_sems.at[j, c],
        )

    packed_copy = pltpu.make_async_copy(packed_ref.at[0], packed, packed_sem)
    packed_copy.start()
    for j in range(2):
        for c in range(far_chunks):

            @pl.when(c * FAR_SLOTS < live[j])
            def _():
                far_copy(j, c).start()

    width = HEAD_SIZE * (heads + 2)

    def summed_block(start):
        return sum(piece[:, start : start + LANES].astype(jnp.float32) for piece in piece_refs)

    sums = summed_block(2 * width)
    scale_rows = row_scale(from_lanes(sums, 0))
    tables = [
        piece[:, 2 * width + LANES : 2 * width + 2 * LANES].astype(jnp.float32) for piece in piece_refs
    ]
    tables = [t[0:1] + t[1:2] for t in tables]
    far_tables = [
        sum(
            jnp.where(lax.bitwise_xor(group, d) == j * (peers // 2), t, 0.0)
            for d, t in enumerate(tables)
        )
        for j in range(2)
    ]
    def cosine_sine(table):
        turned = pltpu.roll(table, HEAD_SIZE // 2, 1)
        lower = lax.broadcasted_iota(jnp.int32, table.shape, 1) < HEAD_SIZE // 2
        return jnp.where(lower, table, turned), jnp.where(lower, -turned, table)

    def rotated(block, angles):
        cosine, sine = angles
        return block * cosine + pltpu.roll(block, HEAD_SIZE // 2, 1) * sine

    own_angles = cosine_sine(table_ref[...])
    far_queries = [
        rotated(
            summed_block(2 * width + (2 + j) * LANES) * row_scale(from_lanes(sums, 1 + j)),
            cosine_sine(jnp.broadcast_to(far_tables[j], table_ref.shape)),
        ).astype(jnp.bfloat16)
        for j in range(2)
    ]
    for k in range(2):
        for b in range(heads + 2):
            block = summed_block(k * width + b * HEAD_SIZE) * scale_rows
            if b <= heads:
                block = rotated(block, own_angles)
            block = block.astype(jnp.bfloat16).astype(jnp.float32)
            if b < heads:
                queries[:, k * heads + b, :] = block
            else:
                for h in range(heads):
                    (keys if b == heads else values)[:, k * heads + h, :] = block

    def same_head(columns):
        row = lax.broadcasted_iota(jnp.int32, (pairs, columns), 0)
        column = lax.broadcasted_iota(jnp.int32, (pairs, columns), 1)
        return (row // heads) == (column % 2), column // 2

    def contract(a, b):
        return lax.dot_general(a, b, (((1,), (1,)), ((), ())), preferred_element_type=jnp.float32)

    packed_copy.wait()
    matching, slot = same_head(2 * window)
    first_slots = []
    for r in range(blocks):
        first = jnp.minimum(starts[r], slots - window)
        first_slots.append(first)
        low = starts[r] - first
        segment = packed[pl.ds(first, window), :, 0:HEAD_SIZE].reshape(2 * window, HEAD_SIZE)
        own = contract(queries[r].astype(jnp.bfloat16), segment) * scale
        inside = matching & (slot >= low) & (slot < low + lengths[r])
        scores[r] = jnp.where(inside, own, LOWEST)
    own_score = jnp.sum(queries[...] * keys[...], axis=-1, keepdims=True) * scale
    row_max = jnp.maximum(jnp.max(scores[...], axis=-1, keepdims=True), own_score)
    weights = jnp.exp(scores[...] - row_max).astype(jnp.bfloat16)
    own_weight = jnp.exp(own_score - row_max).astype(jnp.bfloat16).astype(jnp.float32)
    totals = jnp.sum(weights.astype(jnp.float32), axis=-1, keepdims=True) + own_weight
    near_peak = row_max[0] + jnp.log(totals[0])
    for r in range(blocks):
        segment = packed[pl.ds(first_slots[r], window), :, HEAD_SIZE:].reshape(2 * window, HEAD_SIZE)
        summed = jnp.dot(weights[r], segment, preferred_element_type=jnp.float32)
        summed = summed + own_weight[r] * values[r]
        merged_rows[r] = summed / totals[r]

    matching, slot = same_head(2 * FAR_SLOTS)
    log_totals = []
    for j in range(2):
        long_rows = far_queries[j]
        far_state[0] = jnp.full((pairs, LANES), LOWEST, jnp.float32)
        far_state[1] = jnp.zeros((pairs, LANES), jnp.float32)
        far_state[2] = jnp.zeros((pairs, HEAD_SIZE), jnp.float32)

        def rows_of(c, first):
            part = far[j, c * FAR_SLOTS : (c + 1) * FAR_SLOTS, :, first : first + HEAD_SIZE]
            return part.reshape(2 * FAR_SLOTS, HEAD_SIZE)

        for c in range(far_chunks):

            @pl.when(c * FAR_SLOTS < live[j])
            def _():
                far_copy(j, c).wait()
                found = contract(long_rows, rows_of(c, 0)) * scale
                found = jnp.where(matching & (slot < live[j] - c * FAR_SLOTS), found, LOWEST)
                far_scores[c] = found
                far_state[0] = jnp.maximum(far_state[0], fold_lanes(found, jnp.maximum))

        peak = jnp.max(far_state[0], axis=-1, keepdims=True)
        for c in range(far_chunks):

            @pl.when(c * FAR_SLOTS < live[j])
            def _():
                weight = jnp.exp(far_scores[c] - peak).astype(jnp.bfloat16)
                far_state[1] = far_state[1] + fold_lanes(weight.astype(jnp.float32), jnp.add)
                far_state[2] = far_state[2] + jnp.dot(
                    weight, rows_of(c, HEAD_SIZE), preferred_element_type=jnp.float32
                )

        total = jnp.sum(far_state[1], axis=-1, keepdims=True)
        summed = far_state[2]
        far_peak = peak + jnp.log(total)
        result = summed / total
        owner = group == j * (peers // 2)
        top = jnp.maximum(far_peak, near_peak)
        far_part = jnp.exp(far_peak - top)
        near_part = jnp.exp(near_peak - top)
        both = far_part + near_part
        result = jnp.where(owner, (result * far_part + merged_rows[0] * near_part) / both, result)
        log_total = jnp.where(owner, top + jnp.log(both), far_peak)
        out_ref[:, (pairs + j) * LANES : (pairs + j + 1) * LANES] = result.astype(jnp.bfloat16)
        log_totals.append(log_total)
    out_ref[:, (pairs + 2) * LANES :] = in_lanes(log_totals).astype(jnp.bfloat16)
    for b in range(pairs):
        out_ref[:, b * HEAD_SIZE : (b + 1) * HEAD_SIZE] = merged_rows[:, b, :].astype(jnp.bfloat16)


def attend(pieces, table, starts, lengths, split, packed_cache, long_cache):
    peers = len(pieces)
    blocks = pieces[0].shape[0]
    heads = QUERY_HEADS // KEY_VALUE_HEADS
    pairs = 2 * heads
    slots = packed_cache.shape[1]
    far_slots = long_cache.shape[2]
    return pl.pallas_call(
        functools.partial(attention_kernel, peers),
        out_shape=jax.ShapeDtypeStruct((blocks, (pairs + 3) * HEAD_SIZE), jnp.bfloat16),
        in_specs=in_vmem(peers + 1) + in_smem(3) + in_hbm(2),
        out_specs=pl.BlockSpec(memory_space=pltpu.VMEM),
        scratch_shapes=[
            pltpu.VMEM((slots, 2, 2 * HEAD_SIZE), jnp.bfloat16),
            pltpu.VMEM((2, far_slots, 2, 2 * HEAD_SIZE), jnp.bfloat16),
            pltpu.VMEM((blocks, pairs, HEAD_SIZE), jnp.float32),
            pltpu.VMEM((blocks, pairs, HEAD_SIZE), jnp.float32),
            pltpu.VMEM((blocks, pairs, HEAD_SIZE), jnp.float32),
            pltpu.VMEM((blocks, pairs, 2 * MOST_SLOTS), jnp.float32),
            pltpu.VMEM((far_slots // FAR_SLOTS, pairs, 2 * FAR_SLOTS), jnp.float32),
            pltpu.VMEM((3, pairs, LANES), jnp.float32),
            pltpu.VMEM((blocks, pairs, HEAD_SIZE), jnp.float32),
            pltpu.SemaphoreType.DMA,
            pltpu.SemaphoreType.DMA((2, far_slots // FAR_SLOTS)),
        ],
        compiler_params=params(),
        name="attend",
    )(*pieces, table, starts, lengths, split, packed_cache, long_cache)


def start_copies(pieces, weights, sems):
    copies = []
    for c, (start, width) in enumerate(column_chunks(weights.shape[1])):
        parts, row = [], 0
        for p, (weight_at, first_row, rows, first_column) in enumerate(pieces):
            parts.append(
                pltpu.make_async_copy(
                    weight_at.at[pl.ds(first_row, rows), pl.ds(first_column + start, width)],
                    weights.at[pl.ds(row, rows), pl.ds(start, width)],
                    sems.at[p, c],
                )
            )
            row += rows
        copies.append(parts)
    for parts in copies:
        for copy in parts:
            copy.start()
    return copies


def multiply_columns(rows_of, weights, copies, write):
    for parts, (start, width) in zip(copies, column_chunks(weights.shape[1])):
        for copy in parts:
            copy.wait()
        lanes = slice(start, start + width)
        write(lanes, jnp.dot(rows_of[...], weights[:, lanes], preferred_element_type=jnp.float32))


def output_early_kernel(peers, *refs):
    piece_refs, refs = refs[:peers], refs[peers:]
    weight_ref, out_ref, whole, weights, sems = refs
    group = lax.axis_index("req")
    blocks = piece_refs[0].shape[0]
    depth, half = weights.shape
    pairs = depth // LANES
    first = pl.multiple_of(half_start(True, half), half)
    copies = start_copies([(weight_ref, 0, depth, first)], weights, sems)
    for d, piece in enumerate(piece_refs):
        start = pl.multiple_of(lax.bitwise_xor(group, d) * blocks, blocks)
        whole[pl.ds(start, blocks)] = piece[:, 0:depth]
    ends = [piece[:, depth:].astype(jnp.float32) for piece in piece_refs]
    for j in range(2):
        peaks = [from_lanes(end[:, 2 * LANES :], j) for end in ends]
        top = functools.reduce(jnp.maximum, peaks)
        parts = [jnp.exp(peak - top) for peak in peaks]
        merged = sum(end[:, j * LANES : (j + 1) * LANES] * part for end, part in zip(ends, parts))
        merged = merged / sum(parts)
        merged_row = jnp.concatenate([merged[i : i + 1] for i in range(pairs)], 1)
        rows = slice(j * (peers // 2) * blocks, j * (peers // 2) * blocks + blocks)
        row = lax.broadcasted_iota(jnp.int32, (blocks, depth), 0)
        whole[rows] = jnp.where(
            row == 0, merged_row, whole[rows].astype(jnp.float32)
        ).astype(jnp.bfloat16)

    def write(lanes, result):
        out_ref[:, lanes] = result.astype(jnp.bfloat16)

    multiply_columns(whole, weights, copies, write)


def output_late_kernel(whole, weight_ref, out_ref, weights, sems):
    depth, half = weights.shape
    first = pl.multiple_of(half_start(False, half), half)
    copies = start_copies([(weight_ref, 0, depth, first)], weights, sems)

    def write(lanes, result):
        out_ref[:, lanes] = result.astype(jnp.bfloat16)

    multiply_columns(whole, weights, copies, write)


def project_output(pieces, weight):
    rows = len(pieces) * pieces[0].shape[0]
    depth, width = weight.shape
    half = width // 2
    shape = jax.ShapeDtypeStruct((rows, half), jnp.bfloat16)
    scratch = [
        pltpu.VMEM((depth, half), jnp.bfloat16),
        pltpu.SemaphoreType.DMA((1, len(column_chunks(half)))),
    ]
    sent, whole = pl.pallas_call(
        functools.partial(output_early_kernel, len(pieces)),
        out_shape=[shape, jax.ShapeDtypeStruct((rows, depth), jnp.bfloat16)],
        in_specs=in_vmem(len(pieces)) + in_hbm(1),
        out_specs=in_vmem(2),
        scratch_shapes=scratch,
        compiler_params=params(),
        name="project_output_sent",
    )(*pieces, weight)
    kept = pl.pallas_call(
        output_late_kernel,
        out_shape=shape,
        in_specs=in_vmem(1) + in_hbm(1),
        out_specs=pl.BlockSpec(memory_space=pltpu.VMEM),
        scratch_shapes=scratch,
        compiler_params=params(),
        name="project_output_kept",
    )(whole, weight)
    return sent, kept


def down_kernel(distances, other, *refs):
    count = len(distances)
    piece_refs, (weight_ref, *refs) = refs[:count], refs[count:]
    partial_ref = None if other is None else refs.pop(0)
    out_ref, whole, weights, sems = refs
    group = lax.axis_index("req")
    units = piece_refs[0].shape[1]
    width = weights.shape[1]
    first = 0 if other is None else pl.multiple_of(half_start(other, width), width)
    rows = [pl.multiple_of(lax.bitwise_xor(group, d) * units, LANES) for d in distances]
    copies = start_copies([(weight_ref.at[0], row, units, first) for row in rows], weights, sems)
    for p, piece in enumerate(piece_refs):
        whole[:, p * units : (p + 1) * units] = piece[...]

    def write(lanes, result):
        if other is not None:
            start = pl.multiple_of(first + lanes.start, LANES)
            result = result + partial_ref[:, pl.ds(start, lanes.stop - lanes.start)]
        out_ref[:, lanes] = result.astype(out_ref.dtype)

    multiply_columns(whole, weights, copies, write)


def call_down(distances, other, pieces, weight, partial, name):
    rows, units = pieces[0].shape
    depth, width = len(distances) * units, weight.shape[2]
    if other is not None:
        width = width // 2
    dtype = jnp.float32 if other is None else jnp.bfloat16
    return pl.pallas_call(
        functools.partial(down_kernel, distances, other),
        out_shape=jax.ShapeDtypeStruct((rows, width), dtype),
        in_specs=in_vmem(len(pieces)) + in_hbm(1) + in_vmem(len(partial)),
        out_specs=pl.BlockSpec(memory_space=pltpu.VMEM),
        scratch_shapes=[
            pltpu.VMEM((rows, depth), jnp.bfloat16),
            pltpu.VMEM((depth, width), jnp.bfloat16),
            pltpu.SemaphoreType.DMA((len(distances), len(column_chunks(width)))),
        ],
        compiler_params=params(),
        name=name,
    )(*pieces, weight, *partial)


def project_down(pieces, weight):
    early = (0, len(pieces) - 1)
    late = tuple(range(1, len(pieces) - 1))
    partial = call_down(early, None, [pieces[d] for d in early], weight, [], "project_down_early")
    rest = [pieces[d] for d in late]
    sent = call_down(late, True, rest, weight, [partial], "project_down_sent")
    kept = call_down(late, False, rest, weight, [partial], "project_down_kept")
    return sent, kept


def hidden_kernel(peers, *refs):
    piece_refs, out_ref = refs[:peers], refs[peers]
    rows, width = out_ref.shape
    sums = sum(piece[0:rows, width:].astype(jnp.float32) for piece in piece_refs)
    factor = row_scale(from_lanes(sums, 0))

    def summed(first):
        return sum(piece[first : first + rows, 0:width].astype(jnp.float32) for piece in piece_refs) * factor

    gate, up = summed(0), summed(rows)
    out_ref[...] = (gate / (1.0 + jnp.exp(-gate)) * up).astype(jnp.bfloat16)


def gated_units(pieces):
    rows, width = pieces[0].shape[0] // 2, pieces[0].shape[1] - LANES
    return pl.pallas_call(
        functools.partial(hidden_kernel, len(pieces)),
        out_shape=jax.ShapeDtypeStruct((rows, width), jnp.bfloat16),
        in_specs=in_vmem(len(pieces)),
        out_specs=pl.BlockSpec(memory_space=pltpu.VMEM),
        compiler_params=pltpu.CompilerParams(vmem_limit_bytes=16 * 2**20),
        name="gated_units",
    )(*pieces)


def fast_layer(section, own, other, attention_gain, query_key_value_weight, head_output_weight, feedforward_gain, gate_up, down_weight, packed_cache, long_cache, table, *segments):
    req_count = lax.axis_size("req")
    terms = project_qkv(own, other, attention_gain, query_key_value_weight, table, req_count, section > 0)
    attended = attend(swap_all(terms, "req", section), table, *segments, packed_cache, long_cache)
    out_weight = head_output_weight.reshape(-1, head_output_weight.shape[3])
    sent, kept = project_output(spread(attended, "req", section), out_weight)
    attended = finish_sum(sent, kept, "head", section)
    residual = (own.astype(jnp.float32) + attended).astype(jnp.bfloat16)
    other_residual = swap(residual, "head", 1, section)
    terms = project_gate_up(residual, other_residual, feedforward_gain, gate_up, req_count)
    hidden = gated_units(swap_all(terms, "req", section))
    sent, kept = project_down(spread(hidden, "req", section), down_weight)
    lowered = finish_sum(sent, kept, "head", section)
    return (residual.astype(jnp.float32) + lowered).astype(jnp.bfloat16)


def rope_table(lengths):
    req_count, group = lax.axis_size("req"), lax.axis_index("req")
    owner = (group == 0) | (group == req_count // 2)
    long_row = (jnp.arange(lengths.shape[1]) == 0) & owner
    position = lengths[0] + jnp.where(long_row, LONG, 0).astype(jnp.int32)
    half_dim = HEAD_SIZE // 2
    inverse = 1.0 / 10000.0 ** (jnp.arange(half_dim).astype(jnp.float32) * 2.0 / HEAD_SIZE)
    angles = position.astype(jnp.float32)[:, None] * inverse[None, :]
    return jnp.concatenate([jnp.cos(angles), jnp.sin(angles)], 1)


def fast_local(tokens, attention_gain, query_key_value_weight, head_output_weight, feedforward_gain, gate_up, down_weight, packed_cache, long_cache, lengths, long_split):
    layer_arrays = (
        attention_gain,
        query_key_value_weight,
        head_output_weight,
        feedforward_gain,
        gate_up,
        down_weight,
        packed_cache,
        long_cache,
        rope_table(lengths),
        jnp.cumsum(lengths[0]) - lengths[0],
        lengths[0],
        long_split,
    )
    half = tokens.shape[1] // 2
    own, other = [lax.dynamic_slice_in_dim(tokens, half_start(o, half), half, 1) for o in (False, True)]
    first = fast_layer(0, own, other, *layer_arrays)
    own, other = [swap(first, "head", d, 0, 1) for d in range(2)]
    first_other = swap(first, "head", 1, 0)
    second = fast_layer(1, own, other, *layer_arrays)
    second_other = swap(second, "head", 1, 1)
    is_first = lax.axis_index("section") == 0
    own, other = jnp.where(is_first, first, second), jnp.where(is_first, first_other, second_other)
    own_first = half_start(False, half) == 0
    return jnp.where(
        own_first, jnp.concatenate([own, other], 1), jnp.concatenate([other, own], 1)
    )[None]


def is_power_of_two(value):
    return value & (value - 1) == 0


def fits_fast(mesh):
    req_count, head_count = mesh.shape["req"], mesh.shape["head"]
    columns = MODEL_WIDTH // req_count // 2
    return (
        mesh.shape["section"] == 2
        and is_power_of_two(req_count)
        and is_power_of_two(head_count)
        and req_count >= 4
        and head_count >= 2
        and KEY_VALUE_HEADS == 2 * head_count
        and columns % COLUMNS == 0
        and FF % (head_count * COLUMNS) == 0
        and FF % (head_count * req_count * LANES) == 0
    )


def solution(mesh):
    placed = (
        P(None, "req"),
        P("section", "req"),
        P("section", "req", "head", None),
        P("section", "head", None, "req"),
        P("section", "req"),
        P("section", "req", None, "head"),
        P("section", "head", "req"),
        P("section", "req", "head", None),
        P("section", None, "req", "head", None),
        P("req", None),
        P(None, "req"),
    )
    return jax.shard_map(
        fast_local if fits_fast(mesh) else local,
        mesh=mesh,
        in_specs=placed, out_specs=P("section", None, "req"), check_vma=False
    )
```

```python
import functools
import math

import jax
import jax.numpy as jnp
from jax import lax
from jax.experimental import pallas as pl
from jax.experimental.pallas import tpu as pltpu
from jax.sharding import PartitionSpec as P

MODEL_WIDTH = 8192
QUERY_HEADS = 64
KEY_VALUE_HEADS = 8
HEAD_SIZE = 128
LONG = 16384
FF = 14336
MOST_SLOTS = 256
LANES = 128
COLUMNS = 512
FAR_SLOTS = 2048
LOWEST = -1e30
PARTS = 4


EPSILON = 1e-05


def merged(part, axis, combine):
    gathered = jax.tree.map(lambda a: lax.all_gather(a, axis), part)

    def take(source):
        return jax.tree.map(lambda a: lax.dynamic_index_in_dim(a, source, 0, False), gathered)

    return lax.fori_loop(
        1, lax.axis_size(axis), lambda source, state: combine(state, take(source)), take(0)
    )


def shifted(value, axis, by):
    peers = lax.axis_size(axis)
    pairs = [(i, i + by) for i in range(peers) if 0 <= i + by < peers]
    return lax.ppermute(value, axis, pairs)


def rotate(values, position):
    half_dim = values.shape[-1] // 2
    freq_ids = jnp.arange(half_dim).astype(jnp.float32)
    inverse = 1.0 / 10000.0 ** (freq_ids * 2.0 / values.shape[-1])
    angles = position.astype(jnp.float32)[:, None] * inverse[None, :]
    cosine = jnp.cos(angles)[:, None, None, :]
    sine_part = jnp.sin(angles)[:, None, None, :]
    lower_half = values[..., :half_dim]
    upper_half = values[..., half_dim:]
    return jnp.concatenate(
        [
            lower_half * cosine - upper_half * sine_part,
            upper_half * cosine + lower_half * sine_part,
        ],
        -1,
    )


def add_pair(earlier, second_part):
    return earlier + second_part


def combine_partial(earlier, second_part):
    peak = jnp.maximum(earlier[0], second_part[0])
    left_factor = jnp.exp(earlier[0] - peak)
    right_factor = jnp.exp(second_part[0] - peak)
    softmax_total = earlier[1] * left_factor + second_part[1] * right_factor
    weighted_sum = earlier[2] * left_factor[..., None] + second_part[2] * right_factor[..., None]
    return (peak, softmax_total, weighted_sum)


def over_requests(values, combiner):
    return merged(values, "req", combiner)


def rows_apply(values, row_fn):
    return row_fn(lax.all_gather(values, "req", axis=0, tiled=True), jnp.int32(0))


def rows_project(term_fn, row_count):
    return lax.psum_scatter(
        term_fn(jnp.int32(0), row_count * lax.axis_size("req")),
        "req",
        scatter_dimension=0,
        tiled=True,
    )


def head_total(values):
    return lax.psum(values, "head")


def keep_rows(piece_rows, start_row):
    return piece_rows


def norm_rows(values, gain_row):
    floats = values.astype(jnp.float32)
    squares = over_requests(jnp.sum(floats * floats, axis=-1), add_pair)
    return (
        floats * lax.rsqrt(squares / MODEL_WIDTH + EPSILON)[:, None] * gain_row.astype(jnp.float32)
    ).astype(jnp.bfloat16)


def decoder_layer(
    inputs,
    micro_batch,
    attention_gain,
    query_key_value_weight,
    head_output_weight,
    feedforward_gain,
    gate_up,
    down_weight,
    packed_cache,
    long_cache,
    lengths,
    long_split,
):
    req_count = lax.axis_size("req")
    group_index = lax.axis_index("req")
    blocks = inputs.shape[0] // req_count
    columns = query_key_value_weight.shape[1]
    kv_local = query_key_value_weight.shape[2]
    requests_per_group = QUERY_HEADS // KEY_VALUE_HEADS
    score_scale = 1.0 / math.sqrt(HEAD_SIZE)
    normalized_input = norm_rows(inputs, attention_gain[0])
    in_weights = query_key_value_weight[0].reshape(
        columns, kv_local * (requests_per_group + 2) * HEAD_SIZE
    )

    def qkv_term(start_row, row_count):
        return jnp.dot(normalized_input, in_weights, preferred_element_type=jnp.float32)

    projected_rows = rows_project(qkv_term, blocks).reshape(
        blocks, kv_local, requests_per_group + 2, HEAD_SIZE
    )
    local_rows = jnp.arange(blocks)
    row_lengths = lengths[0]
    owner_long = (group_index == 0) | (group_index == req_count // 2)
    long_row = (local_rows == 0) & (micro_batch == 0) & owner_long
    position = row_lengths + jnp.where(long_row, LONG, 0).astype(jnp.int32)
    queries = rotate(projected_rows[:, :, :requests_per_group], position).astype(jnp.bfloat16)
    new_key = rotate(projected_rows[:, :, requests_per_group : requests_per_group + 1], position)[
        :, :, 0
    ].astype(jnp.bfloat16)
    new_value = projected_rows[:, :, requests_per_group + 1].astype(jnp.bfloat16)
    gathered = rows_apply(
        queries[0:1].reshape(1, kv_local * requests_per_group * HEAD_SIZE), keep_rows
    )
    long_queries = jnp.stack([gathered[0], gathered[req_count // 2]]).reshape(
        2, kv_local, requests_per_group, HEAD_SIZE
    )
    far_cache = long_cache[0]
    far_live = (jnp.arange(far_cache.shape[1])[None, :] < long_split[:, 0][:, None])[
        :, None, None, :
    ]
    far_scores = (
        jnp.einsum(
            "jkhd,jpkd->jkhp",
            long_queries,
            far_cache[..., :HEAD_SIZE],
            preferred_element_type=jnp.float32,
        )
        * score_scale
    )
    far_max = jnp.max(jnp.where(far_live, far_scores, -jnp.inf), axis=-1)
    far_weights = jnp.where(
        far_live, jnp.exp(jnp.where(far_live, far_scores - far_max[..., None], 0.0)), 0.0
    ).astype(jnp.bfloat16)
    far_totals = jnp.sum(far_weights.astype(jnp.float32), axis=-1)
    far_summed = jnp.einsum(
        "jkhp,jpkd->jkhd",
        far_weights,
        far_cache[..., HEAD_SIZE:],
        preferred_element_type=jnp.float32,
    )
    far_max, far_totals, far_summed = over_requests(
        (far_max, far_totals, far_summed), combine_partial
    )
    far_index = jnp.where(group_index == 0, 0, 1)
    chosen_max = lax.dynamic_index_in_dim(far_max, far_index, 0, keepdims=False)
    chosen_totals = lax.dynamic_index_in_dim(far_totals, far_index, 0, keepdims=False)
    chosen_summed = lax.dynamic_index_in_dim(far_summed, far_index, 0, keepdims=False)
    pack_part = packed_cache[0]
    seg_ends = jnp.cumsum(lengths[0])
    slot_ids = jnp.arange(pack_part.shape[0])
    slot_owner = jnp.sum((slot_ids[:, None] >= seg_ends[None, :]).astype(jnp.int32), axis=1)
    request_ids = micro_batch * blocks + local_rows
    in_segment = (slot_owner[None, :] == request_ids[:, None])[:, None, None, :]
    scores = (
        jnp.einsum(
            "rkhd,pkd->rkhp",
            queries,
            pack_part[..., :HEAD_SIZE],
            preferred_element_type=jnp.float32,
        )
        * score_scale
    )
    own_score = (
        jnp.einsum("rkhd,rkd->rkh", queries, new_key, preferred_element_type=jnp.float32)
        * score_scale
    )
    row_max = jnp.maximum(jnp.max(jnp.where(in_segment, scores, -jnp.inf), axis=-1), own_score)
    long_mask = long_row[:, None, None]
    row_max = jnp.where(long_mask, jnp.maximum(row_max, chosen_max[None]), row_max)
    weights = jnp.where(
        in_segment, jnp.exp(jnp.where(in_segment, scores - row_max[..., None], 0.0)), 0.0
    ).astype(jnp.bfloat16)
    own_weights = jnp.exp(own_score - row_max).astype(jnp.bfloat16)
    far_factor = jnp.where(
        long_mask, jnp.exp(jnp.where(long_mask, chosen_max[None] - row_max, 0.0)), 0.0
    )
    softmax_total = (
        jnp.sum(weights.astype(jnp.float32), axis=-1)
        + own_weights.astype(jnp.float32)
        + far_factor * chosen_totals[None]
    )
    weighted_sum = jnp.einsum(
        "rkhp,pkd->rkhd", weights, pack_part[..., HEAD_SIZE:], preferred_element_type=jnp.float32
    )
    weighted_sum = (
        weighted_sum
        + own_weights.astype(jnp.float32)[..., None] * new_value.astype(jnp.float32)[:, :, None, :]
    )
    weighted_sum = weighted_sum + far_factor[..., None] * chosen_summed[None]
    attended_heads = (
        (weighted_sum / softmax_total[..., None])
        .astype(jnp.bfloat16)
        .reshape(blocks, kv_local * requests_per_group * HEAD_SIZE)
    )
    out_weights = head_output_weight[0].reshape(kv_local * requests_per_group * HEAD_SIZE, columns)

    def project_heads(piece_rows, start_row):
        return jnp.dot(piece_rows, out_weights, preferred_element_type=jnp.float32)

    attended = head_total(rows_apply(attended_heads, project_heads))
    residual = (inputs.astype(jnp.float32) + attended).astype(jnp.bfloat16)
    normed_two = norm_rows(residual, feedforward_gain[0])
    ff_weights = gate_up[0].reshape(columns, -1)

    def ff_term(start_row, row_count):
        return jnp.dot(normed_two, ff_weights, preferred_element_type=jnp.float32)

    gate_and_up = rows_project(ff_term, blocks)
    hidden_width = gate_and_up.shape[1] // 2
    hidden = (jax.nn.silu(gate_and_up[:, :hidden_width]) * gate_and_up[:, hidden_width:]).astype(
        jnp.bfloat16
    )
    lower_weights = down_weight[0]

    def project_hidden(piece_rows, start_row):
        return jnp.dot(piece_rows, lower_weights, preferred_element_type=jnp.float32)

    lowered = head_total(rows_apply(hidden, project_hidden))
    return (residual.astype(jnp.float32) + lowered).astype(jnp.bfloat16)


def local(
    tokens,
    attention_gain,
    query_key_value_weight,
    head_output_weight,
    feedforward_gain,
    gate_up,
    down_weight,
    packed_cache,
    long_cache,
    lengths,
    long_split,
):
    req_count = lax.axis_size("req")
    section_index = lax.axis_index("section")
    batch_count = 1
    per_group = tokens.shape[0] // req_count
    blocks = per_group // batch_count
    columns = tokens.shape[1]
    token_grid = tokens.reshape(req_count, per_group, columns)
    result = jnp.zeros_like(token_grid)
    incoming = jnp.zeros((req_count * blocks, columns), jnp.bfloat16)
    for phase_step in range(batch_count + 1):
        micro_batch = phase_step - section_index
        is_active = (micro_batch >= 0) & (micro_batch < batch_count)
        micro_batch = jnp.clip(micro_batch, 0, batch_count - 1)
        new_batch = token_grid.reshape(req_count * blocks, columns)
        inputs = jnp.where(section_index == 0, new_batch, incoming)
        output = decoder_layer(
            inputs,
            micro_batch,
            attention_gain,
            query_key_value_weight,
            head_output_weight,
            feedforward_gain,
            gate_up,
            down_weight,
            packed_cache,
            long_cache,
            lengths,
            long_split,
        )
        placed = output.reshape(req_count, blocks, columns)
        result = jnp.where(is_active, placed, result)
        if phase_step < batch_count:
            incoming = shifted(output, "section", 1)
    return result.reshape(1, req_count * per_group, columns)

def swap(value, axis, distance, section, target_section=None):
    size = lax.axis_size(axis)
    target_section = section if target_section is None else target_section
    pairs = [(section * size + i, target_section * size + (i ^ distance)) for i in range(size)]
    return lax.ppermute(value, ("section", axis), pairs)


def swap_all(values, axis, section):
    received = {d: swap(values[d], axis, d, section) for d in reversed(range(1, len(values)))}
    return [values[0]] + [received[d] for d in range(1, len(values))]


def spread(value, axis, section):
    return swap_all([value] * lax.axis_size(axis), axis, section)


def sum_doubling(value, axis, section):
    distance = 2
    total = value.astype(jnp.float32)
    while distance < lax.axis_size(axis):
        other = swap(value, axis, distance, section)
        total = value.astype(jnp.float32) + other.astype(jnp.float32)
        value = total.astype(jnp.bfloat16)
        distance *= 2
    return total


def sum_pair(sent, kept, axis, section):
    pair = kept.astype(jnp.float32) + swap(sent, axis, 1, section).astype(jnp.float32)
    return pair.astype(jnp.bfloat16)


def half_start(other, half):
    index = lax.bitwise_and(lax.axis_index("head"), 1)
    return (1 - index if other else index) * half


def in_vmem(count):
    return [pl.BlockSpec(memory_space=pltpu.VMEM)] * count


def in_hbm(count):
    return [pl.BlockSpec(memory_space=pltpu.HBM)] * count


def in_smem(count):
    return [pl.BlockSpec(memory_space=pltpu.SMEM)] * count


def params(mebibytes):
    return pltpu.CompilerParams(vmem_limit_bytes=mebibytes * 2**20)


def in_any(count):
    return [pl.BlockSpec(memory_space=pl.ANY)] * count


def ordered(tokens, kernel):
    def run(*refs):
        kernel(*refs[len(tokens) :])

    return run


def fetch_kernel(count, plan, *refs):
    sources, refs = refs[:count], refs[count + 1 :]
    *targets, token, sems = refs
    token[...] = jnp.zeros_like(token)
    copies = [
        pltpu.make_async_copy(source, target, sems.at[i])
        for i, (source, target) in enumerate(plan(sources, targets))
    ]
    for copy in copies:
        copy.start()
    for copy in copies:
        copy.wait()


def fetch(plan, copies, arrays, shapes, after, name):
    return pl.pallas_call(
        functools.partial(fetch_kernel, len(arrays), plan),
        out_shape=[pltpu.VMEM(shape, jnp.bfloat16) for shape in shapes]
        + [jax.ShapeDtypeStruct((8, LANES), jnp.float32)],
        in_specs=in_hbm(len(arrays)) + in_any(1),
        out_specs=in_vmem(len(shapes) + 1),
        scratch_shapes=[pltpu.SemaphoreType.DMA((copies,))],
        compiler_params=params(2),
        name=name,
    )(*arrays, after)


def row_parts(source, first, target, rows, parts):
    size = rows // parts
    return [
        (source.at[pl.ds(first + i * size, size)], target.at[pl.ds(i * size, size)])
        for i in range(parts)
    ]


def fetch_halves(weight, others, after, name):
    half, shape = weight.shape[1] // 2, weight.shape[2:]

    def plan(sources, targets):
        parts = []
        for other, target in zip(others, targets):
            first = pl.multiple_of(half_start(other, half), half)
            parts += row_parts(sources[0].at[0], first, target, half, PARTS)
        return parts

    shapes = [(half, *shape)] * len(others)
    return fetch(plan, PARTS * len(others), [weight], shapes, after, name)


def fetch_output(weight, after):
    depth, half = weight.shape[0], weight.shape[1] // 2

    def plan(sources, targets):
        parts = []
        for other, target in zip((True, False), targets):
            first = pl.multiple_of(half_start(other, half), half)
            parts += row_parts(sources[0].at[:, pl.ds(first, half)], 0, target, depth, PARTS)
        return parts

    return fetch(plan, 2 * PARTS, [weight], [(depth, half)] * 2, after, "fetch_output")


def fetch_down(weight, peers, after):
    depth, width = weight.shape[1:]
    units, half = depth // peers, width // 2
    early, late = down_order(peers)

    def plan(sources, targets):
        group = lax.axis_index("req")
        parts = []
        for target, distances, other in zip(targets, (early, late, late), (None, True, False)):
            columns = target.shape[1]
            first = 0 if other is None else pl.multiple_of(half_start(other, half), half)
            for p, d in enumerate(distances):
                row = pl.multiple_of(lax.bitwise_xor(group, d) * units, LANES)
                parts.append(
                    (
                        sources[0].at[0, pl.ds(row, units), pl.ds(first, columns)],
                        target.at[pl.ds(p * units, units)],
                    )
                )
        return parts

    shapes = [(len(early) * units, width)] + [(len(late) * units, half)] * 2
    copies = len(early) + 2 * len(late)
    return fetch(plan, copies, [weight], shapes, after, "fetch_down")


def fetch_caches(packed_cache, long_cache, after):
    far_slots = long_cache.shape[2]

    def plan(sources, targets):
        parts = [(sources[0].at[0], targets[0])]
        for j in range(2):
            parts += row_parts(sources[1].at[0, j], 0, targets[1].at[j], far_slots, PARTS)
        return parts

    shapes = [packed_cache.shape[1:], long_cache.shape[1:]]
    return fetch(plan, 2 * PARTS + 1, [packed_cache, long_cache], shapes, after, "fetch_caches")


def down_order(peers):
    return (0, 1), tuple(range(2, peers))


def column_chunks(width):
    edge = COLUMNS // 2
    starts = [0] + list(range(edge, width - edge, COLUMNS)) + [width - edge]
    return [(a, b - a) for a, b in zip(starts, starts[1:] + [width]) if b > a]


def split_parts(value):
    high = value.astype(jnp.bfloat16)
    low = (value - high.astype(jnp.float32)).astype(jnp.bfloat16)
    return high, low


def sum_squares(values):
    floats = values.astype(jnp.float32)
    return jnp.sum(floats * floats, axis=-1, keepdims=True)


def in_lanes(columns):
    rows = columns[0].shape[0]
    lane = lax.broadcasted_iota(jnp.int32, (rows, LANES), 1)
    block = jnp.zeros((rows, LANES), jnp.float32)
    for i, column in enumerate(columns):
        high, low = split_parts(column)
        block = jnp.where(lane == 2 * i, high.astype(jnp.float32), block)
        block = jnp.where(lane == 2 * i + 1, low.astype(jnp.float32), block)
    return block


def from_lanes(block, i):
    return block[:, 2 * i : 2 * i + 1] + block[:, 2 * i + 1 : 2 * i + 2]


def row_scale(squares):
    return lax.rsqrt(squares / MODEL_WIDTH + EPSILON)


def expand_rows(scaled, wide_ref):
    rows, columns = scaled.shape
    chunk = 2 * LANES
    source = lax.broadcasted_iota(jnp.int32, (chunk, 2 * chunk), 0)
    target = lax.broadcasted_iota(jnp.int32, (chunk, 2 * chunk), 1)
    count = columns // chunk
    stacked = jnp.concatenate([scaled[:, c * chunk : (c + 1) * chunk] for c in range(count)], 0)
    for half in range(2):
        select = jnp.where(target == 2 * source + half, 1.0, 0.0).astype(jnp.bfloat16)
        spread = jnp.dot(stacked, select, preferred_element_type=jnp.float32).astype(jnp.bfloat16)
        for c in range(count):
            wide_ref[half * rows : (half + 1) * rows, 2 * c * chunk : 2 * (c + 1) * chunk] = spread[
                c * rows : (c + 1) * rows
            ]


def scale_columns(values, gain):
    return (values.astype(jnp.float32) * gain.astype(jnp.float32)).astype(jnp.bfloat16)


def multiply_halves(others, add, resident, refs):
    count = len(others)
    input_refs, refs = refs[:count], refs[count:]
    (gain_ref, weight_ref), refs = refs[:2], refs[2:]
    if add:
        (partial_ref, squares_ref), refs = refs[:2], refs[2:]
    if resident:
        rest, (wide, total) = refs[:-2], refs[-2:]
        weights = weight_ref
    else:
        rest, (wide, total, weights, sems) = refs[:-4], refs[-4:]
    half = input_refs[0].shape[1]
    starts = [pl.multiple_of(half_start(other, half), half) for other in others]
    chunks = column_chunks(total.shape[1])
    copies = [[] for _ in chunks]
    if not resident:
        for c, (start, width) in enumerate(chunks):
            for p, first in enumerate(starts):
                copy = pltpu.make_async_copy(
                    weight_ref.at[0, pl.ds(first, half), :, pl.ds(start, width)],
                    weights.at[pl.ds(p * half, half), :, pl.ds(start, width)],
                    sems.at[p, c],
                )
                copy.start()
                copies[c].append(copy)
    scaled = [
        scale_columns(ref[...], gain_ref[:, pl.ds(first, half)])
        for ref, first in zip(input_refs, starts)
    ]
    expand_rows(jnp.concatenate(scaled, 1), wide)
    squares = sum(sum_squares(ref[...]) for ref in input_refs)
    if add:
        squares = squares + squares_ref[:, 0:1]

    def fill():
        for parts, (start, width) in zip(copies, chunks):
            for copy in parts:
                copy.wait()
            lanes = slice(start, start + width)
            result = jnp.dot(
                wide[...],
                weights[:, :, lanes].reshape(wide.shape[1], width),
                preferred_element_type=jnp.float32,
            )
            total[:, lanes] = result + partial_ref[:, lanes] if add else result

    return rest, squares, total, fill


def partial_kernel(*refs):
    (partial_out, squares_out), squares, total, fill = multiply_halves((False,), False, True, refs)
    squares_out[...] = jnp.broadcast_to(squares, squares_out.shape)
    fill()
    partial_out[...] = total[...]


def qkv_kernel(peers, others, add, resident, *refs):
    (table_ref, *outs), squares, total, fill = multiply_halves(others, add, resident, refs)
    group = lax.axis_index("req")
    rows = squares.shape[0]
    blocks = rows // peers
    far = peers // 2 * blocks
    width = total.shape[1]
    long_squares = [jnp.broadcast_to(squares[r : r + 1], squares.shape) for r in (0, far)]
    sums = in_lanes([squares] + long_squares)
    high, low = split_parts(table_ref[0:1])
    table = jnp.concatenate(
        [high.astype(jnp.float32), low.astype(jnp.float32), jnp.zeros((blocks - 2, LANES), jnp.float32)], 0
    ).astype(jnp.bfloat16)
    fill()
    heads = QUERY_HEADS // KEY_VALUE_HEADS
    long_queries = [
        jnp.concatenate(
            [
                total[k * rows + r : k * rows + r + 1, h * HEAD_SIZE : (h + 1) * HEAD_SIZE]
                for k in range(2)
                for h in range(heads)
            ],
            0,
        ).astype(jnp.bfloat16)
        for r in (0, far)
    ]
    for d, out in enumerate(outs):
        peer = pl.multiple_of(lax.bitwise_xor(group, d) * blocks, blocks)
        for k in range(2):
            out[:, k * width : (k + 1) * width] = total[pl.ds(k * rows + peer, blocks)].astype(
                jnp.bfloat16
            )
        out[:, 2 * width + LANES : 2 * width + 2 * LANES] = table
        for j in range(2):
            first = 2 * width + (2 + j) * LANES
            out[:, first : first + LANES] = long_queries[j]
    total[0:rows, 0:LANES] = sums
    for d, out in enumerate(outs):
        peer = pl.multiple_of(lax.bitwise_xor(group, d) * blocks, blocks)
        out[:, 2 * width : 2 * width + LANES] = total[pl.ds(peer, blocks), 0:LANES].astype(jnp.bfloat16)


def gate_up_kernel(peers, *refs):
    outs, squares, total, fill = multiply_halves((True,), True, False, refs)
    group = lax.axis_index("req")
    rows = squares.shape[0]
    width = total.shape[1] // peers
    sums = in_lanes([squares]).astype(jnp.bfloat16)
    fill()
    for d, out in enumerate(outs):
        start = pl.multiple_of(lax.bitwise_xor(group, d) * width, LANES)
        out[:, 0:width] = total[:, pl.ds(start, width)].astype(jnp.bfloat16)
        out[0:rows, width:] = sums
        out[rows:, width:] = sums


def project_pairs(kernel, resident, inputs, gain, weight, partial, extra, out_shapes, name):
    rows, half = inputs[0].shape
    pair, width = weight.shape[-2:]
    depth = len(inputs) * half
    operands = [*inputs, gain, weight, *partial, *extra]
    weight_spec = in_vmem(1) if resident else in_hbm(1)
    specs = in_vmem(len(inputs) + 1) + weight_spec + in_vmem(len(partial) + len(extra))
    scratch = [
        pltpu.VMEM((pair * rows, pair * depth), jnp.bfloat16),
        pltpu.VMEM((pair * rows, width), jnp.float32),
    ]
    if not resident:
        scratch += [
            pltpu.VMEM((depth, pair, width), jnp.bfloat16),
            pltpu.SemaphoreType.DMA((len(inputs), len(column_chunks(width)))),
        ]
    return pl.pallas_call(
        kernel,
        out_shape=out_shapes,
        in_specs=specs,
        out_specs=in_vmem(len(out_shapes)),
        scratch_shapes=scratch,
        compiler_params=params(14 if resident else 24),
        name=name,
    )(*operands)


def project_early(own, gain, weights, tokens, name):
    rows, half = own.shape
    pair, width = weights.shape[-2:]
    shapes = [
        jax.ShapeDtypeStruct((pair * rows, width), jnp.float32),
        jax.ShapeDtypeStruct((rows, LANES), jnp.float32),
    ]
    return pl.pallas_call(
        ordered(tokens, partial_kernel),
        out_shape=shapes,
        in_specs=in_any(len(tokens)) + in_vmem(3),
        out_specs=in_vmem(2),
        scratch_shapes=[
            pltpu.VMEM((pair * rows, pair * half), jnp.bfloat16),
            pltpu.VMEM((pair * rows, width), jnp.float32),
        ],
        compiler_params=params(14),
        name=name,
    )(*tokens, own, gain, weights)


def project_qkv(own, other, gain, weight, fetched, tokens, table, peers):
    blocks = own.shape[0] // peers
    shapes = [jax.ShapeDtypeStruct((blocks, 2 * weight.shape[3] + 4 * LANES), jnp.bfloat16)] * peers
    if fetched is None:
        kernel = functools.partial(qkv_kernel, peers, (False, True), False, False)
        return project_pairs(kernel, False, [own, other], gain, weight, [], [table], shapes, "project_qkv")
    partial = project_early(own, gain, fetched[0], tokens, "project_qkv_early")
    kernel = functools.partial(qkv_kernel, peers, (True,), True, True)
    return project_pairs(kernel, True, [other], gain, fetched[1], partial, [table], shapes, "project_qkv")


def project_gate_up(own, other, gain, weight, fetched, peers):
    rows, width = own.shape[0], weight.shape[3] // peers + LANES
    shapes = [jax.ShapeDtypeStruct((2 * rows, width), jnp.bfloat16)] * peers
    partial = project_early(own, gain, fetched, [], "project_gate_up_early")
    kernel = functools.partial(gate_up_kernel, peers)
    return project_pairs(kernel, False, [other], gain, weight, partial, [], shapes, "project_gate_up")


def fold_lanes(values, combine):
    blocks = [values[:, i : i + LANES] for i in range(0, values.shape[1], LANES)]
    while len(blocks) > 1:
        pairs = [combine(a, b) for a, b in zip(blocks[::2], blocks[1::2])]
        blocks = pairs + blocks[2 * len(pairs) :]
    return blocks[0]


def attention_kernel(peers, resident, *refs):
    piece_refs, refs = refs[:peers], refs[peers:]
    table_ref, starts, lengths, split, packed_ref, long_ref, out_ref = refs[:7]
    (queries, keys, values, scores, far_scores, far_state, merged_rows) = refs[7:14]
    packed, far, packed_sem, far_sems = (packed_ref, long_ref, None, None) if resident else refs[14:]
    group = lax.axis_index("req")
    blocks = out_ref.shape[0]
    heads = QUERY_HEADS // KEY_VALUE_HEADS
    pairs = 2 * heads
    window = scores.shape[2] // 2
    slots = packed.shape[0]
    far_chunks = far.shape[1] // FAR_SLOTS
    scale = 1.0 / math.sqrt(HEAD_SIZE)
    live = [split[0, 0], split[1, 0]]

    def far_copy(j, c):
        return pltpu.make_async_copy(
            long_ref.at[0, j, pl.ds(c * FAR_SLOTS, FAR_SLOTS)],
            far.at[j, pl.ds(c * FAR_SLOTS, FAR_SLOTS)],
            far_sems.at[j, c],
        )

    if not resident:
        packed_copy = pltpu.make_async_copy(packed_ref.at[0], packed, packed_sem)
        packed_copy.start()
    for j in range(0 if resident else 2):
        for c in range(far_chunks):

            @pl.when(c * FAR_SLOTS < live[j])
            def _():
                far_copy(j, c).start()

    width = HEAD_SIZE * (heads + 2)

    def summed_block(start):
        return sum(piece[:, start : start + LANES].astype(jnp.float32) for piece in piece_refs)

    sums = summed_block(2 * width)
    scale_rows = row_scale(from_lanes(sums, 0))
    tables = [
        piece[:, 2 * width + LANES : 2 * width + 2 * LANES].astype(jnp.float32) for piece in piece_refs
    ]
    tables = [t[0:1] + t[1:2] for t in tables]
    far_tables = [
        sum(
            jnp.where(lax.bitwise_xor(group, d) == j * (peers // 2), t, 0.0)
            for d, t in enumerate(tables)
        )
        for j in range(2)
    ]
    def cosine_sine(table):
        turned = pltpu.roll(table, HEAD_SIZE // 2, 1)
        lower = lax.broadcasted_iota(jnp.int32, table.shape, 1) < HEAD_SIZE // 2
        return jnp.where(lower, table, turned), jnp.where(lower, -turned, table)

    def rotated(block, angles):
        cosine, sine = angles
        return block * cosine + pltpu.roll(block, HEAD_SIZE // 2, 1) * sine

    own_angles = cosine_sine(table_ref[...])
    far_queries = [
        rotated(
            summed_block(2 * width + (2 + j) * LANES) * row_scale(from_lanes(sums, 1 + j)),
            cosine_sine(jnp.broadcast_to(far_tables[j], table_ref.shape)),
        ).astype(jnp.bfloat16)
        for j in range(2)
    ]
    for k in range(2):
        for b in range(heads + 2):
            block = summed_block(k * width + b * HEAD_SIZE) * scale_rows
            if b <= heads:
                block = rotated(block, own_angles)
            block = block.astype(jnp.bfloat16).astype(jnp.float32)
            if b < heads:
                queries[:, k * heads + b, :] = block
            else:
                for h in range(heads):
                    (keys if b == heads else values)[:, k * heads + h, :] = block

    def same_head(columns):
        row = lax.broadcasted_iota(jnp.int32, (pairs, columns), 0)
        column = lax.broadcasted_iota(jnp.int32, (pairs, columns), 1)
        return (row // heads) == (column % 2), column // 2

    def contract(a, b):
        return lax.dot_general(a, b, (((1,), (1,)), ((), ())), preferred_element_type=jnp.float32)

    if not resident:
        packed_copy.wait()
    matching, slot = same_head(2 * window)
    first_slots = []
    for r in range(blocks):
        first = jnp.minimum(starts[r], slots - window)
        first_slots.append(first)
        low = starts[r] - first
        segment = packed[pl.ds(first, window), :, 0:HEAD_SIZE].reshape(2 * window, HEAD_SIZE)
        own = contract(queries[r].astype(jnp.bfloat16), segment) * scale
        inside = matching & (slot >= low) & (slot < low + lengths[r])
        scores[r] = jnp.where(inside, own, LOWEST)
    own_score = jnp.sum(queries[...] * keys[...], axis=-1, keepdims=True) * scale
    row_max = jnp.maximum(jnp.max(scores[...], axis=-1, keepdims=True), own_score)
    weights = jnp.exp(scores[...] - row_max).astype(jnp.bfloat16)
    own_weight = jnp.exp(own_score - row_max).astype(jnp.bfloat16).astype(jnp.float32)
    totals = jnp.sum(weights.astype(jnp.float32), axis=-1, keepdims=True) + own_weight
    near_peak = row_max[0] + jnp.log(totals[0])
    for r in range(blocks):
        segment = packed[pl.ds(first_slots[r], window), :, HEAD_SIZE:].reshape(2 * window, HEAD_SIZE)
        summed = jnp.dot(weights[r], segment, preferred_element_type=jnp.float32)
        summed = summed + own_weight[r] * values[r]
        merged_rows[r] = summed / totals[r]

    matching, slot = same_head(2 * FAR_SLOTS)
    log_totals = []
    for j in range(2):
        long_rows = far_queries[j]
        far_state[0] = jnp.full((pairs, LANES), LOWEST, jnp.float32)
        far_state[1] = jnp.zeros((pairs, LANES), jnp.float32)
        far_state[2] = jnp.zeros((pairs, HEAD_SIZE), jnp.float32)

        def rows_of(c, first):
            part = far[j, c * FAR_SLOTS : (c + 1) * FAR_SLOTS, :, first : first + HEAD_SIZE]
            return part.reshape(2 * FAR_SLOTS, HEAD_SIZE)

        for c in range(far_chunks):

            @pl.when(c * FAR_SLOTS < live[j])
            def _():
                if not resident:
                    far_copy(j, c).wait()
                found = contract(long_rows, rows_of(c, 0)) * scale
                found = jnp.where(matching & (slot < live[j] - c * FAR_SLOTS), found, LOWEST)
                far_scores[c] = found
                far_state[0] = jnp.maximum(far_state[0], fold_lanes(found, jnp.maximum))

        peak = jnp.max(far_state[0], axis=-1, keepdims=True)
        for c in range(far_chunks):

            @pl.when(c * FAR_SLOTS < live[j])
            def _():
                weight = jnp.exp(far_scores[c] - peak).astype(jnp.bfloat16)
                far_state[1] = far_state[1] + fold_lanes(weight.astype(jnp.float32), jnp.add)
                far_state[2] = far_state[2] + jnp.dot(
                    weight, rows_of(c, HEAD_SIZE), preferred_element_type=jnp.float32
                )

        total = jnp.sum(far_state[1], axis=-1, keepdims=True)
        summed = far_state[2]
        far_peak = peak + jnp.log(total)
        result = summed / total
        owner = group == j * (peers // 2)
        top = jnp.maximum(far_peak, near_peak)
        far_part = jnp.exp(far_peak - top)
        near_part = jnp.exp(near_peak - top)
        both = far_part + near_part
        result = jnp.where(owner, (result * far_part + merged_rows[0] * near_part) / both, result)
        log_total = jnp.where(owner, top + jnp.log(both), far_peak)
        out_ref[:, (pairs + j) * LANES : (pairs + j + 1) * LANES] = result.astype(jnp.bfloat16)
        log_totals.append(log_total)
    out_ref[:, (pairs + 2) * LANES :] = in_lanes(log_totals).astype(jnp.bfloat16)
    for b in range(pairs):
        out_ref[:, b * HEAD_SIZE : (b + 1) * HEAD_SIZE] = merged_rows[:, b, :].astype(jnp.bfloat16)


def attend(pieces, table, starts, lengths, split, packed_cache, long_cache, resident, tokens):
    peers = len(pieces)
    blocks = pieces[0].shape[0]
    heads = QUERY_HEADS // KEY_VALUE_HEADS
    pairs = 2 * heads
    slots = packed_cache.shape[-3]
    far_slots = long_cache.shape[-3]
    scratch = [
        pltpu.VMEM((blocks, pairs, HEAD_SIZE), jnp.float32),
        pltpu.VMEM((blocks, pairs, HEAD_SIZE), jnp.float32),
        pltpu.VMEM((blocks, pairs, HEAD_SIZE), jnp.float32),
        pltpu.VMEM((blocks, pairs, 2 * MOST_SLOTS), jnp.float32),
        pltpu.VMEM((far_slots // FAR_SLOTS, pairs, 2 * FAR_SLOTS), jnp.float32),
        pltpu.VMEM((3, pairs, LANES), jnp.float32),
        pltpu.VMEM((blocks, pairs, HEAD_SIZE), jnp.float32),
    ]
    if not resident:
        scratch += [
            pltpu.VMEM((slots, 2, 2 * HEAD_SIZE), jnp.bfloat16),
            pltpu.VMEM((2, far_slots, 2, 2 * HEAD_SIZE), jnp.bfloat16),
            pltpu.SemaphoreType.DMA,
            pltpu.SemaphoreType.DMA((2, far_slots // FAR_SLOTS)),
        ]
    return pl.pallas_call(
        ordered(tokens, functools.partial(attention_kernel, peers, resident)),
        out_shape=jax.ShapeDtypeStruct((blocks, (pairs + 3) * HEAD_SIZE), jnp.bfloat16),
        in_specs=in_any(len(tokens))
        + in_vmem(peers + 1)
        + in_smem(3)
        + (in_vmem(2) if resident else in_hbm(2)),
        out_specs=pl.BlockSpec(memory_space=pltpu.VMEM),
        scratch_shapes=scratch,
        compiler_params=params(14 if resident else 34),
        name="attend",
    )(*tokens, *pieces, table, starts, lengths, split, packed_cache, long_cache)


def multiply_columns(rows_of, weights, write):
    for start, width in column_chunks(weights.shape[1]):
        lanes = slice(start, start + width)
        write(lanes, jnp.dot(rows_of[...], weights[:, lanes], preferred_element_type=jnp.float32))


def output_early_kernel(peers, *refs):
    piece_refs, refs = refs[:peers], refs[peers:]
    weights, out_ref, whole = refs
    group = lax.axis_index("req")
    blocks = piece_refs[0].shape[0]
    depth = weights.shape[0]
    pairs = depth // LANES
    for d, piece in enumerate(piece_refs):
        start = pl.multiple_of(lax.bitwise_xor(group, d) * blocks, blocks)
        whole[pl.ds(start, blocks)] = piece[:, 0:depth]
    ends = [piece[:, depth:].astype(jnp.float32) for piece in piece_refs]
    for j in range(2):
        peaks = [from_lanes(end[:, 2 * LANES :], j) for end in ends]
        top = functools.reduce(jnp.maximum, peaks)
        parts = [jnp.exp(peak - top) for peak in peaks]
        merged = sum(end[:, j * LANES : (j + 1) * LANES] * part for end, part in zip(ends, parts))
        merged = merged / sum(parts)
        merged_row = jnp.concatenate([merged[i : i + 1] for i in range(pairs)], 1)
        rows = slice(j * (peers // 2) * blocks, j * (peers // 2) * blocks + blocks)
        row = lax.broadcasted_iota(jnp.int32, (blocks, depth), 0)
        whole[rows] = jnp.where(
            row == 0, merged_row, whole[rows].astype(jnp.float32)
        ).astype(jnp.bfloat16)

    def write(lanes, result):
        out_ref[:, lanes] = result.astype(jnp.bfloat16)

    multiply_columns(whole, weights, write)


def output_late_kernel(whole, weights, out_ref):
    def write(lanes, result):
        out_ref[:, lanes] = result.astype(jnp.bfloat16)

    multiply_columns(whole, weights, write)


def project_output(pieces, weights):
    rows = len(pieces) * pieces[0].shape[0]
    depth, half = weights[0].shape
    shape = jax.ShapeDtypeStruct((rows, half), jnp.bfloat16)
    sent, whole = pl.pallas_call(
        functools.partial(output_early_kernel, len(pieces)),
        out_shape=[shape, jax.ShapeDtypeStruct((rows, depth), jnp.bfloat16)],
        in_specs=in_vmem(len(pieces) + 1),
        out_specs=in_vmem(2),
        compiler_params=params(12),
        name="project_output_sent",
    )(*pieces, weights[0])
    kept = pl.pallas_call(
        output_late_kernel,
        out_shape=shape,
        in_specs=in_vmem(2),
        out_specs=pl.BlockSpec(memory_space=pltpu.VMEM),
        compiler_params=params(12),
        name="project_output_kept",
    )(whole, weights[1])
    return sent, kept


def down_kernel(count, other, *refs):
    piece_refs, (weights, *refs) = refs[:count], refs[count:]
    partial_ref = None if other is None else refs.pop(0)
    out_ref, whole = refs
    units = piece_refs[0].shape[1]
    width = weights.shape[1]
    first = 0 if other is None else pl.multiple_of(half_start(other, width), width)
    for p, piece in enumerate(piece_refs):
        whole[:, p * units : (p + 1) * units] = piece[...]

    def write(lanes, result):
        if other is not None:
            start = pl.multiple_of(first + lanes.start, LANES)
            result = result + partial_ref[:, pl.ds(start, lanes.stop - lanes.start)]
        out_ref[:, lanes] = result.astype(out_ref.dtype)

    multiply_columns(whole, weights, write)


def call_down(other, pieces, weights, partial, name):
    rows = pieces[0].shape[0]
    depth, width = weights.shape
    dtype = jnp.float32 if other is None else jnp.bfloat16
    return pl.pallas_call(
        functools.partial(down_kernel, len(pieces), other),
        out_shape=jax.ShapeDtypeStruct((rows, width), dtype),
        in_specs=in_vmem(len(pieces) + 1 + len(partial)),
        out_specs=pl.BlockSpec(memory_space=pltpu.VMEM),
        scratch_shapes=[pltpu.VMEM((rows, depth), jnp.bfloat16)],
        compiler_params=params(12),
        name=name,
    )(*pieces, weights, *partial)


def project_down(pieces, weights):
    early, late = down_order(len(pieces))
    partial = call_down(None, [pieces[d] for d in early], weights[0], [], "project_down_early")
    rest = [pieces[d] for d in late]
    sent = call_down(True, rest, weights[1], [partial], "project_down_sent")
    kept = call_down(False, rest, weights[2], [partial], "project_down_kept")
    return sent, kept


def hidden_kernel(peers, *refs):
    piece_refs, out_ref = refs[:peers], refs[peers]
    rows, width = out_ref.shape
    sums = sum(piece[0:rows, width:].astype(jnp.float32) for piece in piece_refs)
    factor = row_scale(from_lanes(sums, 0))

    def summed(first):
        return sum(piece[first : first + rows, 0:width].astype(jnp.float32) for piece in piece_refs) * factor

    gate, up = summed(0), summed(rows)
    out_ref[...] = (gate / (1.0 + jnp.exp(-gate)) * up).astype(jnp.bfloat16)


def gated_units(pieces, token):
    rows, width = pieces[0].shape[0] // 2, pieces[0].shape[1] - LANES
    return pl.pallas_call(
        ordered([token], functools.partial(hidden_kernel, len(pieces))),
        out_shape=jax.ShapeDtypeStruct((rows, width), jnp.bfloat16),
        in_specs=in_any(1) + in_vmem(len(pieces)),
        out_specs=pl.BlockSpec(memory_space=pltpu.VMEM),
        compiler_params=params(8),
        name="gated_units",
    )(token, *pieces)


def residual_kernel(base, terms, out):
    out[...] = (base[...].astype(jnp.float32) + terms[...]).astype(jnp.bfloat16)


def add_residual(base, terms, token):
    return pl.pallas_call(
        ordered([token], residual_kernel),
        out_shape=jax.ShapeDtypeStruct(base.shape, jnp.bfloat16),
        in_specs=in_any(1) + in_vmem(2),
        out_specs=pl.BlockSpec(memory_space=pltpu.VMEM),
        compiler_params=params(4),
        name="add_residual",
    )(token, base, terms)


def fast_layer(section, own, other, fetched, attention_gain, query_key_value_weight, out_weight, feedforward_gain, gate_up, down_weight, packed_cache, long_cache, table, *segments):
    req_count = lax.axis_size("req")
    qkv_fetched, out_fetched, caches, tokens = fetched or (None, None, None, [])
    terms = project_qkv(
        own, other, attention_gain, query_key_value_weight, qkv_fetched, tokens, table, req_count
    )
    terms = swap_all(terms, "req", section)
    if fetched is None:
        *out_fetched, token = fetch_output(out_weight, terms[1])
        attended = attend(terms, table, *segments, packed_cache, long_cache, False, [token])
    else:
        attended = attend(terms, table, *segments, *caches, True, [])
    sent, kept = project_output(spread(attended, "req", section), out_fetched)
    pair = sum_pair(sent, kept, "head", section)
    gate_fetched, token = fetch_halves(gate_up, (False,), pair, "fetch_gate_up")
    residual = add_residual(own, sum_doubling(pair, "head", section), token)
    other_residual = swap(residual, "head", 1, section)
    terms = project_gate_up(residual, other_residual, feedforward_gain, gate_up, gate_fetched, req_count)
    terms = swap_all(terms, "req", section)
    *down_fetched, token = fetch_down(down_weight, req_count, terms[1])
    hidden = spread(gated_units(terms, token), "req", section)
    sent, kept = project_down(hidden, down_fetched)
    lowered = sum_doubling(sum_pair(sent, kept, "head", section), "head", section)
    return (residual.astype(jnp.float32) + lowered).astype(jnp.bfloat16)


def rope_table(lengths):
    req_count, group = lax.axis_size("req"), lax.axis_index("req")
    owner = (group == 0) | (group == req_count // 2)
    long_row = (jnp.arange(lengths.shape[1]) == 0) & owner
    position = lengths[0] + jnp.where(long_row, LONG, 0).astype(jnp.int32)
    half_dim = HEAD_SIZE // 2
    inverse = 1.0 / 10000.0 ** (jnp.arange(half_dim).astype(jnp.float32) * 2.0 / HEAD_SIZE)
    angles = position.astype(jnp.float32)[:, None] * inverse[None, :]
    return jnp.concatenate([jnp.cos(angles), jnp.sin(angles)], 1)


def fast_local(tokens, attention_gain, query_key_value_weight, head_output_weight, feedforward_gain, gate_up, down_weight, packed_cache, long_cache, lengths, long_split):
    out_weight = head_output_weight.reshape(-1, head_output_weight.shape[3])
    query_key_value_weight, out_weight, gate_up, down_weight, packed_cache, long_cache = [
        pltpu.with_memory_space_constraint(array, pltpu.HBM)
        for array in (query_key_value_weight, out_weight, gate_up, down_weight, packed_cache, long_cache)
    ]
    layer_arrays = (
        attention_gain,
        query_key_value_weight,
        out_weight,
        feedforward_gain,
        gate_up,
        down_weight,
        packed_cache,
        long_cache,
        rope_table(lengths),
        jnp.cumsum(lengths[0]) - lengths[0],
        lengths[0],
        long_split,
    )
    half = tokens.shape[1] // 2
    own, other = [lax.dynamic_slice_in_dim(tokens, half_start(o, half), half, 1) for o in (False, True)]
    first = fast_layer(0, own, other, None, *layer_arrays)
    own, other = [swap(first, "head", d, 0, 1) for d in range(2)]
    *qkv_fetched, qkv_token = fetch_halves(query_key_value_weight, (False, True), first, "fetch_qkv")
    *out_fetched, out_token = fetch_output(out_weight, first)
    *caches, caches_token = fetch_caches(packed_cache, long_cache, first)
    fetched = (qkv_fetched, out_fetched, caches, [qkv_token, out_token, caches_token])
    first_other = swap(first, "head", 1, 0)
    second = fast_layer(1, own, other, fetched, *layer_arrays)
    second_other = swap(second, "head", 1, 1)
    is_first = lax.axis_index("section") == 0
    own, other = jnp.where(is_first, first, second), jnp.where(is_first, first_other, second_other)
    own_first = half_start(False, half) == 0
    return jnp.where(
        own_first, jnp.concatenate([own, other], 1), jnp.concatenate([other, own], 1)
    )[None]


def is_power_of_two(value):
    return value & (value - 1) == 0


def fits_fast(mesh):
    req_count, head_count = mesh.shape["req"], mesh.shape["head"]
    columns = MODEL_WIDTH // req_count // 2
    return (
        mesh.shape["section"] == 2
        and is_power_of_two(req_count)
        and is_power_of_two(head_count)
        and req_count >= 4
        and head_count >= 2
        and KEY_VALUE_HEADS == 2 * head_count
        and columns % COLUMNS == 0
        and FF % (head_count * COLUMNS) == 0
        and FF % (head_count * req_count * LANES) == 0
    )


def solution(mesh):
    placed = (
        P(None, "req"),
        P("section", "req"),
        P("section", "req", "head", None),
        P("section", "head", None, "req"),
        P("section", "req"),
        P("section", "req", None, "head"),
        P("section", "head", "req"),
        P("section", "req", "head", None),
        P("section", None, "req", "head", None),
        P("req", None),
        P(None, "req"),
    )
    return jax.shard_map(
        fast_local if fits_fast(mesh) else local,
        mesh=mesh,
        in_specs=placed, out_specs=P("section", None, "req"), check_vma=False
    )
```

```python
import functools
import math

import jax
import jax.numpy as jnp
from jax import lax
from jax.experimental import pallas as pl
from jax.experimental.pallas import tpu as pltpu
from jax.sharding import PartitionSpec as P

MODEL_WIDTH = 8192
QUERY_HEADS = 64
KEY_VALUE_HEADS = 8
HEAD_SIZE = 128
LONG = 16384
FF = 14336
MOST_SLOTS = 256
LANES = 128
COLUMNS = 512
FAR_SLOTS = 2048
LOWEST = -1e30
PARTS = 4


EPSILON = 1e-05


def merged(part, axis, combine):
    gathered = jax.tree.map(lambda a: lax.all_gather(a, axis), part)

    def take(source):
        return jax.tree.map(lambda a: lax.dynamic_index_in_dim(a, source, 0, False), gathered)

    return lax.fori_loop(
        1, lax.axis_size(axis), lambda source, state: combine(state, take(source)), take(0)
    )


def shifted(value, axis, by):
    peers = lax.axis_size(axis)
    pairs = [(i, i + by) for i in range(peers) if 0 <= i + by < peers]
    return lax.ppermute(value, axis, pairs)


def rotate(values, position):
    half_dim = values.shape[-1] // 2
    freq_ids = jnp.arange(half_dim).astype(jnp.float32)
    inverse = 1.0 / 10000.0 ** (freq_ids * 2.0 / values.shape[-1])
    angles = position.astype(jnp.float32)[:, None] * inverse[None, :]
    cosine = jnp.cos(angles)[:, None, None, :]
    sine_part = jnp.sin(angles)[:, None, None, :]
    lower_half = values[..., :half_dim]
    upper_half = values[..., half_dim:]
    return jnp.concatenate(
        [
            lower_half * cosine - upper_half * sine_part,
            upper_half * cosine + lower_half * sine_part,
        ],
        -1,
    )


def add_pair(earlier, second_part):
    return earlier + second_part


def combine_partial(earlier, second_part):
    peak = jnp.maximum(earlier[0], second_part[0])
    left_factor = jnp.exp(earlier[0] - peak)
    right_factor = jnp.exp(second_part[0] - peak)
    softmax_total = earlier[1] * left_factor + second_part[1] * right_factor
    weighted_sum = earlier[2] * left_factor[..., None] + second_part[2] * right_factor[..., None]
    return (peak, softmax_total, weighted_sum)


def over_requests(values, combiner):
    return merged(values, "req", combiner)


def rows_apply(values, row_fn):
    return row_fn(lax.all_gather(values, "req", axis=0, tiled=True), jnp.int32(0))


def rows_project(term_fn, row_count):
    return lax.psum_scatter(
        term_fn(jnp.int32(0), row_count * lax.axis_size("req")),
        "req",
        scatter_dimension=0,
        tiled=True,
    )


def head_total(values):
    return lax.psum(values, "head")


def keep_rows(piece_rows, start_row):
    return piece_rows


def norm_rows(values, gain_row):
    floats = values.astype(jnp.float32)
    squares = over_requests(jnp.sum(floats * floats, axis=-1), add_pair)
    return (
        floats * lax.rsqrt(squares / MODEL_WIDTH + EPSILON)[:, None] * gain_row.astype(jnp.float32)
    ).astype(jnp.bfloat16)


def decoder_layer(
    inputs,
    micro_batch,
    attention_gain,
    query_key_value_weight,
    head_output_weight,
    feedforward_gain,
    gate_up,
    down_weight,
    packed_cache,
    long_cache,
    lengths,
    long_split,
):
    req_count = lax.axis_size("req")
    group_index = lax.axis_index("req")
    blocks = inputs.shape[0] // req_count
    columns = query_key_value_weight.shape[1]
    kv_local = query_key_value_weight.shape[2]
    requests_per_group = QUERY_HEADS // KEY_VALUE_HEADS
    score_scale = 1.0 / math.sqrt(HEAD_SIZE)
    normalized_input = norm_rows(inputs, attention_gain[0])
    in_weights = query_key_value_weight[0].reshape(
        columns, kv_local * (requests_per_group + 2) * HEAD_SIZE
    )

    def qkv_term(start_row, row_count):
        return jnp.dot(normalized_input, in_weights, preferred_element_type=jnp.float32)

    projected_rows = rows_project(qkv_term, blocks).reshape(
        blocks, kv_local, requests_per_group + 2, HEAD_SIZE
    )
    local_rows = jnp.arange(blocks)
    row_lengths = lengths[0]
    owner_long = (group_index == 0) | (group_index == req_count // 2)
    long_row = (local_rows == 0) & (micro_batch == 0) & owner_long
    position = row_lengths + jnp.where(long_row, LONG, 0).astype(jnp.int32)
    queries = rotate(projected_rows[:, :, :requests_per_group], position).astype(jnp.bfloat16)
    new_key = rotate(projected_rows[:, :, requests_per_group : requests_per_group + 1], position)[
        :, :, 0
    ].astype(jnp.bfloat16)
    new_value = projected_rows[:, :, requests_per_group + 1].astype(jnp.bfloat16)
    gathered = rows_apply(
        queries[0:1].reshape(1, kv_local * requests_per_group * HEAD_SIZE), keep_rows
    )
    long_queries = jnp.stack([gathered[0], gathered[req_count // 2]]).reshape(
        2, kv_local, requests_per_group, HEAD_SIZE
    )
    far_cache = long_cache[0]
    far_live = (jnp.arange(far_cache.shape[1])[None, :] < long_split[:, 0][:, None])[
        :, None, None, :
    ]
    far_scores = (
        jnp.einsum(
            "jkhd,jpkd->jkhp",
            long_queries,
            far_cache[..., :HEAD_SIZE],
            preferred_element_type=jnp.float32,
        )
        * score_scale
    )
    far_max = jnp.max(jnp.where(far_live, far_scores, -jnp.inf), axis=-1)
    far_weights = jnp.where(
        far_live, jnp.exp(jnp.where(far_live, far_scores - far_max[..., None], 0.0)), 0.0
    ).astype(jnp.bfloat16)
    far_totals = jnp.sum(far_weights.astype(jnp.float32), axis=-1)
    far_summed = jnp.einsum(
        "jkhp,jpkd->jkhd",
        far_weights,
        far_cache[..., HEAD_SIZE:],
        preferred_element_type=jnp.float32,
    )
    far_max, far_totals, far_summed = over_requests(
        (far_max, far_totals, far_summed), combine_partial
    )
    far_index = jnp.where(group_index == 0, 0, 1)
    chosen_max = lax.dynamic_index_in_dim(far_max, far_index, 0, keepdims=False)
    chosen_totals = lax.dynamic_index_in_dim(far_totals, far_index, 0, keepdims=False)
    chosen_summed = lax.dynamic_index_in_dim(far_summed, far_index, 0, keepdims=False)
    pack_part = packed_cache[0]
    seg_ends = jnp.cumsum(lengths[0])
    slot_ids = jnp.arange(pack_part.shape[0])
    slot_owner = jnp.sum((slot_ids[:, None] >= seg_ends[None, :]).astype(jnp.int32), axis=1)
    request_ids = micro_batch * blocks + local_rows
    in_segment = (slot_owner[None, :] == request_ids[:, None])[:, None, None, :]
    scores = (
        jnp.einsum(
            "rkhd,pkd->rkhp",
            queries,
            pack_part[..., :HEAD_SIZE],
            preferred_element_type=jnp.float32,
        )
        * score_scale
    )
    own_score = (
        jnp.einsum("rkhd,rkd->rkh", queries, new_key, preferred_element_type=jnp.float32)
        * score_scale
    )
    row_max = jnp.maximum(jnp.max(jnp.where(in_segment, scores, -jnp.inf), axis=-1), own_score)
    long_mask = long_row[:, None, None]
    row_max = jnp.where(long_mask, jnp.maximum(row_max, chosen_max[None]), row_max)
    weights = jnp.where(
        in_segment, jnp.exp(jnp.where(in_segment, scores - row_max[..., None], 0.0)), 0.0
    ).astype(jnp.bfloat16)
    own_weights = jnp.exp(own_score - row_max).astype(jnp.bfloat16)
    far_factor = jnp.where(
        long_mask, jnp.exp(jnp.where(long_mask, chosen_max[None] - row_max, 0.0)), 0.0
    )
    softmax_total = (
        jnp.sum(weights.astype(jnp.float32), axis=-1)
        + own_weights.astype(jnp.float32)
        + far_factor * chosen_totals[None]
    )
    weighted_sum = jnp.einsum(
        "rkhp,pkd->rkhd", weights, pack_part[..., HEAD_SIZE:], preferred_element_type=jnp.float32
    )
    weighted_sum = (
        weighted_sum
        + own_weights.astype(jnp.float32)[..., None] * new_value.astype(jnp.float32)[:, :, None, :]
    )
    weighted_sum = weighted_sum + far_factor[..., None] * chosen_summed[None]
    attended_heads = (
        (weighted_sum / softmax_total[..., None])
        .astype(jnp.bfloat16)
        .reshape(blocks, kv_local * requests_per_group * HEAD_SIZE)
    )
    out_weights = head_output_weight[0].reshape(kv_local * requests_per_group * HEAD_SIZE, columns)

    def project_heads(piece_rows, start_row):
        return jnp.dot(piece_rows, out_weights, preferred_element_type=jnp.float32)

    attended = head_total(rows_apply(attended_heads, project_heads))
    residual = (inputs.astype(jnp.float32) + attended).astype(jnp.bfloat16)
    normed_two = norm_rows(residual, feedforward_gain[0])
    ff_weights = gate_up[0].reshape(columns, -1)

    def ff_term(start_row, row_count):
        return jnp.dot(normed_two, ff_weights, preferred_element_type=jnp.float32)

    gate_and_up = rows_project(ff_term, blocks)
    hidden_width = gate_and_up.shape[1] // 2
    hidden = (jax.nn.silu(gate_and_up[:, :hidden_width]) * gate_and_up[:, hidden_width:]).astype(
        jnp.bfloat16
    )
    lower_weights = down_weight[0]

    def project_hidden(piece_rows, start_row):
        return jnp.dot(piece_rows, lower_weights, preferred_element_type=jnp.float32)

    lowered = head_total(rows_apply(hidden, project_hidden))
    return (residual.astype(jnp.float32) + lowered).astype(jnp.bfloat16)


def local(
    tokens,
    attention_gain,
    query_key_value_weight,
    head_output_weight,
    feedforward_gain,
    gate_up,
    down_weight,
    packed_cache,
    long_cache,
    lengths,
    long_split,
):
    req_count = lax.axis_size("req")
    section_index = lax.axis_index("section")
    batch_count = 1
    per_group = tokens.shape[0] // req_count
    blocks = per_group // batch_count
    columns = tokens.shape[1]
    token_grid = tokens.reshape(req_count, per_group, columns)
    result = jnp.zeros_like(token_grid)
    incoming = jnp.zeros((req_count * blocks, columns), jnp.bfloat16)
    for phase_step in range(batch_count + 1):
        micro_batch = phase_step - section_index
        is_active = (micro_batch >= 0) & (micro_batch < batch_count)
        micro_batch = jnp.clip(micro_batch, 0, batch_count - 1)
        new_batch = token_grid.reshape(req_count * blocks, columns)
        inputs = jnp.where(section_index == 0, new_batch, incoming)
        output = decoder_layer(
            inputs,
            micro_batch,
            attention_gain,
            query_key_value_weight,
            head_output_weight,
            feedforward_gain,
            gate_up,
            down_weight,
            packed_cache,
            long_cache,
            lengths,
            long_split,
        )
        placed = output.reshape(req_count, blocks, columns)
        result = jnp.where(is_active, placed, result)
        if phase_step < batch_count:
            incoming = shifted(output, "section", 1)
    return result.reshape(1, req_count * per_group, columns)

def swap(value, axis, distance, section, target_section=None):
    size = lax.axis_size(axis)
    target_section = section if target_section is None else target_section
    pairs = [(section * size + i, target_section * size + (i ^ distance)) for i in range(size)]
    return lax.ppermute(value, ("section", axis), pairs)


def swap_all(values, axis, section):
    received = {d: swap(values[d], axis, d, section) for d in reversed(range(1, len(values)))}
    return [values[0]] + [received[d] for d in range(1, len(values))]


def spread(value, axis, section):
    return swap_all([value] * lax.axis_size(axis), axis, section)


def sum_doubling(value, axis, section):
    distance = 2
    total = value.astype(jnp.float32)
    while distance < lax.axis_size(axis):
        other = swap(value, axis, distance, section)
        total = value.astype(jnp.float32) + other.astype(jnp.float32)
        value = total.astype(jnp.bfloat16)
        distance *= 2
    return total


def sum_pair(sent, kept, axis, section):
    pair = kept.astype(jnp.float32) + swap(sent, axis, 1, section).astype(jnp.float32)
    return pair.astype(jnp.bfloat16)


def half_start(other, half):
    index = lax.bitwise_and(lax.axis_index("head"), 1)
    return (1 - index if other else index) * half


def in_vmem(count):
    return [pl.BlockSpec(memory_space=pltpu.VMEM)] * count


def in_hbm(count):
    return [pl.BlockSpec(memory_space=pltpu.HBM)] * count


def in_smem(count):
    return [pl.BlockSpec(memory_space=pltpu.SMEM)] * count


def params(mebibytes):
    return pltpu.CompilerParams(vmem_limit_bytes=mebibytes * 2**20)


def in_any(count):
    return [pl.BlockSpec(memory_space=pl.ANY)] * count


def ordered(tokens, kernel):
    def run(*refs):
        kernel(*refs[len(tokens) :])

    return run


def fetch_kernel(count, plan, *refs):
    sources, refs = refs[:count], refs[count + 1 :]
    *targets, token, sems = refs
    token[...] = jnp.zeros_like(token)
    copies = [
        pltpu.make_async_copy(source, target, sems.at[i])
        for i, (source, target) in enumerate(plan(sources, targets))
    ]
    for copy in copies:
        copy.start()
    for copy in copies:
        copy.wait()


def fetch(plan, copies, arrays, shapes, after, name):
    return pl.pallas_call(
        functools.partial(fetch_kernel, len(arrays), plan),
        out_shape=[pltpu.VMEM(shape, jnp.bfloat16) for shape in shapes]
        + [jax.ShapeDtypeStruct((8, LANES), jnp.float32)],
        in_specs=in_hbm(len(arrays)) + in_any(1),
        out_specs=in_vmem(len(shapes) + 1),
        scratch_shapes=[pltpu.SemaphoreType.DMA((copies,))],
        compiler_params=params(2),
        name=name,
    )(*arrays, after)


def row_parts(source, first, target, rows, parts):
    size = rows // parts
    return [
        (source.at[pl.ds(first + i * size, size)], target.at[pl.ds(i * size, size)])
        for i in range(parts)
    ]


def fetch_halves(weight, others, after, name):
    half, shape = weight.shape[1] // 2, weight.shape[2:]

    def plan(sources, targets):
        parts = []
        for other, target in zip(others, targets):
            first = pl.multiple_of(half_start(other, half), half)
            parts += row_parts(sources[0].at[0], first, target, half, PARTS)
        return parts

    shapes = [(half, *shape)] * len(others)
    return fetch(plan, PARTS * len(others), [weight], shapes, after, name)


def fetch_quarter(weight, part, after, name):
    half, shape = weight.shape[1] // 2, weight.shape[2:]
    quarter = half // 2

    def plan(sources, targets):
        first = pl.multiple_of(half_start(True, half) + part * quarter, quarter)
        return row_parts(sources[0].at[0], first, targets[0], quarter, PARTS)

    return fetch(plan, PARTS, [weight], [(quarter, *shape)], after, name)


def fetch_output(weight, after):
    depth, half = weight.shape[0], weight.shape[1] // 2

    def plan(sources, targets):
        parts = []
        for other, target in zip((True, False), targets):
            first = pl.multiple_of(half_start(other, half), half)
            parts += row_parts(sources[0].at[:, pl.ds(first, half)], 0, target, depth, PARTS)
        return parts

    return fetch(plan, 2 * PARTS, [weight], [(depth, half)] * 2, after, "fetch_output")


def fetch_down(weight, peers, after):
    depth, width = weight.shape[1:]
    units, half = depth // peers, width // 2
    early, late = down_order(peers)

    def plan(sources, targets):
        group = lax.axis_index("req")
        parts = []
        for target, distances, other in zip(targets, (early, late, late), (None, True, False)):
            columns = target.shape[1]
            first = 0 if other is None else pl.multiple_of(half_start(other, half), half)
            for p, d in enumerate(distances):
                row = pl.multiple_of(lax.bitwise_xor(group, d) * units, LANES)
                parts.append(
                    (
                        sources[0].at[0, pl.ds(row, units), pl.ds(first, columns)],
                        target.at[pl.ds(p * units, units)],
                    )
                )
        return parts

    shapes = [(len(early) * units, width)] + [(len(late) * units, half)] * 2
    copies = len(early) + 2 * len(late)
    return fetch(plan, copies, [weight], shapes, after, "fetch_down")


def fetch_caches(packed_cache, long_cache, after):
    far_slots = long_cache.shape[2]

    def plan(sources, targets):
        parts = [(sources[0].at[0], targets[0])]
        for j in range(2):
            parts += row_parts(sources[1].at[0, j], 0, targets[1].at[j], far_slots, PARTS)
        return parts

    shapes = [packed_cache.shape[1:], long_cache.shape[1:]]
    return fetch(plan, 2 * PARTS + 1, [packed_cache, long_cache], shapes, after, "fetch_caches")


def down_order(peers):
    return (0, 1), tuple(range(2, peers))


def column_chunks(width):
    edge = COLUMNS // 2
    starts = [0] + list(range(edge, width - edge, COLUMNS)) + [width - edge]
    return [(a, b - a) for a, b in zip(starts, starts[1:] + [width]) if b > a]


def split_parts(value):
    high = value.astype(jnp.bfloat16)
    low = (value - high.astype(jnp.float32)).astype(jnp.bfloat16)
    return high, low


def sum_squares(values):
    floats = values.astype(jnp.float32)
    return jnp.sum(floats * floats, axis=-1, keepdims=True)


def in_lanes(columns):
    rows = columns[0].shape[0]
    lane = lax.broadcasted_iota(jnp.int32, (rows, LANES), 1)
    block = jnp.zeros((rows, LANES), jnp.float32)
    for i, column in enumerate(columns):
        high, low = split_parts(column)
        block = jnp.where(lane == 2 * i, high.astype(jnp.float32), block)
        block = jnp.where(lane == 2 * i + 1, low.astype(jnp.float32), block)
    return block


def from_lanes(block, i):
    return block[:, 2 * i : 2 * i + 1] + block[:, 2 * i + 1 : 2 * i + 2]


def row_scale(squares):
    return lax.rsqrt(squares / MODEL_WIDTH + EPSILON)


def expand_rows(scaled, wide_ref):
    rows, columns = scaled.shape
    chunk = 2 * LANES
    source = lax.broadcasted_iota(jnp.int32, (chunk, 2 * chunk), 0)
    target = lax.broadcasted_iota(jnp.int32, (chunk, 2 * chunk), 1)
    count = columns // chunk
    stacked = jnp.concatenate([scaled[:, c * chunk : (c + 1) * chunk] for c in range(count)], 0)
    for half in range(2):
        select = jnp.where(target == 2 * source + half, 1.0, 0.0).astype(jnp.bfloat16)
        spread = jnp.dot(stacked, select, preferred_element_type=jnp.float32).astype(jnp.bfloat16)
        for c in range(count):
            wide_ref[half * rows : (half + 1) * rows, 2 * c * chunk : 2 * (c + 1) * chunk] = spread[
                c * rows : (c + 1) * rows
            ]


def scale_columns(values, gain):
    return (values.astype(jnp.float32) * gain.astype(jnp.float32)).astype(jnp.bfloat16)


def multiply_halves(others, add, resident, refs):
    count = len(others)
    input_refs, refs = refs[:count], refs[count:]
    (gain_ref, weight_ref), refs = refs[:2], refs[2:]
    if add:
        (partial_ref, squares_ref), refs = refs[:2], refs[2:]
    if resident:
        rest, (wide, total) = refs[:-2], refs[-2:]
        weights = weight_ref
    else:
        rest, (wide, total, weights, sems) = refs[:-4], refs[-4:]
    half = input_refs[0].shape[1]
    starts = [pl.multiple_of(half_start(other, half), half) for other in others]
    chunks = column_chunks(total.shape[1])
    copies = [[] for _ in chunks]
    if not resident:
        for c, (start, width) in enumerate(chunks):
            for p, first in enumerate(starts):
                copy = pltpu.make_async_copy(
                    weight_ref.at[0, pl.ds(first, half), :, pl.ds(start, width)],
                    weights.at[pl.ds(p * half, half), :, pl.ds(start, width)],
                    sems.at[p, c],
                )
                copy.start()
                copies[c].append(copy)
    scaled = [
        scale_columns(ref[...], gain_ref[:, pl.ds(first, half)])
        for ref, first in zip(input_refs, starts)
    ]
    expand_rows(jnp.concatenate(scaled, 1), wide)
    squares = sum(sum_squares(ref[...]) for ref in input_refs)
    if add:
        squares = squares + squares_ref[:, 0:1]

    def fill():
        for parts, (start, width) in zip(copies, chunks):
            for copy in parts:
                copy.wait()
            lanes = slice(start, start + width)
            result = jnp.dot(
                wide[...],
                weights[:, :, lanes].reshape(wide.shape[1], width),
                preferred_element_type=jnp.float32,
            )
            total[:, lanes] = result + partial_ref[:, lanes] if add else result

    return rest, squares, total, fill


def partial_kernel(*refs):
    (partial_out, squares_out), squares, total, fill = multiply_halves((False,), False, True, refs)
    squares_out[...] = jnp.broadcast_to(squares, squares_out.shape)
    fill()
    partial_out[...] = total[...]


def qkv_kernel(peers, others, add, resident, *refs):
    (table_ref, *outs), squares, total, fill = multiply_halves(others, add, resident, refs)
    group = lax.axis_index("req")
    rows = squares.shape[0]
    blocks = rows // peers
    far = peers // 2 * blocks
    width = total.shape[1]
    long_squares = [jnp.broadcast_to(squares[r : r + 1], squares.shape) for r in (0, far)]
    sums = in_lanes([squares] + long_squares)
    high, low = split_parts(table_ref[0:1])
    table = jnp.concatenate(
        [high.astype(jnp.float32), low.astype(jnp.float32), jnp.zeros((blocks - 2, LANES), jnp.float32)], 0
    ).astype(jnp.bfloat16)
    fill()
    heads = QUERY_HEADS // KEY_VALUE_HEADS
    long_queries = [
        jnp.concatenate(
            [
                total[k * rows + r : k * rows + r + 1, h * HEAD_SIZE : (h + 1) * HEAD_SIZE]
                for k in range(2)
                for h in range(heads)
            ],
            0,
        ).astype(jnp.bfloat16)
        for r in (0, far)
    ]
    for d, out in enumerate(outs):
        peer = pl.multiple_of(lax.bitwise_xor(group, d) * blocks, blocks)
        for k in range(2):
            out[:, k * width : (k + 1) * width] = total[pl.ds(k * rows + peer, blocks)].astype(
                jnp.bfloat16
            )
        out[:, 2 * width + LANES : 2 * width + 2 * LANES] = table
        for j in range(2):
            first = 2 * width + (2 + j) * LANES
            out[:, first : first + LANES] = long_queries[j]
    total[0:rows, 0:LANES] = sums
    for d, out in enumerate(outs):
        peer = pl.multiple_of(lax.bitwise_xor(group, d) * blocks, blocks)
        out[:, 2 * width : 2 * width + LANES] = total[pl.ds(peer, blocks), 0:LANES].astype(jnp.bfloat16)


def multiply_quarters(distance, wide, weight_refs, partial_ref, sums, out):
    rows, width = sums.shape[0], out.shape[1] - LANES
    start = pl.multiple_of(lax.bitwise_xor(lax.axis_index("req"), distance) * width, LANES)
    result = partial_ref[:, pl.ds(start, width)]
    depth = wide.shape[1] // len(weight_refs)
    for i, weights in enumerate(weight_refs):
        result = result + jnp.dot(
            wide[:, i * depth : (i + 1) * depth],
            weights[:, :, pl.ds(start, width)].reshape(depth, width),
            preferred_element_type=jnp.float32,
        )
    out[:, 0:width] = result.astype(jnp.bfloat16)
    out[0:rows, width:] = sums
    out[rows:, width:] = sums


def gate_up_first_kernel(distance, input_ref, gain_ref, *refs):
    *weight_refs, partial_ref, squares_ref, out, wide, sums_out = refs
    half = input_ref.shape[1]
    first = pl.multiple_of(half_start(True, half), half)
    expand_rows(scale_columns(input_ref[...], gain_ref[:, pl.ds(first, half)]), wide)
    squares = squares_ref[:, 0:1] + sum_squares(input_ref[...])
    sums = in_lanes([squares]).astype(jnp.bfloat16)
    sums_out[...] = sums
    multiply_quarters(distance, wide, weight_refs, partial_ref, sums, out)


def gate_up_next_kernel(distance, wide, sums_ref, *refs):
    *weight_refs, partial_ref, out = refs
    multiply_quarters(distance, wide, weight_refs, partial_ref, sums_ref[...], out)


def project_pairs(kernel, resident, inputs, gain, weight, partial, extra, out_shapes, name):
    rows, half = inputs[0].shape
    pair, width = weight.shape[-2:]
    depth = len(inputs) * half
    operands = [*inputs, gain, weight, *partial, *extra]
    weight_spec = in_vmem(1) if resident else in_hbm(1)
    specs = in_vmem(len(inputs) + 1) + weight_spec + in_vmem(len(partial) + len(extra))
    scratch = [
        pltpu.VMEM((pair * rows, pair * depth), jnp.bfloat16),
        pltpu.VMEM((pair * rows, width), jnp.float32),
    ]
    if not resident:
        scratch += [
            pltpu.VMEM((depth, pair, width), jnp.bfloat16),
            pltpu.SemaphoreType.DMA((len(inputs), len(column_chunks(width)))),
        ]
    return pl.pallas_call(
        kernel,
        out_shape=out_shapes,
        in_specs=specs,
        out_specs=in_vmem(len(out_shapes)),
        scratch_shapes=scratch,
        compiler_params=params(14 if resident else 24),
        name=name,
    )(*operands)


def project_early(own, gain, weights, tokens, name):
    rows, half = own.shape
    pair, width = weights.shape[-2:]
    shapes = [
        jax.ShapeDtypeStruct((pair * rows, width), jnp.float32),
        jax.ShapeDtypeStruct((rows, LANES), jnp.float32),
    ]
    return pl.pallas_call(
        ordered(tokens, partial_kernel),
        out_shape=shapes,
        in_specs=in_any(len(tokens)) + in_vmem(3),
        out_specs=in_vmem(2),
        scratch_shapes=[
            pltpu.VMEM((pair * rows, pair * half), jnp.bfloat16),
            pltpu.VMEM((pair * rows, width), jnp.float32),
        ],
        compiler_params=params(14),
        name=name,
    )(*tokens, own, gain, weights)


def project_qkv(own, other, gain, weight, fetched, tokens, table, peers):
    blocks = own.shape[0] // peers
    shapes = [jax.ShapeDtypeStruct((blocks, 2 * weight.shape[3] + 4 * LANES), jnp.bfloat16)] * peers
    if fetched is None:
        kernel = functools.partial(qkv_kernel, peers, (False, True), False, False)
        return project_pairs(kernel, False, [own, other], gain, weight, [], [table], shapes, "project_qkv")
    partial = project_early(own, gain, fetched[0], tokens, "project_qkv_early")
    kernel = functools.partial(qkv_kernel, peers, (True,), True, True)
    return project_pairs(kernel, True, [other], gain, fetched[1], partial, [table], shapes, "project_qkv")


def exchange_gate_up(section, own, other, gain, fetched, quarters, peers):
    rows, half = own.shape
    shape = jax.ShapeDtypeStruct((2 * rows, quarters[0].shape[2] // peers + LANES), jnp.bfloat16)
    partial, squares = project_early(own, gain, fetched, [], "project_gate_up_early")
    count = len(quarters)
    farthest, wide, sums = pl.pallas_call(
        functools.partial(gate_up_first_kernel, peers - 1),
        out_shape=[
            shape,
            jax.ShapeDtypeStruct((2 * rows, 2 * half), jnp.bfloat16),
            jax.ShapeDtypeStruct((rows, LANES), jnp.bfloat16),
        ],
        in_specs=in_vmem(4 + count),
        out_specs=in_vmem(3),
        compiler_params=params(10),
        name="project_gate_up_first",
    )(other, gain, *quarters, partial, squares)
    received = {peers - 1: swap(farthest, "req", peers - 1, section)}
    tokens = [wide]
    for d in [*range(1, peers - 1), 0]:
        if d == 0:
            tokens.append(received[peers - 1])
        term = pl.pallas_call(
            ordered(tokens, functools.partial(gate_up_next_kernel, d)),
            out_shape=shape,
            in_specs=in_any(len(tokens)) + in_vmem(3 + count),
            out_specs=pl.BlockSpec(memory_space=pltpu.VMEM),
            compiler_params=params(10),
            name="project_gate_up_next",
        )(*tokens, wide, sums, *quarters, partial)
        received[d] = term if d == 0 else swap(term, "req", d, section)
        tokens = [term]
    return [received[d] for d in range(peers)]


def fold_lanes(values, combine):
    blocks = [values[:, i : i + LANES] for i in range(0, values.shape[1], LANES)]
    while len(blocks) > 1:
        pairs = [combine(a, b) for a, b in zip(blocks[::2], blocks[1::2])]
        blocks = pairs + blocks[2 * len(pairs) :]
    return blocks[0]


def attention_kernel(peers, resident, *refs):
    piece_refs, refs = refs[:peers], refs[peers:]
    table_ref, starts, lengths, split, packed_ref, long_ref, out_ref = refs[:7]
    (queries, keys, values, scores, far_scores, far_state, merged_rows) = refs[7:14]
    packed, far, packed_sem, far_sems = (packed_ref, long_ref, None, None) if resident else refs[14:]
    group = lax.axis_index("req")
    blocks = out_ref.shape[0]
    heads = QUERY_HEADS // KEY_VALUE_HEADS
    pairs = 2 * heads
    window = scores.shape[2] // 2
    slots = packed.shape[0]
    far_chunks = far.shape[1] // FAR_SLOTS
    scale = 1.0 / math.sqrt(HEAD_SIZE)
    live = [split[0, 0], split[1, 0]]

    def far_copy(j, c):
        return pltpu.make_async_copy(
            long_ref.at[0, j, pl.ds(c * FAR_SLOTS, FAR_SLOTS)],
            far.at[j, pl.ds(c * FAR_SLOTS, FAR_SLOTS)],
            far_sems.at[j, c],
        )

    if not resident:
        packed_copy = pltpu.make_async_copy(packed_ref.at[0], packed, packed_sem)
        packed_copy.start()
    for j in range(0 if resident else 2):
        for c in range(far_chunks):

            @pl.when(c * FAR_SLOTS < live[j])
            def _():
                far_copy(j, c).start()

    width = HEAD_SIZE * (heads + 2)

    def summed_block(start):
        return sum(piece[:, start : start + LANES].astype(jnp.float32) for piece in piece_refs)

    sums = summed_block(2 * width)
    scale_rows = row_scale(from_lanes(sums, 0))
    tables = [
        piece[:, 2 * width + LANES : 2 * width + 2 * LANES].astype(jnp.float32) for piece in piece_refs
    ]
    tables = [t[0:1] + t[1:2] for t in tables]
    far_tables = [
        sum(
            jnp.where(lax.bitwise_xor(group, d) == j * (peers // 2), t, 0.0)
            for d, t in enumerate(tables)
        )
        for j in range(2)
    ]
    def cosine_sine(table):
        turned = pltpu.roll(table, HEAD_SIZE // 2, 1)
        lower = lax.broadcasted_iota(jnp.int32, table.shape, 1) < HEAD_SIZE // 2
        return jnp.where(lower, table, turned), jnp.where(lower, -turned, table)

    def rotated(block, angles):
        cosine, sine = angles
        return block * cosine + pltpu.roll(block, HEAD_SIZE // 2, 1) * sine

    own_angles = cosine_sine(table_ref[...])
    far_queries = [
        rotated(
            summed_block(2 * width + (2 + j) * LANES) * row_scale(from_lanes(sums, 1 + j)),
            cosine_sine(jnp.broadcast_to(far_tables[j], table_ref.shape)),
        ).astype(jnp.bfloat16)
        for j in range(2)
    ]
    for k in range(2):
        for b in range(heads + 2):
            block = summed_block(k * width + b * HEAD_SIZE) * scale_rows
            if b <= heads:
                block = rotated(block, own_angles)
            block = block.astype(jnp.bfloat16).astype(jnp.float32)
            if b < heads:
                queries[:, k * heads + b, :] = block
            else:
                for h in range(heads):
                    (keys if b == heads else values)[:, k * heads + h, :] = block

    def same_head(columns):
        row = lax.broadcasted_iota(jnp.int32, (pairs, columns), 0)
        column = lax.broadcasted_iota(jnp.int32, (pairs, columns), 1)
        return (row // heads) == (column % 2), column // 2

    def contract(a, b):
        return lax.dot_general(a, b, (((1,), (1,)), ((), ())), preferred_element_type=jnp.float32)

    if not resident:
        packed_copy.wait()
    matching, slot = same_head(2 * window)
    first_slots = []
    for r in range(blocks):
        first = jnp.minimum(starts[r], slots - window)
        first_slots.append(first)
        low = starts[r] - first
        segment = packed[pl.ds(first, window), :, 0:HEAD_SIZE].reshape(2 * window, HEAD_SIZE)
        own = contract(queries[r].astype(jnp.bfloat16), segment) * scale
        inside = matching & (slot >= low) & (slot < low + lengths[r])
        scores[r] = jnp.where(inside, own, LOWEST)
    own_score = jnp.sum(queries[...] * keys[...], axis=-1, keepdims=True) * scale
    row_max = jnp.maximum(jnp.max(scores[...], axis=-1, keepdims=True), own_score)
    weights = jnp.exp(scores[...] - row_max).astype(jnp.bfloat16)
    own_weight = jnp.exp(own_score - row_max).astype(jnp.bfloat16).astype(jnp.float32)
    totals = jnp.sum(weights.astype(jnp.float32), axis=-1, keepdims=True) + own_weight
    near_peak = row_max[0] + jnp.log(totals[0])
    for r in range(blocks):
        segment = packed[pl.ds(first_slots[r], window), :, HEAD_SIZE:].reshape(2 * window, HEAD_SIZE)
        summed = jnp.dot(weights[r], segment, preferred_element_type=jnp.float32)
        summed = summed + own_weight[r] * values[r]
        merged_rows[r] = summed / totals[r]

    matching, slot = same_head(2 * FAR_SLOTS)
    log_totals = []
    for j in range(2):
        long_rows = far_queries[j]
        far_state[0] = jnp.full((pairs, LANES), LOWEST, jnp.float32)
        far_state[1] = jnp.zeros((pairs, LANES), jnp.float32)
        far_state[2] = jnp.zeros((pairs, HEAD_SIZE), jnp.float32)

        def rows_of(c, first):
            part = far[j, c * FAR_SLOTS : (c + 1) * FAR_SLOTS, :, first : first + HEAD_SIZE]
            return part.reshape(2 * FAR_SLOTS, HEAD_SIZE)

        for c in range(far_chunks):

            @pl.when(c * FAR_SLOTS < live[j])
            def _():
                if not resident:
                    far_copy(j, c).wait()
                found = contract(long_rows, rows_of(c, 0)) * scale
                found = jnp.where(matching & (slot < live[j] - c * FAR_SLOTS), found, LOWEST)
                far_scores[c] = found
                far_state[0] = jnp.maximum(far_state[0], fold_lanes(found, jnp.maximum))

        peak = jnp.max(far_state[0], axis=-1, keepdims=True)
        for c in range(far_chunks):

            @pl.when(c * FAR_SLOTS < live[j])
            def _():
                weight = jnp.exp(far_scores[c] - peak).astype(jnp.bfloat16)
                far_state[1] = far_state[1] + fold_lanes(weight.astype(jnp.float32), jnp.add)
                far_state[2] = far_state[2] + jnp.dot(
                    weight, rows_of(c, HEAD_SIZE), preferred_element_type=jnp.float32
                )

        total = jnp.sum(far_state[1], axis=-1, keepdims=True)
        summed = far_state[2]
        far_peak = peak + jnp.log(total)
        result = summed / total
        owner = group == j * (peers // 2)
        top = jnp.maximum(far_peak, near_peak)
        far_part = jnp.exp(far_peak - top)
        near_part = jnp.exp(near_peak - top)
        both = far_part + near_part
        result = jnp.where(owner, (result * far_part + merged_rows[0] * near_part) / both, result)
        log_total = jnp.where(owner, top + jnp.log(both), far_peak)
        out_ref[:, (pairs + j) * LANES : (pairs + j + 1) * LANES] = result.astype(jnp.bfloat16)
        log_totals.append(log_total)
    out_ref[:, (pairs + 2) * LANES :] = in_lanes(log_totals).astype(jnp.bfloat16)
    for b in range(pairs):
        out_ref[:, b * HEAD_SIZE : (b + 1) * HEAD_SIZE] = merged_rows[:, b, :].astype(jnp.bfloat16)


def attend(pieces, table, starts, lengths, split, packed_cache, long_cache, resident, tokens):
    peers = len(pieces)
    blocks = pieces[0].shape[0]
    heads = QUERY_HEADS // KEY_VALUE_HEADS
    pairs = 2 * heads
    slots = packed_cache.shape[-3]
    far_slots = long_cache.shape[-3]
    scratch = [
        pltpu.VMEM((blocks, pairs, HEAD_SIZE), jnp.float32),
        pltpu.VMEM((blocks, pairs, HEAD_SIZE), jnp.float32),
        pltpu.VMEM((blocks, pairs, HEAD_SIZE), jnp.float32),
        pltpu.VMEM((blocks, pairs, 2 * MOST_SLOTS), jnp.float32),
        pltpu.VMEM((far_slots // FAR_SLOTS, pairs, 2 * FAR_SLOTS), jnp.float32),
        pltpu.VMEM((3, pairs, LANES), jnp.float32),
        pltpu.VMEM((blocks, pairs, HEAD_SIZE), jnp.float32),
    ]
    if not resident:
        scratch += [
            pltpu.VMEM((slots, 2, 2 * HEAD_SIZE), jnp.bfloat16),
            pltpu.VMEM((2, far_slots, 2, 2 * HEAD_SIZE), jnp.bfloat16),
            pltpu.SemaphoreType.DMA,
            pltpu.SemaphoreType.DMA((2, far_slots // FAR_SLOTS)),
        ]
    return pl.pallas_call(
        ordered(tokens, functools.partial(attention_kernel, peers, resident)),
        out_shape=jax.ShapeDtypeStruct((blocks, (pairs + 3) * HEAD_SIZE), jnp.bfloat16),
        in_specs=in_any(len(tokens))
        + in_vmem(peers + 1)
        + in_smem(3)
        + (in_vmem(2) if resident else in_hbm(2)),
        out_specs=pl.BlockSpec(memory_space=pltpu.VMEM),
        scratch_shapes=scratch,
        compiler_params=params(14 if resident else 34),
        name="attend",
    )(*tokens, *pieces, table, starts, lengths, split, packed_cache, long_cache)


def multiply_columns(rows_of, weights, write):
    for start, width in column_chunks(weights.shape[1]):
        lanes = slice(start, start + width)
        write(lanes, jnp.dot(rows_of[...], weights[:, lanes], preferred_element_type=jnp.float32))


def output_early_kernel(peers, *refs):
    piece_refs, refs = refs[:peers], refs[peers:]
    weights, out_ref, whole = refs
    group = lax.axis_index("req")
    blocks = piece_refs[0].shape[0]
    depth = weights.shape[0]
    pairs = depth // LANES
    for d, piece in enumerate(piece_refs):
        start = pl.multiple_of(lax.bitwise_xor(group, d) * blocks, blocks)
        whole[pl.ds(start, blocks)] = piece[:, 0:depth]
    ends = [piece[:, depth:].astype(jnp.float32) for piece in piece_refs]
    for j in range(2):
        peaks = [from_lanes(end[:, 2 * LANES :], j) for end in ends]
        top = functools.reduce(jnp.maximum, peaks)
        parts = [jnp.exp(peak - top) for peak in peaks]
        merged = sum(end[:, j * LANES : (j + 1) * LANES] * part for end, part in zip(ends, parts))
        merged = merged / sum(parts)
        merged_row = jnp.concatenate([merged[i : i + 1] for i in range(pairs)], 1)
        rows = slice(j * (peers // 2) * blocks, j * (peers // 2) * blocks + blocks)
        row = lax.broadcasted_iota(jnp.int32, (blocks, depth), 0)
        whole[rows] = jnp.where(
            row == 0, merged_row, whole[rows].astype(jnp.float32)
        ).astype(jnp.bfloat16)

    def write(lanes, result):
        out_ref[:, lanes] = result.astype(jnp.bfloat16)

    multiply_columns(whole, weights, write)


def output_late_kernel(whole, weights, out_ref):
    def write(lanes, result):
        out_ref[:, lanes] = result.astype(jnp.bfloat16)

    multiply_columns(whole, weights, write)


def project_output(pieces, weights, token):
    rows = len(pieces) * pieces[0].shape[0]
    depth, half = weights[0].shape
    shape = jax.ShapeDtypeStruct((rows, half), jnp.bfloat16)
    sent, whole = pl.pallas_call(
        ordered([token], functools.partial(output_early_kernel, len(pieces))),
        out_shape=[shape, jax.ShapeDtypeStruct((rows, depth), jnp.bfloat16)],
        in_specs=in_any(1) + in_vmem(len(pieces) + 1),
        out_specs=in_vmem(2),
        compiler_params=params(12),
        name="project_output_sent",
    )(token, *pieces, weights[0])
    kept = pl.pallas_call(
        output_late_kernel,
        out_shape=shape,
        in_specs=in_vmem(2),
        out_specs=pl.BlockSpec(memory_space=pltpu.VMEM),
        compiler_params=params(12),
        name="project_output_kept",
    )(whole, weights[1])
    return sent, kept


def down_kernel(count, other, *refs):
    piece_refs, (weights, *refs) = refs[:count], refs[count:]
    partial_ref = None if other is None else refs.pop(0)
    out_ref, whole = refs
    units = piece_refs[0].shape[1]
    width = weights.shape[1]
    first = 0 if other is None else pl.multiple_of(half_start(other, width), width)
    for p, piece in enumerate(piece_refs):
        whole[:, p * units : (p + 1) * units] = piece[...]

    def write(lanes, result):
        if other is not None:
            start = pl.multiple_of(first + lanes.start, LANES)
            result = result + partial_ref[:, pl.ds(start, lanes.stop - lanes.start)]
        out_ref[:, lanes] = result.astype(out_ref.dtype)

    multiply_columns(whole, weights, write)


def call_down(other, pieces, weights, partial, name):
    rows = pieces[0].shape[0]
    depth, width = weights.shape
    dtype = jnp.float32 if other is None else jnp.bfloat16
    return pl.pallas_call(
        functools.partial(down_kernel, len(pieces), other),
        out_shape=jax.ShapeDtypeStruct((rows, width), dtype),
        in_specs=in_vmem(len(pieces) + 1 + len(partial)),
        out_specs=pl.BlockSpec(memory_space=pltpu.VMEM),
        scratch_shapes=[pltpu.VMEM((rows, depth), jnp.bfloat16)],
        compiler_params=params(12),
        name=name,
    )(*pieces, weights, *partial)


def project_down(pieces, weights):
    early, late = down_order(len(pieces))
    partial = call_down(None, [pieces[d] for d in early], weights[0], [], "project_down_early")
    rest = [pieces[d] for d in late]
    sent = call_down(True, rest, weights[1], [partial], "project_down_sent")
    kept = call_down(False, rest, weights[2], [partial], "project_down_kept")
    return sent, kept


def hidden_kernel(peers, *refs):
    piece_refs, out_ref = refs[:peers], refs[peers]
    rows, width = out_ref.shape
    sums = sum(piece[0:rows, width:].astype(jnp.float32) for piece in piece_refs)
    factor = row_scale(from_lanes(sums, 0))

    def summed(first):
        return sum(piece[first : first + rows, 0:width].astype(jnp.float32) for piece in piece_refs) * factor

    gate, up = summed(0), summed(rows)
    out_ref[...] = (gate / (1.0 + jnp.exp(-gate)) * up).astype(jnp.bfloat16)


def gated_units(pieces, token):
    rows, width = pieces[0].shape[0] // 2, pieces[0].shape[1] - LANES
    return pl.pallas_call(
        ordered([token], functools.partial(hidden_kernel, len(pieces))),
        out_shape=jax.ShapeDtypeStruct((rows, width), jnp.bfloat16),
        in_specs=in_any(1) + in_vmem(len(pieces)),
        out_specs=pl.BlockSpec(memory_space=pltpu.VMEM),
        compiler_params=params(8),
        name="gated_units",
    )(token, *pieces)


def residual_kernel(base, terms, out):
    out[...] = (base[...].astype(jnp.float32) + terms[...]).astype(jnp.bfloat16)


def add_residual(base, terms, token):
    return pl.pallas_call(
        ordered([token], residual_kernel),
        out_shape=jax.ShapeDtypeStruct(base.shape, jnp.bfloat16),
        in_specs=in_any(1) + in_vmem(2),
        out_specs=pl.BlockSpec(memory_space=pltpu.VMEM),
        compiler_params=params(4),
        name="add_residual",
    )(token, base, terms)


def fast_layer(section, own, other, fetched, attention_gain, query_key_value_weight, out_weight, feedforward_gain, gate_up, down_weight, packed_cache, long_cache, table, *segments):
    req_count = lax.axis_size("req")
    qkv_fetched, out_fetched, caches, tokens = fetched or (None, None, None, [])
    terms = project_qkv(
        own, other, attention_gain, query_key_value_weight, qkv_fetched, tokens, table, req_count
    )
    terms = swap_all(terms, "req", section)
    first_quarter, token = fetch_quarter(gate_up, 0, terms[1], "fetch_gate_up_first")
    if fetched is None:
        *out_fetched, out_token = fetch_output(out_weight, terms[1])
        attended = attend(terms, table, *segments, packed_cache, long_cache, False, [token, out_token])
    else:
        attended = attend(terms, table, *segments, *caches, True, [token])
    pieces = spread(attended, "req", section)
    second_quarter, token = fetch_quarter(gate_up, 1, pieces[1], "fetch_gate_up_second")
    sent, kept = project_output(pieces, out_fetched, token)
    pair = sum_pair(sent, kept, "head", section)
    gate_fetched, token = fetch_halves(gate_up, (False,), pair, "fetch_gate_up")
    residual = add_residual(own, sum_doubling(pair, "head", section), token)
    other_residual = swap(residual, "head", 1, section)
    quarters = [first_quarter, second_quarter]
    terms = exchange_gate_up(
        section, residual, other_residual, feedforward_gain, gate_fetched, quarters, req_count
    )
    *down_fetched, token = fetch_down(down_weight, req_count, terms[1])
    hidden = spread(gated_units(terms, token), "req", section)
    sent, kept = project_down(hidden, down_fetched)
    lowered = sum_doubling(sum_pair(sent, kept, "head", section), "head", section)
    return (residual.astype(jnp.float32) + lowered).astype(jnp.bfloat16)


def rope_table(lengths):
    req_count, group = lax.axis_size("req"), lax.axis_index("req")
    owner = (group == 0) | (group == req_count // 2)
    long_row = (jnp.arange(lengths.shape[1]) == 0) & owner
    position = lengths[0] + jnp.where(long_row, LONG, 0).astype(jnp.int32)
    half_dim = HEAD_SIZE // 2
    inverse = 1.0 / 10000.0 ** (jnp.arange(half_dim).astype(jnp.float32) * 2.0 / HEAD_SIZE)
    angles = position.astype(jnp.float32)[:, None] * inverse[None, :]
    return jnp.concatenate([jnp.cos(angles), jnp.sin(angles)], 1)


def fast_local(tokens, attention_gain, query_key_value_weight, head_output_weight, feedforward_gain, gate_up, down_weight, packed_cache, long_cache, lengths, long_split):
    out_weight = head_output_weight.reshape(-1, head_output_weight.shape[3])
    query_key_value_weight, out_weight, gate_up, down_weight, packed_cache, long_cache = [
        pltpu.with_memory_space_constraint(array, pltpu.HBM)
        for array in (query_key_value_weight, out_weight, gate_up, down_weight, packed_cache, long_cache)
    ]
    layer_arrays = (
        attention_gain,
        query_key_value_weight,
        out_weight,
        feedforward_gain,
        gate_up,
        down_weight,
        packed_cache,
        long_cache,
        rope_table(lengths),
        jnp.cumsum(lengths[0]) - lengths[0],
        lengths[0],
        long_split,
    )
    half = tokens.shape[1] // 2
    own, other = [lax.dynamic_slice_in_dim(tokens, half_start(o, half), half, 1) for o in (False, True)]
    first = fast_layer(0, own, other, None, *layer_arrays)
    own, other = [swap(first, "head", d, 0, 1) for d in range(2)]
    *qkv_fetched, qkv_token = fetch_halves(query_key_value_weight, (False, True), first, "fetch_qkv")
    *out_fetched, out_token = fetch_output(out_weight, first)
    *caches, caches_token = fetch_caches(packed_cache, long_cache, first)
    fetched = (qkv_fetched, out_fetched, caches, [qkv_token, out_token, caches_token])
    first_other = swap(first, "head", 1, 0)
    second = fast_layer(1, own, other, fetched, *layer_arrays)
    second_other = swap(second, "head", 1, 1)
    is_first = lax.axis_index("section") == 0
    own, other = jnp.where(is_first, first, second), jnp.where(is_first, first_other, second_other)
    own_first = half_start(False, half) == 0
    return jnp.where(
        own_first, jnp.concatenate([own, other], 1), jnp.concatenate([other, own], 1)
    )[None]


def is_power_of_two(value):
    return value & (value - 1) == 0


def fits_fast(mesh):
    req_count, head_count = mesh.shape["req"], mesh.shape["head"]
    columns = MODEL_WIDTH // req_count // 2
    return (
        mesh.shape["section"] == 2
        and is_power_of_two(req_count)
        and is_power_of_two(head_count)
        and req_count >= 4
        and head_count >= 2
        and KEY_VALUE_HEADS == 2 * head_count
        and columns % COLUMNS == 0
        and FF % (head_count * COLUMNS) == 0
        and FF % (head_count * req_count * LANES) == 0
    )


def solution(mesh):
    placed = (
        P(None, "req"),
        P("section", "req"),
        P("section", "req", "head", None),
        P("section", "head", None, "req"),
        P("section", "req"),
        P("section", "req", None, "head"),
        P("section", "head", "req"),
        P("section", "req", "head", None),
        P("section", None, "req", "head", None),
        P("req", None),
        P(None, "req"),
    )
    return jax.shard_map(
        fast_local if fits_fast(mesh) else local,
        mesh=mesh,
        in_specs=placed, out_specs=P("section", None, "req"), check_vma=False
    )
```

```python
import functools
import math

import jax
import jax.numpy as jnp
from jax import lax
from jax.experimental import pallas as pl
from jax.experimental.pallas import tpu as pltpu
from jax.sharding import PartitionSpec as P

MODEL_WIDTH = 8192
QUERY_HEADS = 64
KEY_VALUE_HEADS = 8
HEAD_SIZE = 128
LONG = 16384
FF = 14336
MOST_SLOTS = 256
LANES = 128
COLUMNS = 512
FAR_SLOTS = 2048
LOWEST = -1e30
PARTS = 4


EPSILON = 1e-05


def merged(part, axis, combine):
    gathered = jax.tree.map(lambda a: lax.all_gather(a, axis), part)

    def take(source):
        return jax.tree.map(lambda a: lax.dynamic_index_in_dim(a, source, 0, False), gathered)

    return lax.fori_loop(
        1, lax.axis_size(axis), lambda source, state: combine(state, take(source)), take(0)
    )


def shifted(value, axis, by):
    peers = lax.axis_size(axis)
    pairs = [(i, i + by) for i in range(peers) if 0 <= i + by < peers]
    return lax.ppermute(value, axis, pairs)


def rotate(values, position):
    half_dim = values.shape[-1] // 2
    freq_ids = jnp.arange(half_dim).astype(jnp.float32)
    inverse = 1.0 / 10000.0 ** (freq_ids * 2.0 / values.shape[-1])
    angles = position.astype(jnp.float32)[:, None] * inverse[None, :]
    cosine = jnp.cos(angles)[:, None, None, :]
    sine_part = jnp.sin(angles)[:, None, None, :]
    lower_half = values[..., :half_dim]
    upper_half = values[..., half_dim:]
    return jnp.concatenate(
        [
            lower_half * cosine - upper_half * sine_part,
            upper_half * cosine + lower_half * sine_part,
        ],
        -1,
    )


def add_pair(earlier, second_part):
    return earlier + second_part


def combine_partial(earlier, second_part):
    peak = jnp.maximum(earlier[0], second_part[0])
    left_factor = jnp.exp(earlier[0] - peak)
    right_factor = jnp.exp(second_part[0] - peak)
    softmax_total = earlier[1] * left_factor + second_part[1] * right_factor
    weighted_sum = earlier[2] * left_factor[..., None] + second_part[2] * right_factor[..., None]
    return (peak, softmax_total, weighted_sum)


def over_requests(values, combiner):
    return merged(values, "req", combiner)


def rows_apply(values, row_fn):
    return row_fn(lax.all_gather(values, "req", axis=0, tiled=True), jnp.int32(0))


def rows_project(term_fn, row_count):
    return lax.psum_scatter(
        term_fn(jnp.int32(0), row_count * lax.axis_size("req")),
        "req",
        scatter_dimension=0,
        tiled=True,
    )


def head_total(values):
    return lax.psum(values, "head")


def keep_rows(piece_rows, start_row):
    return piece_rows


def norm_rows(values, gain_row):
    floats = values.astype(jnp.float32)
    squares = over_requests(jnp.sum(floats * floats, axis=-1), add_pair)
    return (
        floats * lax.rsqrt(squares / MODEL_WIDTH + EPSILON)[:, None] * gain_row.astype(jnp.float32)
    ).astype(jnp.bfloat16)


def decoder_layer(
    inputs,
    micro_batch,
    attention_gain,
    query_key_value_weight,
    head_output_weight,
    feedforward_gain,
    gate_up,
    down_weight,
    packed_cache,
    long_cache,
    lengths,
    long_split,
):
    req_count = lax.axis_size("req")
    group_index = lax.axis_index("req")
    blocks = inputs.shape[0] // req_count
    columns = query_key_value_weight.shape[1]
    kv_local = query_key_value_weight.shape[2]
    requests_per_group = QUERY_HEADS // KEY_VALUE_HEADS
    score_scale = 1.0 / math.sqrt(HEAD_SIZE)
    normalized_input = norm_rows(inputs, attention_gain[0])
    in_weights = query_key_value_weight[0].reshape(
        columns, kv_local * (requests_per_group + 2) * HEAD_SIZE
    )

    def qkv_term(start_row, row_count):
        return jnp.dot(normalized_input, in_weights, preferred_element_type=jnp.float32)

    projected_rows = rows_project(qkv_term, blocks).reshape(
        blocks, kv_local, requests_per_group + 2, HEAD_SIZE
    )
    local_rows = jnp.arange(blocks)
    row_lengths = lengths[0]
    owner_long = (group_index == 0) | (group_index == req_count // 2)
    long_row = (local_rows == 0) & (micro_batch == 0) & owner_long
    position = row_lengths + jnp.where(long_row, LONG, 0).astype(jnp.int32)
    queries = rotate(projected_rows[:, :, :requests_per_group], position).astype(jnp.bfloat16)
    new_key = rotate(projected_rows[:, :, requests_per_group : requests_per_group + 1], position)[
        :, :, 0
    ].astype(jnp.bfloat16)
    new_value = projected_rows[:, :, requests_per_group + 1].astype(jnp.bfloat16)
    gathered = rows_apply(
        queries[0:1].reshape(1, kv_local * requests_per_group * HEAD_SIZE), keep_rows
    )
    long_queries = jnp.stack([gathered[0], gathered[req_count // 2]]).reshape(
        2, kv_local, requests_per_group, HEAD_SIZE
    )
    far_cache = long_cache[0]
    far_live = (jnp.arange(far_cache.shape[1])[None, :] < long_split[:, 0][:, None])[
        :, None, None, :
    ]
    far_scores = (
        jnp.einsum(
            "jkhd,jpkd->jkhp",
            long_queries,
            far_cache[..., :HEAD_SIZE],
            preferred_element_type=jnp.float32,
        )
        * score_scale
    )
    far_max = jnp.max(jnp.where(far_live, far_scores, -jnp.inf), axis=-1)
    far_weights = jnp.where(
        far_live, jnp.exp(jnp.where(far_live, far_scores - far_max[..., None], 0.0)), 0.0
    ).astype(jnp.bfloat16)
    far_totals = jnp.sum(far_weights.astype(jnp.float32), axis=-1)
    far_summed = jnp.einsum(
        "jkhp,jpkd->jkhd",
        far_weights,
        far_cache[..., HEAD_SIZE:],
        preferred_element_type=jnp.float32,
    )
    far_max, far_totals, far_summed = over_requests(
        (far_max, far_totals, far_summed), combine_partial
    )
    far_index = jnp.where(group_index == 0, 0, 1)
    chosen_max = lax.dynamic_index_in_dim(far_max, far_index, 0, keepdims=False)
    chosen_totals = lax.dynamic_index_in_dim(far_totals, far_index, 0, keepdims=False)
    chosen_summed = lax.dynamic_index_in_dim(far_summed, far_index, 0, keepdims=False)
    pack_part = packed_cache[0]
    seg_ends = jnp.cumsum(lengths[0])
    slot_ids = jnp.arange(pack_part.shape[0])
    slot_owner = jnp.sum((slot_ids[:, None] >= seg_ends[None, :]).astype(jnp.int32), axis=1)
    request_ids = micro_batch * blocks + local_rows
    in_segment = (slot_owner[None, :] == request_ids[:, None])[:, None, None, :]
    scores = (
        jnp.einsum(
            "rkhd,pkd->rkhp",
            queries,
            pack_part[..., :HEAD_SIZE],
            preferred_element_type=jnp.float32,
        )
        * score_scale
    )
    own_score = (
        jnp.einsum("rkhd,rkd->rkh", queries, new_key, preferred_element_type=jnp.float32)
        * score_scale
    )
    row_max = jnp.maximum(jnp.max(jnp.where(in_segment, scores, -jnp.inf), axis=-1), own_score)
    long_mask = long_row[:, None, None]
    row_max = jnp.where(long_mask, jnp.maximum(row_max, chosen_max[None]), row_max)
    weights = jnp.where(
        in_segment, jnp.exp(jnp.where(in_segment, scores - row_max[..., None], 0.0)), 0.0
    ).astype(jnp.bfloat16)
    own_weights = jnp.exp(own_score - row_max).astype(jnp.bfloat16)
    far_factor = jnp.where(
        long_mask, jnp.exp(jnp.where(long_mask, chosen_max[None] - row_max, 0.0)), 0.0
    )
    softmax_total = (
        jnp.sum(weights.astype(jnp.float32), axis=-1)
        + own_weights.astype(jnp.float32)
        + far_factor * chosen_totals[None]
    )
    weighted_sum = jnp.einsum(
        "rkhp,pkd->rkhd", weights, pack_part[..., HEAD_SIZE:], preferred_element_type=jnp.float32
    )
    weighted_sum = (
        weighted_sum
        + own_weights.astype(jnp.float32)[..., None] * new_value.astype(jnp.float32)[:, :, None, :]
    )
    weighted_sum = weighted_sum + far_factor[..., None] * chosen_summed[None]
    attended_heads = (
        (weighted_sum / softmax_total[..., None])
        .astype(jnp.bfloat16)
        .reshape(blocks, kv_local * requests_per_group * HEAD_SIZE)
    )
    out_weights = head_output_weight[0].reshape(kv_local * requests_per_group * HEAD_SIZE, columns)

    def project_heads(piece_rows, start_row):
        return jnp.dot(piece_rows, out_weights, preferred_element_type=jnp.float32)

    attended = head_total(rows_apply(attended_heads, project_heads))
    residual = (inputs.astype(jnp.float32) + attended).astype(jnp.bfloat16)
    normed_two = norm_rows(residual, feedforward_gain[0])
    ff_weights = gate_up[0].reshape(columns, -1)

    def ff_term(start_row, row_count):
        return jnp.dot(normed_two, ff_weights, preferred_element_type=jnp.float32)

    gate_and_up = rows_project(ff_term, blocks)
    hidden_width = gate_and_up.shape[1] // 2
    hidden = (jax.nn.silu(gate_and_up[:, :hidden_width]) * gate_and_up[:, hidden_width:]).astype(
        jnp.bfloat16
    )
    lower_weights = down_weight[0]

    def project_hidden(piece_rows, start_row):
        return jnp.dot(piece_rows, lower_weights, preferred_element_type=jnp.float32)

    lowered = head_total(rows_apply(hidden, project_hidden))
    return (residual.astype(jnp.float32) + lowered).astype(jnp.bfloat16)


def local(
    tokens,
    attention_gain,
    query_key_value_weight,
    head_output_weight,
    feedforward_gain,
    gate_up,
    down_weight,
    packed_cache,
    long_cache,
    lengths,
    long_split,
):
    req_count = lax.axis_size("req")
    section_index = lax.axis_index("section")
    batch_count = 1
    per_group = tokens.shape[0] // req_count
    blocks = per_group // batch_count
    columns = tokens.shape[1]
    token_grid = tokens.reshape(req_count, per_group, columns)
    result = jnp.zeros_like(token_grid)
    incoming = jnp.zeros((req_count * blocks, columns), jnp.bfloat16)
    for phase_step in range(batch_count + 1):
        micro_batch = phase_step - section_index
        is_active = (micro_batch >= 0) & (micro_batch < batch_count)
        micro_batch = jnp.clip(micro_batch, 0, batch_count - 1)
        new_batch = token_grid.reshape(req_count * blocks, columns)
        inputs = jnp.where(section_index == 0, new_batch, incoming)
        output = decoder_layer(
            inputs,
            micro_batch,
            attention_gain,
            query_key_value_weight,
            head_output_weight,
            feedforward_gain,
            gate_up,
            down_weight,
            packed_cache,
            long_cache,
            lengths,
            long_split,
        )
        placed = output.reshape(req_count, blocks, columns)
        result = jnp.where(is_active, placed, result)
        if phase_step < batch_count:
            incoming = shifted(output, "section", 1)
    return result.reshape(1, req_count * per_group, columns)

def swap(value, axis, distance, section, target_section=None):
    size = lax.axis_size(axis)
    target_section = section if target_section is None else target_section
    pairs = [(section * size + i, target_section * size + (i ^ distance)) for i in range(size)]
    return lax.ppermute(value, ("section", axis), pairs)


def swap_all(values, axis, section):
    received = {d: swap(values[d], axis, d, section) for d in reversed(range(1, len(values)))}
    return [values[0]] + [received[d] for d in range(1, len(values))]


def spread(value, axis, section):
    return swap_all([value] * lax.axis_size(axis), axis, section)


def sum_doubling(value, axis, section):
    distance = 2
    total = value.astype(jnp.float32)
    while distance < lax.axis_size(axis):
        other = swap(value, axis, distance, section)
        total = value.astype(jnp.float32) + other.astype(jnp.float32)
        value = total.astype(jnp.bfloat16)
        distance *= 2
    return total


def sum_pair(sent, kept, axis, section):
    pair = kept.astype(jnp.float32) + swap(sent, axis, 1, section).astype(jnp.float32)
    return pair.astype(jnp.bfloat16)


def half_start(other, half):
    index = lax.bitwise_and(lax.axis_index("head"), 1)
    return (1 - index if other else index) * half


def in_vmem(count):
    return [pl.BlockSpec(memory_space=pltpu.VMEM)] * count


def in_hbm(count):
    return [pl.BlockSpec(memory_space=pltpu.HBM)] * count


def in_smem(count):
    return [pl.BlockSpec(memory_space=pltpu.SMEM)] * count


def params(mebibytes):
    return pltpu.CompilerParams(vmem_limit_bytes=mebibytes * 2**20)


def in_any(count):
    return [pl.BlockSpec(memory_space=pl.ANY)] * count


def ordered(tokens, kernel):
    def run(*refs):
        kernel(*refs[len(tokens) :])

    return run


def fetch_kernel(count, plan, *refs):
    sources, refs = refs[:count], refs[count + 1 :]
    *targets, token, sems = refs
    token[...] = jnp.zeros_like(token)
    copies = [
        pltpu.make_async_copy(source, target, sems.at[i])
        for i, (source, target) in enumerate(plan(sources, targets))
    ]
    for copy in copies:
        copy.start()
    for copy in copies:
        copy.wait()


def fetch(plan, copies, arrays, shapes, after, name):
    return pl.pallas_call(
        functools.partial(fetch_kernel, len(arrays), plan),
        out_shape=[pltpu.VMEM(shape, jnp.bfloat16) for shape in shapes]
        + [jax.ShapeDtypeStruct((8, LANES), jnp.float32)],
        in_specs=in_hbm(len(arrays)) + in_any(1),
        out_specs=in_vmem(len(shapes) + 1),
        scratch_shapes=[pltpu.SemaphoreType.DMA((copies,))],
        compiler_params=params(2),
        name=name,
    )(*arrays, after)


def row_parts(source, first, target, rows, parts):
    size = rows // parts
    return [
        (source.at[pl.ds(first + i * size, size)], target.at[pl.ds(i * size, size)])
        for i in range(parts)
    ]


def fetch_halves(weight, others, after, name):
    half, shape = weight.shape[1] // 2, weight.shape[2:]

    def plan(sources, targets):
        parts = []
        for other, target in zip(others, targets):
            first = pl.multiple_of(half_start(other, half), half)
            parts += row_parts(sources[0].at[0], first, target, half, PARTS)
        return parts

    shapes = [(half, *shape)] * len(others)
    return fetch(plan, PARTS * len(others), [weight], shapes, after, name)


def fetch_quarter(weight, part, after, name):
    half, shape = weight.shape[1] // 2, weight.shape[2:]
    quarter = half // 2

    def plan(sources, targets):
        first = pl.multiple_of(half_start(True, half) + part * quarter, quarter)
        return row_parts(sources[0].at[0], first, targets[0], quarter, PARTS)

    return fetch(plan, PARTS, [weight], [(quarter, *shape)], after, name)


def fetch_output(weight, after):
    depth, half = weight.shape[0], weight.shape[1] // 2

    def plan(sources, targets):
        parts = []
        for other, target in zip((True, False), targets):
            first = pl.multiple_of(half_start(other, half), half)
            parts += row_parts(sources[0].at[:, pl.ds(first, half)], 0, target, depth, PARTS)
        return parts

    return fetch(plan, 2 * PARTS, [weight], [(depth, half)] * 2, after, "fetch_output")


def fetch_down(weight, peers, early, after, name):
    depth, width = weight.shape[1:]
    units, half = depth // peers, width // 2
    distances = down_order(peers)[0 if early else 1]
    others = (None,) if early else (True, False)

    def plan(sources, targets):
        group = lax.axis_index("req")
        parts = []
        for target, other in zip(targets, others):
            columns = target.shape[1]
            first = 0 if other is None else pl.multiple_of(half_start(other, half), half)
            for p, d in enumerate(distances):
                row = pl.multiple_of(lax.bitwise_xor(group, d) * units, LANES)
                parts.append(
                    (
                        sources[0].at[0, pl.ds(row, units), pl.ds(first, columns)],
                        target.at[pl.ds(p * units, units)],
                    )
                )
        return parts

    rows = len(distances) * units
    shapes = [(rows, width if other is None else half) for other in others]
    return fetch(plan, len(distances) * len(others), [weight], shapes, after, name)


def fetch_caches(packed_cache, long_cache, after):
    far_slots = long_cache.shape[2]

    def plan(sources, targets):
        parts = [(sources[0].at[0], targets[0])]
        for j in range(2):
            parts += row_parts(sources[1].at[0, j], 0, targets[1].at[j], far_slots, PARTS)
        return parts

    shapes = [packed_cache.shape[1:], long_cache.shape[1:]]
    return fetch(plan, 2 * PARTS + 1, [packed_cache, long_cache], shapes, after, "fetch_caches")


def down_order(peers):
    return (0, 1), tuple(range(2, peers))


def column_chunks(width):
    edge = COLUMNS // 2
    starts = [0] + list(range(edge, width - edge, COLUMNS)) + [width - edge]
    return [(a, b - a) for a, b in zip(starts, starts[1:] + [width]) if b > a]


def split_parts(value):
    high = value.astype(jnp.bfloat16)
    low = (value - high.astype(jnp.float32)).astype(jnp.bfloat16)
    return high, low


def sum_squares(values):
    floats = values.astype(jnp.float32)
    return jnp.sum(floats * floats, axis=-1, keepdims=True)


def in_lanes(columns):
    rows = columns[0].shape[0]
    lane = lax.broadcasted_iota(jnp.int32, (rows, LANES), 1)
    block = jnp.zeros((rows, LANES), jnp.float32)
    for i, column in enumerate(columns):
        high, low = split_parts(column)
        block = jnp.where(lane == 2 * i, high.astype(jnp.float32), block)
        block = jnp.where(lane == 2 * i + 1, low.astype(jnp.float32), block)
    return block


def from_lanes(block, i):
    return block[:, 2 * i : 2 * i + 1] + block[:, 2 * i + 1 : 2 * i + 2]


def row_scale(squares):
    return lax.rsqrt(squares / MODEL_WIDTH + EPSILON)


def expand_rows(scaled, wide_ref):
    rows, columns = scaled.shape
    chunk = 2 * LANES
    source = lax.broadcasted_iota(jnp.int32, (chunk, 2 * chunk), 0)
    target = lax.broadcasted_iota(jnp.int32, (chunk, 2 * chunk), 1)
    count = columns // chunk
    stacked = jnp.concatenate([scaled[:, c * chunk : (c + 1) * chunk] for c in range(count)], 0)
    for half in range(2):
        select = jnp.where(target == 2 * source + half, 1.0, 0.0).astype(jnp.bfloat16)
        spread = jnp.dot(stacked, select, preferred_element_type=jnp.float32).astype(jnp.bfloat16)
        for c in range(count):
            wide_ref[half * rows : (half + 1) * rows, 2 * c * chunk : 2 * (c + 1) * chunk] = spread[
                c * rows : (c + 1) * rows
            ]


def scale_columns(values, gain):
    return (values.astype(jnp.float32) * gain.astype(jnp.float32)).astype(jnp.bfloat16)


def multiply_halves(others, add, resident, refs):
    count = len(others)
    input_refs, refs = refs[:count], refs[count:]
    (gain_ref, weight_ref), refs = refs[:2], refs[2:]
    if add:
        (partial_ref, squares_ref), refs = refs[:2], refs[2:]
    if resident:
        rest, (wide, total) = refs[:-2], refs[-2:]
        weights = weight_ref
    else:
        rest, (wide, total, weights, sems) = refs[:-4], refs[-4:]
    half = input_refs[0].shape[1]
    starts = [pl.multiple_of(half_start(other, half), half) for other in others]
    chunks = column_chunks(total.shape[1])
    copies = [[] for _ in chunks]
    if not resident:
        for c, (start, width) in enumerate(chunks):
            for p, first in enumerate(starts):
                copy = pltpu.make_async_copy(
                    weight_ref.at[0, pl.ds(first, half), :, pl.ds(start, width)],
                    weights.at[pl.ds(p * half, half), :, pl.ds(start, width)],
                    sems.at[p, c],
                )
                copies[c].append(copy)
    for copy in sum(copies[:2], []):
        copy.start()
    scaled = [
        scale_columns(ref[...], gain_ref[:, pl.ds(first, half)])
        for ref, first in zip(input_refs, starts)
    ]
    expand_rows(jnp.concatenate(scaled, 1), wide)
    squares = sum(sum_squares(ref[...]) for ref in input_refs)
    if add:
        squares = squares + squares_ref[:, 0:1]

    def fill():
        for c, (start, width) in enumerate(chunks):
            for copy in copies[c]:
                copy.wait()
            for copy in sum(copies[c + 2 : c + 3], []):
                copy.start()
            lanes = slice(start, start + width)
            result = jnp.dot(
                wide[...],
                weights[:, :, lanes].reshape(wide.shape[1], width),
                preferred_element_type=jnp.float32,
            )
            total[:, lanes] = result + partial_ref[:, lanes] if add else result

    return rest, squares, total, fill


def partial_kernel(*refs):
    (partial_out, squares_out), squares, total, fill = multiply_halves((False,), False, True, refs)
    squares_out[...] = jnp.broadcast_to(squares, squares_out.shape)
    fill()
    partial_out[...] = total[...]


def qkv_kernel(peers, others, add, resident, *refs):
    (table_ref, *outs), squares, total, fill = multiply_halves(others, add, resident, refs)
    group = lax.axis_index("req")
    rows = squares.shape[0]
    blocks = rows // peers
    far = peers // 2 * blocks
    width = total.shape[1]
    long_squares = [jnp.broadcast_to(squares[r : r + 1], squares.shape) for r in (0, far)]
    sums = in_lanes([squares] + long_squares)
    high, low = split_parts(table_ref[0:1])
    table = jnp.concatenate(
        [high.astype(jnp.float32), low.astype(jnp.float32), jnp.zeros((blocks - 2, LANES), jnp.float32)], 0
    ).astype(jnp.bfloat16)
    fill()
    heads = QUERY_HEADS // KEY_VALUE_HEADS
    long_queries = [
        jnp.concatenate(
            [
                total[k * rows + r : k * rows + r + 1, h * HEAD_SIZE : (h + 1) * HEAD_SIZE]
                for k in range(2)
                for h in range(heads)
            ],
            0,
        ).astype(jnp.bfloat16)
        for r in (0, far)
    ]
    for d, out in enumerate(outs):
        peer = pl.multiple_of(lax.bitwise_xor(group, d) * blocks, blocks)
        for k in range(2):
            out[:, k * width : (k + 1) * width] = total[pl.ds(k * rows + peer, blocks)].astype(
                jnp.bfloat16
            )
        out[:, 2 * width + LANES : 2 * width + 2 * LANES] = table
        for j in range(2):
            first = 2 * width + (2 + j) * LANES
            out[:, first : first + LANES] = long_queries[j]
    total[0:rows, 0:LANES] = sums
    for d, out in enumerate(outs):
        peer = pl.multiple_of(lax.bitwise_xor(group, d) * blocks, blocks)
        out[:, 2 * width : 2 * width + LANES] = total[pl.ds(peer, blocks), 0:LANES].astype(jnp.bfloat16)


def multiply_quarters(distance, wide, weight_refs, partial_ref, sums, out):
    rows, width = sums.shape[0], out.shape[1] - LANES
    start = pl.multiple_of(lax.bitwise_xor(lax.axis_index("req"), distance) * width, LANES)
    result = partial_ref[:, pl.ds(start, width)]
    depth = wide.shape[1] // len(weight_refs)
    for i, weights in enumerate(weight_refs):
        result = result + jnp.dot(
            wide[:, i * depth : (i + 1) * depth],
            weights[:, :, pl.ds(start, width)].reshape(depth, width),
            preferred_element_type=jnp.float32,
        )
    out[:, 0:width] = result.astype(jnp.bfloat16)
    out[0:rows, width:] = sums
    out[rows:, width:] = sums


def gate_up_first_kernel(distance, input_ref, gain_ref, *refs):
    *weight_refs, partial_ref, squares_ref, out, wide, sums_out = refs
    half = input_ref.shape[1]
    first = pl.multiple_of(half_start(True, half), half)
    expand_rows(scale_columns(input_ref[...], gain_ref[:, pl.ds(first, half)]), wide)
    squares = squares_ref[:, 0:1] + sum_squares(input_ref[...])
    sums = in_lanes([squares]).astype(jnp.bfloat16)
    sums_out[...] = sums
    multiply_quarters(distance, wide, weight_refs, partial_ref, sums, out)


def gate_up_next_kernel(distance, wide, sums_ref, *refs):
    *weight_refs, partial_ref, out = refs
    multiply_quarters(distance, wide, weight_refs, partial_ref, sums_ref[...], out)


def project_pairs(kernel, resident, inputs, gain, weight, partial, extra, out_shapes, name):
    rows, half = inputs[0].shape
    pair, width = weight.shape[-2:]
    depth = len(inputs) * half
    operands = [*inputs, gain, weight, *partial, *extra]
    weight_spec = in_vmem(1) if resident else in_hbm(1)
    specs = in_vmem(len(inputs) + 1) + weight_spec + in_vmem(len(partial) + len(extra))
    scratch = [
        pltpu.VMEM((pair * rows, pair * depth), jnp.bfloat16),
        pltpu.VMEM((pair * rows, width), jnp.float32),
    ]
    if not resident:
        scratch += [
            pltpu.VMEM((depth, pair, width), jnp.bfloat16),
            pltpu.SemaphoreType.DMA((len(inputs), len(column_chunks(width)))),
        ]
    return pl.pallas_call(
        kernel,
        out_shape=out_shapes,
        in_specs=specs,
        out_specs=in_vmem(len(out_shapes)),
        scratch_shapes=scratch,
        compiler_params=params(14 if resident else 24),
        name=name,
    )(*operands)


def project_early(own, gain, weights, tokens, name):
    rows, half = own.shape
    pair, width = weights.shape[-2:]
    shapes = [
        jax.ShapeDtypeStruct((pair * rows, width), jnp.float32),
        jax.ShapeDtypeStruct((rows, LANES), jnp.float32),
    ]
    return pl.pallas_call(
        ordered(tokens, partial_kernel),
        out_shape=shapes,
        in_specs=in_any(len(tokens)) + in_vmem(3),
        out_specs=in_vmem(2),
        scratch_shapes=[
            pltpu.VMEM((pair * rows, pair * half), jnp.bfloat16),
            pltpu.VMEM((pair * rows, width), jnp.float32),
        ],
        compiler_params=params(14),
        name=name,
    )(*tokens, own, gain, weights)


def project_qkv(own, other, gain, weight, fetched, tokens, table, peers):
    blocks = own.shape[0] // peers
    shapes = [jax.ShapeDtypeStruct((blocks, 2 * weight.shape[3] + 4 * LANES), jnp.bfloat16)] * peers
    if fetched is None:
        kernel = functools.partial(qkv_kernel, peers, (False, True), False, False)
        return project_pairs(kernel, False, [own, other], gain, weight, [], [table], shapes, "project_qkv")
    partial = project_early(own, gain, fetched[0], tokens, "project_qkv_early")
    kernel = functools.partial(qkv_kernel, peers, (True,), True, True)
    return project_pairs(kernel, True, [other], gain, fetched[1], partial, [table], shapes, "project_qkv")


def exchange_gate_up(section, own, other, gain, fetched, quarters, peers):
    rows, half = own.shape
    shape = jax.ShapeDtypeStruct((2 * rows, quarters[0].shape[2] // peers + LANES), jnp.bfloat16)
    partial, squares = project_early(own, gain, fetched, [], "project_gate_up_early")
    count = len(quarters)
    farthest, wide, sums = pl.pallas_call(
        functools.partial(gate_up_first_kernel, peers - 1),
        out_shape=[
            shape,
            jax.ShapeDtypeStruct((2 * rows, 2 * half), jnp.bfloat16),
            jax.ShapeDtypeStruct((rows, LANES), jnp.bfloat16),
        ],
        in_specs=in_vmem(4 + count),
        out_specs=in_vmem(3),
        compiler_params=params(10),
        name="project_gate_up_first",
    )(other, gain, *quarters, partial, squares)
    received = {peers - 1: swap(farthest, "req", peers - 1, section)}
    tokens = [wide]
    for d in [*range(1, peers - 1), 0]:
        if d == 0:
            tokens.append(received[peers - 1])
        term = pl.pallas_call(
            ordered(tokens, functools.partial(gate_up_next_kernel, d)),
            out_shape=shape,
            in_specs=in_any(len(tokens)) + in_vmem(3 + count),
            out_specs=pl.BlockSpec(memory_space=pltpu.VMEM),
            compiler_params=params(10),
            name="project_gate_up_next",
        )(*tokens, wide, sums, *quarters, partial)
        received[d] = term if d == 0 else swap(term, "req", d, section)
        tokens = [term]
    return [received[d] for d in range(peers)]


def fold_lanes(values, combine):
    blocks = [values[:, i : i + LANES] for i in range(0, values.shape[1], LANES)]
    while len(blocks) > 1:
        pairs = [combine(a, b) for a, b in zip(blocks[::2], blocks[1::2])]
        blocks = pairs + blocks[2 * len(pairs) :]
    return blocks[0]


def attention_kernel(peers, resident, *refs):
    piece_refs, refs = refs[:peers], refs[peers:]
    table_ref, starts, lengths, split, packed_ref, long_ref, out_ref = refs[:7]
    (queries, keys, values, scores, far_scores, far_state, far_sum, merged_rows) = refs[7:15]
    packed, far, packed_sem, far_sems = (packed_ref, long_ref, None, None) if resident else refs[15:]
    group = lax.axis_index("req")
    blocks = out_ref.shape[0]
    heads = QUERY_HEADS // KEY_VALUE_HEADS
    pairs = 2 * heads
    window = scores.shape[2] // 2
    slots = packed.shape[0]
    far_chunks = far.shape[1] // FAR_SLOTS
    scale = 1.0 / math.sqrt(HEAD_SIZE)
    live = [split[0, 0], split[1, 0]]

    def far_copy(j, c):
        return pltpu.make_async_copy(
            long_ref.at[0, j, pl.ds(c * FAR_SLOTS, FAR_SLOTS)],
            far.at[j, pl.ds(c * FAR_SLOTS, FAR_SLOTS)],
            far_sems.at[j, c],
        )

    if not resident:
        packed_copy = pltpu.make_async_copy(packed_ref.at[0], packed, packed_sem)
        packed_copy.start()

    width = HEAD_SIZE * (heads + 2)

    def summed_block(start):
        return sum(piece[:, start : start + LANES].astype(jnp.float32) for piece in piece_refs)

    sums = summed_block(2 * width)
    scale_rows = row_scale(from_lanes(sums, 0))
    tables = [
        piece[:, 2 * width + LANES : 2 * width + 2 * LANES].astype(jnp.float32) for piece in piece_refs
    ]
    tables = [t[0:1] + t[1:2] for t in tables]
    far_tables = [
        sum(
            jnp.where(lax.bitwise_xor(group, d) == j * (peers // 2), t, 0.0)
            for d, t in enumerate(tables)
        )
        for j in range(2)
    ]
    def cosine_sine(table):
        turned = pltpu.roll(table, HEAD_SIZE // 2, 1)
        lower = lax.broadcasted_iota(jnp.int32, table.shape, 1) < HEAD_SIZE // 2
        return jnp.where(lower, table, turned), jnp.where(lower, -turned, table)

    def rotated(block, angles):
        cosine, sine = angles
        return block * cosine + pltpu.roll(block, HEAD_SIZE // 2, 1) * sine

    own_angles = cosine_sine(table_ref[...])
    far_queries = [
        rotated(
            summed_block(2 * width + (2 + j) * LANES) * row_scale(from_lanes(sums, 1 + j)),
            cosine_sine(jnp.broadcast_to(far_tables[j], table_ref.shape)),
        ).astype(jnp.bfloat16)
        for j in range(2)
    ]
    for k in range(2):
        for b in range(heads + 2):
            block = summed_block(k * width + b * HEAD_SIZE) * scale_rows
            if b <= heads:
                block = rotated(block, own_angles)
            block = block.astype(jnp.bfloat16).astype(jnp.float32)
            if b < heads:
                queries[:, k * heads + b, :] = block
            else:
                for h in range(heads):
                    (keys if b == heads else values)[:, k * heads + h, :] = block

    def same_head(rows, columns):
        row = lax.broadcasted_iota(jnp.int32, (rows, columns), 0)
        column = lax.broadcasted_iota(jnp.int32, (rows, columns), 1)
        return (row % pairs // heads) == (column % 2), column // 2 + row // pairs * (columns // 2)

    def contract(a, b):
        return lax.dot_general(a, b, (((1,), (1,)), ((), ())), preferred_element_type=jnp.float32)

    def diagonal(a, b):
        zeros = jnp.zeros_like(a)
        return jnp.concatenate(
            [jnp.concatenate([a, zeros], 1), jnp.concatenate([zeros, b], 1)], 0
        )

    def beside(ref, firsts, count, lanes):
        return jnp.concatenate(
            [ref[pl.ds(first, count), :, lanes].reshape(2 * count, HEAD_SIZE) for first in firsts], 1
        )

    key_lanes, value_lanes = slice(0, HEAD_SIZE), slice(HEAD_SIZE, 2 * HEAD_SIZE)

    if not resident:
        packed_copy.wait()
        for j in range(2):
            for c in range(far_chunks):

                @pl.when(c * FAR_SLOTS < live[j])
                def _():
                    far_copy(j, c).start()

    matching, slot = same_head(pairs, 2 * window)
    first_slots = [jnp.minimum(starts[r], slots - window) for r in range(blocks)]
    for r in range(0, blocks, 2):
        found = contract(
            diagonal(queries[r].astype(jnp.bfloat16), queries[r + 1].astype(jnp.bfloat16)),
            beside(packed, first_slots[r : r + 2], window, key_lanes),
        ) * scale
        for i in range(2):
            low = starts[r + i] - first_slots[r + i]
            inside = matching & (slot >= low) & (slot < low + lengths[r + i])
            scores[r + i] = jnp.where(inside, found[i * pairs : (i + 1) * pairs], LOWEST)
    own_score = jnp.sum(queries[...] * keys[...], axis=-1, keepdims=True) * scale
    row_max = jnp.maximum(jnp.max(scores[...], axis=-1, keepdims=True), own_score)
    weights = jnp.exp(scores[...] - row_max).astype(jnp.bfloat16)
    own_weight = jnp.exp(own_score - row_max).astype(jnp.bfloat16).astype(jnp.float32)
    totals = jnp.sum(weights.astype(jnp.float32), axis=-1, keepdims=True) + own_weight
    near_peak = row_max[0] + jnp.log(totals[0])
    for r in range(0, blocks, 2):
        summed = jnp.dot(
            jnp.concatenate([weights[r], weights[r + 1]], 0),
            beside(packed, first_slots[r : r + 2], window, value_lanes),
            preferred_element_type=jnp.float32,
        )
        for i in range(2):
            part = summed[i * pairs : (i + 1) * pairs, i * HEAD_SIZE : (i + 1) * HEAD_SIZE]
            merged_rows[r + i] = (part + own_weight[r + i] * values[r + i]) / totals[r + i]

    matching, slot = same_head(2 * pairs, FAR_SLOTS)
    log_totals = []
    for j in range(2):
        long_rows = diagonal(far_queries[j], far_queries[j])
        far_state[0] = jnp.full((2 * pairs, LANES), LOWEST, jnp.float32)
        far_state[1] = jnp.zeros((2 * pairs, LANES), jnp.float32)
        far_sum[...] = jnp.zeros_like(far_sum)

        def rows_of(c, lanes):
            first = c * FAR_SLOTS
            return beside(far.at[j], (first, first + FAR_SLOTS // 2), FAR_SLOTS // 2, lanes)

        for c in range(far_chunks):

            @pl.when(c * FAR_SLOTS < live[j])
            def _():
                if not resident:
                    far_copy(j, c).wait()
                found = contract(long_rows, rows_of(c, key_lanes)) * scale
                found = jnp.where(matching & (slot < live[j] - c * FAR_SLOTS), found, LOWEST)
                far_scores[c] = found
                far_state[0] = jnp.maximum(far_state[0], fold_lanes(found, jnp.maximum))

        peak = jnp.max(far_state[0], axis=-1, keepdims=True)
        peak = jnp.maximum(peak[:pairs], peak[pairs:])
        peaks = jnp.concatenate([peak, peak], 0)
        for c in range(far_chunks):

            @pl.when(c * FAR_SLOTS < live[j])
            def _():
                weight = jnp.exp(far_scores[c] - peaks).astype(jnp.bfloat16)
                far_state[1] = far_state[1] + fold_lanes(weight.astype(jnp.float32), jnp.add)
                summed = jnp.dot(weight, rows_of(c, value_lanes), preferred_element_type=jnp.float32)
                far_sum[...] = far_sum[...] + (
                    summed[:pairs, :HEAD_SIZE] + summed[pairs:, HEAD_SIZE:]
                )

        total = jnp.sum(far_state[1], axis=-1, keepdims=True)
        total = total[:pairs] + total[pairs:]
        summed = far_sum[...]
        far_peak = peak + jnp.log(total)
        result = summed / total
        owner = group == j * (peers // 2)
        top = jnp.maximum(far_peak, near_peak)
        far_part = jnp.exp(far_peak - top)
        near_part = jnp.exp(near_peak - top)
        both = far_part + near_part
        result = jnp.where(owner, (result * far_part + merged_rows[0] * near_part) / both, result)
        log_total = jnp.where(owner, top + jnp.log(both), far_peak)
        out_ref[:, (pairs + j) * LANES : (pairs + j + 1) * LANES] = result.astype(jnp.bfloat16)
        log_totals.append(log_total)
    out_ref[:, (pairs + 2) * LANES :] = in_lanes(log_totals).astype(jnp.bfloat16)
    for b in range(pairs):
        out_ref[:, b * HEAD_SIZE : (b + 1) * HEAD_SIZE] = merged_rows[:, b, :].astype(jnp.bfloat16)


def attend(pieces, table, starts, lengths, split, packed_cache, long_cache, resident, tokens):
    peers = len(pieces)
    blocks = pieces[0].shape[0]
    heads = QUERY_HEADS // KEY_VALUE_HEADS
    pairs = 2 * heads
    slots = packed_cache.shape[-3]
    far_slots = long_cache.shape[-3]
    scratch = [
        pltpu.VMEM((blocks, pairs, HEAD_SIZE), jnp.float32),
        pltpu.VMEM((blocks, pairs, HEAD_SIZE), jnp.float32),
        pltpu.VMEM((blocks, pairs, HEAD_SIZE), jnp.float32),
        pltpu.VMEM((blocks, pairs, 2 * MOST_SLOTS), jnp.float32),
        pltpu.VMEM((far_slots // FAR_SLOTS, 2 * pairs, FAR_SLOTS), jnp.float32),
        pltpu.VMEM((2, 2 * pairs, LANES), jnp.float32),
        pltpu.VMEM((pairs, HEAD_SIZE), jnp.float32),
        pltpu.VMEM((blocks, pairs, HEAD_SIZE), jnp.float32),
    ]
    if not resident:
        scratch += [
            pltpu.VMEM((slots, 2, 2 * HEAD_SIZE), jnp.bfloat16),
            pltpu.VMEM((2, far_slots, 2, 2 * HEAD_SIZE), jnp.bfloat16),
            pltpu.SemaphoreType.DMA,
            pltpu.SemaphoreType.DMA((2, far_slots // FAR_SLOTS)),
        ]
    return pl.pallas_call(
        ordered(tokens, functools.partial(attention_kernel, peers, resident)),
        out_shape=jax.ShapeDtypeStruct((blocks, (pairs + 3) * HEAD_SIZE), jnp.bfloat16),
        in_specs=in_any(len(tokens))
        + in_vmem(peers + 1)
        + in_smem(3)
        + (in_vmem(2) if resident else in_hbm(2)),
        out_specs=pl.BlockSpec(memory_space=pltpu.VMEM),
        scratch_shapes=scratch,
        compiler_params=params(14 if resident else 34),
        name="attend",
    )(*tokens, *pieces, table, starts, lengths, split, packed_cache, long_cache)


def multiply_columns(rows_of, weights, write):
    for start, width in column_chunks(weights.shape[1]):
        lanes = slice(start, start + width)
        write(lanes, jnp.dot(rows_of[...], weights[:, lanes], preferred_element_type=jnp.float32))


def output_early_kernel(peers, *refs):
    piece_refs, refs = refs[:peers], refs[peers:]
    weights, out_ref, whole = refs
    group = lax.axis_index("req")
    blocks = piece_refs[0].shape[0]
    depth = weights.shape[0]
    pairs = depth // LANES
    for d, piece in enumerate(piece_refs):
        start = pl.multiple_of(lax.bitwise_xor(group, d) * blocks, blocks)
        whole[pl.ds(start, blocks)] = piece[:, 0:depth]
    ends = [piece[:, depth:].astype(jnp.float32) for piece in piece_refs]
    for j in range(2):
        peaks = [from_lanes(end[:, 2 * LANES :], j) for end in ends]
        top = functools.reduce(jnp.maximum, peaks)
        parts = [jnp.exp(peak - top) for peak in peaks]
        merged = sum(end[:, j * LANES : (j + 1) * LANES] * part for end, part in zip(ends, parts))
        merged = merged / sum(parts)
        merged_row = jnp.concatenate([merged[i : i + 1] for i in range(pairs)], 1)
        rows = slice(j * (peers // 2) * blocks, j * (peers // 2) * blocks + blocks)
        row = lax.broadcasted_iota(jnp.int32, (blocks, depth), 0)
        whole[rows] = jnp.where(
            row == 0, merged_row, whole[rows].astype(jnp.float32)
        ).astype(jnp.bfloat16)

    def write(lanes, result):
        out_ref[:, lanes] = result.astype(jnp.bfloat16)

    multiply_columns(whole, weights, write)


def output_late_kernel(whole, weights, out_ref):
    def write(lanes, result):
        out_ref[:, lanes] = result.astype(jnp.bfloat16)

    multiply_columns(whole, weights, write)


def project_output(pieces, weights, token):
    rows = len(pieces) * pieces[0].shape[0]
    depth, half = weights[0].shape
    shape = jax.ShapeDtypeStruct((rows, half), jnp.bfloat16)
    sent, whole = pl.pallas_call(
        ordered([token], functools.partial(output_early_kernel, len(pieces))),
        out_shape=[shape, jax.ShapeDtypeStruct((rows, depth), jnp.bfloat16)],
        in_specs=in_any(1) + in_vmem(len(pieces) + 1),
        out_specs=in_vmem(2),
        compiler_params=params(12),
        name="project_output_sent",
    )(token, *pieces, weights[0])
    kept = pl.pallas_call(
        output_late_kernel,
        out_shape=shape,
        in_specs=in_vmem(2),
        out_specs=pl.BlockSpec(memory_space=pltpu.VMEM),
        compiler_params=params(12),
        name="project_output_kept",
    )(whole, weights[1])
    return sent, kept


def down_kernel(count, other, *refs):
    piece_refs, (weights, *refs) = refs[:count], refs[count:]
    partial_ref = None if other is None else refs.pop(0)
    out_ref, whole = refs
    units = piece_refs[0].shape[1]
    width = weights.shape[1]
    first = 0 if other is None else pl.multiple_of(half_start(other, width), width)
    for p, piece in enumerate(piece_refs):
        whole[:, p * units : (p + 1) * units] = piece[...]

    def write(lanes, result):
        if other is not None:
            start = pl.multiple_of(first + lanes.start, LANES)
            result = result + partial_ref[:, pl.ds(start, lanes.stop - lanes.start)]
        out_ref[:, lanes] = result.astype(out_ref.dtype)

    multiply_columns(whole, weights, write)


def call_down(other, pieces, weights, partial, tokens, name):
    rows = pieces[0].shape[0]
    depth, width = weights.shape
    dtype = jnp.float32 if other is None else jnp.bfloat16
    return pl.pallas_call(
        ordered(tokens, functools.partial(down_kernel, len(pieces), other)),
        out_shape=jax.ShapeDtypeStruct((rows, width), dtype),
        in_specs=in_any(len(tokens)) + in_vmem(len(pieces) + 1 + len(partial)),
        out_specs=pl.BlockSpec(memory_space=pltpu.VMEM),
        scratch_shapes=[pltpu.VMEM((rows, depth), jnp.bfloat16)],
        compiler_params=params(12),
        name=name,
    )(*tokens, *pieces, weights, *partial)


def project_down(pieces, weights, token):
    early, late = down_order(len(pieces))
    partial = call_down(None, [pieces[d] for d in early], weights[0], [], [], "project_down_early")
    rest = [pieces[d] for d in late]
    sent = call_down(True, rest, weights[1], [partial], [token], "project_down_sent")
    kept = call_down(False, rest, weights[2], [partial], [], "project_down_kept")
    return sent, kept


def hidden_kernel(peers, *refs):
    piece_refs, out_ref = refs[:peers], refs[peers]
    rows, width = out_ref.shape
    sums = sum(piece[0:rows, width:].astype(jnp.float32) for piece in piece_refs)
    factor = row_scale(from_lanes(sums, 0))

    def summed(first):
        return sum(piece[first : first + rows, 0:width].astype(jnp.float32) for piece in piece_refs) * factor

    gate, up = summed(0), summed(rows)
    out_ref[...] = (gate / (1.0 + jnp.exp(-gate)) * up).astype(jnp.bfloat16)


def gated_units(pieces, token):
    rows, width = pieces[0].shape[0] // 2, pieces[0].shape[1] - LANES
    return pl.pallas_call(
        ordered([token], functools.partial(hidden_kernel, len(pieces))),
        out_shape=jax.ShapeDtypeStruct((rows, width), jnp.bfloat16),
        in_specs=in_any(1) + in_vmem(len(pieces)),
        out_specs=pl.BlockSpec(memory_space=pltpu.VMEM),
        compiler_params=params(8),
        name="gated_units",
    )(token, *pieces)


def residual_kernel(base, terms, out):
    out[...] = (base[...].astype(jnp.float32) + terms[...]).astype(jnp.bfloat16)


def add_residual(base, terms, token):
    return pl.pallas_call(
        ordered([token], residual_kernel),
        out_shape=jax.ShapeDtypeStruct(base.shape, jnp.bfloat16),
        in_specs=in_any(1) + in_vmem(2),
        out_specs=pl.BlockSpec(memory_space=pltpu.VMEM),
        compiler_params=params(4),
        name="add_residual",
    )(token, base, terms)


def fast_layer(section, own, other, fetched, attention_gain, query_key_value_weight, out_weight, feedforward_gain, gate_up, down_weight, packed_cache, long_cache, table, *segments):
    req_count = lax.axis_size("req")
    qkv_fetched, out_fetched, caches, tokens, passed = fetched or (None, None, None, [], None)
    terms = project_qkv(
        own, other, attention_gain, query_key_value_weight, qkv_fetched, tokens, table, req_count
    )
    terms = swap_all(terms, "req", section)
    first_quarter, token = fetch_quarter(gate_up, 0, terms[1], "fetch_gate_up_first")
    if fetched is None:
        *out_fetched, out_token = fetch_output(out_weight, terms[1])
        attended = attend(terms, table, *segments, packed_cache, long_cache, False, [token, out_token])
    else:
        attended = attend(terms, table, *segments, *caches, True, [token, passed])
    pieces = spread(attended, "req", section)
    second_quarter, token = fetch_quarter(gate_up, 1, pieces[1], "fetch_gate_up_second")
    sent, kept = project_output(pieces, out_fetched, token)
    pair = sum_pair(sent, kept, "head", section)
    gate_fetched, token = fetch_halves(gate_up, (False,), pair, "fetch_gate_up")
    residual = add_residual(own, sum_doubling(pair, "head", section), token)
    other_residual = swap(residual, "head", 1, section)
    quarters = [first_quarter, second_quarter]
    terms = exchange_gate_up(
        section, residual, other_residual, feedforward_gain, gate_fetched, quarters, req_count
    )
    down_early, token = fetch_down(down_weight, req_count, True, terms[1], "fetch_down_early")
    hidden = spread(gated_units(terms, token), "req", section)
    *down_late, token = fetch_down(down_weight, req_count, False, hidden[1], "fetch_down_late")
    sent, kept = project_down(hidden, [down_early, *down_late], token)
    lowered = sum_doubling(sum_pair(sent, kept, "head", section), "head", section)
    return (residual.astype(jnp.float32) + lowered).astype(jnp.bfloat16)


def rope_table(lengths):
    req_count, group = lax.axis_size("req"), lax.axis_index("req")
    owner = (group == 0) | (group == req_count // 2)
    long_row = (jnp.arange(lengths.shape[1]) == 0) & owner
    position = lengths[0] + jnp.where(long_row, LONG, 0).astype(jnp.int32)
    half_dim = HEAD_SIZE // 2
    inverse = 1.0 / 10000.0 ** (jnp.arange(half_dim).astype(jnp.float32) * 2.0 / HEAD_SIZE)
    angles = position.astype(jnp.float32)[:, None] * inverse[None, :]
    return jnp.concatenate([jnp.cos(angles), jnp.sin(angles)], 1)


def fast_local(tokens, attention_gain, query_key_value_weight, head_output_weight, feedforward_gain, gate_up, down_weight, packed_cache, long_cache, lengths, long_split):
    out_weight = head_output_weight.reshape(-1, head_output_weight.shape[3])
    query_key_value_weight, out_weight, gate_up, down_weight, packed_cache, long_cache = [
        pltpu.with_memory_space_constraint(array, pltpu.HBM)
        for array in (query_key_value_weight, out_weight, gate_up, down_weight, packed_cache, long_cache)
    ]
    layer_arrays = (
        attention_gain,
        query_key_value_weight,
        out_weight,
        feedforward_gain,
        gate_up,
        down_weight,
        packed_cache,
        long_cache,
        rope_table(lengths),
        jnp.cumsum(lengths[0]) - lengths[0],
        lengths[0],
        long_split,
    )
    half = tokens.shape[1] // 2
    own, other = [lax.dynamic_slice_in_dim(tokens, half_start(o, half), half, 1) for o in (False, True)]
    first = fast_layer(0, own, other, None, *layer_arrays)
    own, other = [swap(first, "head", d, 0, 1) for d in range(2)]
    *qkv_fetched, qkv_token = fetch_halves(query_key_value_weight, (False, True), first, "fetch_qkv")
    *out_fetched, out_token = fetch_output(out_weight, first)
    *caches, caches_token = fetch_caches(packed_cache, long_cache, first)
    first_other = swap(first, "head", 1, 0)
    tokens = [qkv_token, out_token, caches_token]
    fetched = (qkv_fetched, out_fetched, caches, tokens, first_other)
    second = fast_layer(1, own, other, fetched, *layer_arrays)
    second_other = swap(second, "head", 1, 1)
    is_first = lax.axis_index("section") == 0
    own, other = jnp.where(is_first, first, second), jnp.where(is_first, first_other, second_other)
    own_first = half_start(False, half) == 0
    return jnp.where(
        own_first, jnp.concatenate([own, other], 1), jnp.concatenate([other, own], 1)
    )[None]


def is_power_of_two(value):
    return value & (value - 1) == 0


def fits_fast(mesh):
    req_count, head_count = mesh.shape["req"], mesh.shape["head"]
    columns = MODEL_WIDTH // req_count // 2
    return (
        mesh.shape["section"] == 2
        and is_power_of_two(req_count)
        and is_power_of_two(head_count)
        and req_count >= 4
        and head_count >= 2
        and KEY_VALUE_HEADS == 2 * head_count
        and columns % COLUMNS == 0
        and FF % (head_count * COLUMNS) == 0
        and FF % (head_count * req_count * LANES) == 0
    )


def solution(mesh):
    placed = (
        P(None, "req"),
        P("section", "req"),
        P("section", "req", "head", None),
        P("section", "head", None, "req"),
        P("section", "req"),
        P("section", "req", None, "head"),
        P("section", "head", "req"),
        P("section", "req", "head", None),
        P("section", None, "req", "head", None),
        P("req", None),
        P(None, "req"),
    )
    return jax.shard_map(
        fast_local if fits_fast(mesh) else local,
        mesh=mesh,
        in_specs=placed, out_specs=P("section", None, "req"), check_vma=False
    )
```

```python
import functools
import math

import jax
import jax.numpy as jnp
from jax import lax
from jax.experimental import pallas as pl
from jax.experimental.pallas import tpu as pltpu
from jax.sharding import PartitionSpec as P

MODEL_WIDTH = 8192
QUERY_HEADS = 64
KEY_VALUE_HEADS = 8
HEAD_SIZE = 128
LONG = 16384
FF = 14336
MOST_SLOTS = 256
LANES = 128
COLUMNS = 512
FAR_SLOTS = 2048
LOWEST = -1e30
PARTS = 4


EPSILON = 1e-05


def merged(part, axis, combine):
    gathered = jax.tree.map(lambda a: lax.all_gather(a, axis), part)

    def take(source):
        return jax.tree.map(lambda a: lax.dynamic_index_in_dim(a, source, 0, False), gathered)

    return lax.fori_loop(
        1, lax.axis_size(axis), lambda source, state: combine(state, take(source)), take(0)
    )


def shifted(value, axis, by):
    peers = lax.axis_size(axis)
    pairs = [(i, i + by) for i in range(peers) if 0 <= i + by < peers]
    return lax.ppermute(value, axis, pairs)


def rotate(values, position):
    half_dim = values.shape[-1] // 2
    freq_ids = jnp.arange(half_dim).astype(jnp.float32)
    inverse = 1.0 / 10000.0 ** (freq_ids * 2.0 / values.shape[-1])
    angles = position.astype(jnp.float32)[:, None] * inverse[None, :]
    cosine = jnp.cos(angles)[:, None, None, :]
    sine_part = jnp.sin(angles)[:, None, None, :]
    lower_half = values[..., :half_dim]
    upper_half = values[..., half_dim:]
    return jnp.concatenate(
        [
            lower_half * cosine - upper_half * sine_part,
            upper_half * cosine + lower_half * sine_part,
        ],
        -1,
    )


def add_pair(earlier, second_part):
    return earlier + second_part


def combine_partial(earlier, second_part):
    peak = jnp.maximum(earlier[0], second_part[0])
    left_factor = jnp.exp(earlier[0] - peak)
    right_factor = jnp.exp(second_part[0] - peak)
    softmax_total = earlier[1] * left_factor + second_part[1] * right_factor
    weighted_sum = earlier[2] * left_factor[..., None] + second_part[2] * right_factor[..., None]
    return (peak, softmax_total, weighted_sum)


def over_requests(values, combiner):
    return merged(values, "req", combiner)


def rows_apply(values, row_fn):
    return row_fn(lax.all_gather(values, "req", axis=0, tiled=True), jnp.int32(0))


def rows_project(term_fn, row_count):
    return lax.psum_scatter(
        term_fn(jnp.int32(0), row_count * lax.axis_size("req")),
        "req",
        scatter_dimension=0,
        tiled=True,
    )


def head_total(values):
    return lax.psum(values, "head")


def keep_rows(piece_rows, start_row):
    return piece_rows


def norm_rows(values, gain_row):
    floats = values.astype(jnp.float32)
    squares = over_requests(jnp.sum(floats * floats, axis=-1), add_pair)
    return (
        floats * lax.rsqrt(squares / MODEL_WIDTH + EPSILON)[:, None] * gain_row.astype(jnp.float32)
    ).astype(jnp.bfloat16)


def decoder_layer(
    inputs,
    micro_batch,
    attention_gain,
    query_key_value_weight,
    head_output_weight,
    feedforward_gain,
    gate_up,
    down_weight,
    packed_cache,
    long_cache,
    lengths,
    long_split,
):
    req_count = lax.axis_size("req")
    group_index = lax.axis_index("req")
    blocks = inputs.shape[0] // req_count
    columns = query_key_value_weight.shape[1]
    kv_local = query_key_value_weight.shape[2]
    requests_per_group = QUERY_HEADS // KEY_VALUE_HEADS
    score_scale = 1.0 / math.sqrt(HEAD_SIZE)
    normalized_input = norm_rows(inputs, attention_gain[0])
    in_weights = query_key_value_weight[0].reshape(
        columns, kv_local * (requests_per_group + 2) * HEAD_SIZE
    )

    def qkv_term(start_row, row_count):
        return jnp.dot(normalized_input, in_weights, preferred_element_type=jnp.float32)

    projected_rows = rows_project(qkv_term, blocks).reshape(
        blocks, kv_local, requests_per_group + 2, HEAD_SIZE
    )
    local_rows = jnp.arange(blocks)
    row_lengths = lengths[0]
    owner_long = (group_index == 0) | (group_index == req_count // 2)
    long_row = (local_rows == 0) & (micro_batch == 0) & owner_long
    position = row_lengths + jnp.where(long_row, LONG, 0).astype(jnp.int32)
    queries = rotate(projected_rows[:, :, :requests_per_group], position).astype(jnp.bfloat16)
    new_key = rotate(projected_rows[:, :, requests_per_group : requests_per_group + 1], position)[
        :, :, 0
    ].astype(jnp.bfloat16)
    new_value = projected_rows[:, :, requests_per_group + 1].astype(jnp.bfloat16)
    gathered = rows_apply(
        queries[0:1].reshape(1, kv_local * requests_per_group * HEAD_SIZE), keep_rows
    )
    long_queries = jnp.stack([gathered[0], gathered[req_count // 2]]).reshape(
        2, kv_local, requests_per_group, HEAD_SIZE
    )
    far_cache = long_cache[0]
    far_live = (jnp.arange(far_cache.shape[1])[None, :] < long_split[:, 0][:, None])[
        :, None, None, :
    ]
    far_scores = (
        jnp.einsum(
            "jkhd,jpkd->jkhp",
            long_queries,
            far_cache[..., :HEAD_SIZE],
            preferred_element_type=jnp.float32,
        )
        * score_scale
    )
    far_max = jnp.max(jnp.where(far_live, far_scores, -jnp.inf), axis=-1)
    far_weights = jnp.where(
        far_live, jnp.exp(jnp.where(far_live, far_scores - far_max[..., None], 0.0)), 0.0
    ).astype(jnp.bfloat16)
    far_totals = jnp.sum(far_weights.astype(jnp.float32), axis=-1)
    far_summed = jnp.einsum(
        "jkhp,jpkd->jkhd",
        far_weights,
        far_cache[..., HEAD_SIZE:],
        preferred_element_type=jnp.float32,
    )
    far_max, far_totals, far_summed = over_requests(
        (far_max, far_totals, far_summed), combine_partial
    )
    far_index = jnp.where(group_index == 0, 0, 1)
    chosen_max = lax.dynamic_index_in_dim(far_max, far_index, 0, keepdims=False)
    chosen_totals = lax.dynamic_index_in_dim(far_totals, far_index, 0, keepdims=False)
    chosen_summed = lax.dynamic_index_in_dim(far_summed, far_index, 0, keepdims=False)
    pack_part = packed_cache[0]
    seg_ends = jnp.cumsum(lengths[0])
    slot_ids = jnp.arange(pack_part.shape[0])
    slot_owner = jnp.sum((slot_ids[:, None] >= seg_ends[None, :]).astype(jnp.int32), axis=1)
    request_ids = micro_batch * blocks + local_rows
    in_segment = (slot_owner[None, :] == request_ids[:, None])[:, None, None, :]
    scores = (
        jnp.einsum(
            "rkhd,pkd->rkhp",
            queries,
            pack_part[..., :HEAD_SIZE],
            preferred_element_type=jnp.float32,
        )
        * score_scale
    )
    own_score = (
        jnp.einsum("rkhd,rkd->rkh", queries, new_key, preferred_element_type=jnp.float32)
        * score_scale
    )
    row_max = jnp.maximum(jnp.max(jnp.where(in_segment, scores, -jnp.inf), axis=-1), own_score)
    long_mask = long_row[:, None, None]
    row_max = jnp.where(long_mask, jnp.maximum(row_max, chosen_max[None]), row_max)
    weights = jnp.where(
        in_segment, jnp.exp(jnp.where(in_segment, scores - row_max[..., None], 0.0)), 0.0
    ).astype(jnp.bfloat16)
    own_weights = jnp.exp(own_score - row_max).astype(jnp.bfloat16)
    far_factor = jnp.where(
        long_mask, jnp.exp(jnp.where(long_mask, chosen_max[None] - row_max, 0.0)), 0.0
    )
    softmax_total = (
        jnp.sum(weights.astype(jnp.float32), axis=-1)
        + own_weights.astype(jnp.float32)
        + far_factor * chosen_totals[None]
    )
    weighted_sum = jnp.einsum(
        "rkhp,pkd->rkhd", weights, pack_part[..., HEAD_SIZE:], preferred_element_type=jnp.float32
    )
    weighted_sum = (
        weighted_sum
        + own_weights.astype(jnp.float32)[..., None] * new_value.astype(jnp.float32)[:, :, None, :]
    )
    weighted_sum = weighted_sum + far_factor[..., None] * chosen_summed[None]
    attended_heads = (
        (weighted_sum / softmax_total[..., None])
        .astype(jnp.bfloat16)
        .reshape(blocks, kv_local * requests_per_group * HEAD_SIZE)
    )
    out_weights = head_output_weight[0].reshape(kv_local * requests_per_group * HEAD_SIZE, columns)

    def project_heads(piece_rows, start_row):
        return jnp.dot(piece_rows, out_weights, preferred_element_type=jnp.float32)

    attended = head_total(rows_apply(attended_heads, project_heads))
    residual = (inputs.astype(jnp.float32) + attended).astype(jnp.bfloat16)
    normed_two = norm_rows(residual, feedforward_gain[0])
    ff_weights = gate_up[0].reshape(columns, -1)

    def ff_term(start_row, row_count):
        return jnp.dot(normed_two, ff_weights, preferred_element_type=jnp.float32)

    gate_and_up = rows_project(ff_term, blocks)
    hidden_width = gate_and_up.shape[1] // 2
    hidden = (jax.nn.silu(gate_and_up[:, :hidden_width]) * gate_and_up[:, hidden_width:]).astype(
        jnp.bfloat16
    )
    lower_weights = down_weight[0]

    def project_hidden(piece_rows, start_row):
        return jnp.dot(piece_rows, lower_weights, preferred_element_type=jnp.float32)

    lowered = head_total(rows_apply(hidden, project_hidden))
    return (residual.astype(jnp.float32) + lowered).astype(jnp.bfloat16)


def local(
    tokens,
    attention_gain,
    query_key_value_weight,
    head_output_weight,
    feedforward_gain,
    gate_up,
    down_weight,
    packed_cache,
    long_cache,
    lengths,
    long_split,
):
    req_count = lax.axis_size("req")
    section_index = lax.axis_index("section")
    batch_count = 1
    per_group = tokens.shape[0] // req_count
    blocks = per_group // batch_count
    columns = tokens.shape[1]
    token_grid = tokens.reshape(req_count, per_group, columns)
    result = jnp.zeros_like(token_grid)
    incoming = jnp.zeros((req_count * blocks, columns), jnp.bfloat16)
    for phase_step in range(batch_count + 1):
        micro_batch = phase_step - section_index
        is_active = (micro_batch >= 0) & (micro_batch < batch_count)
        micro_batch = jnp.clip(micro_batch, 0, batch_count - 1)
        new_batch = token_grid.reshape(req_count * blocks, columns)
        inputs = jnp.where(section_index == 0, new_batch, incoming)
        output = decoder_layer(
            inputs,
            micro_batch,
            attention_gain,
            query_key_value_weight,
            head_output_weight,
            feedforward_gain,
            gate_up,
            down_weight,
            packed_cache,
            long_cache,
            lengths,
            long_split,
        )
        placed = output.reshape(req_count, blocks, columns)
        result = jnp.where(is_active, placed, result)
        if phase_step < batch_count:
            incoming = shifted(output, "section", 1)
    return result.reshape(1, req_count * per_group, columns)

def swap(value, axis, distance, section, target_section=None):
    size = lax.axis_size(axis)
    target_section = section if target_section is None else target_section
    pairs = [(section * size + i, target_section * size + (i ^ distance)) for i in range(size)]
    return lax.ppermute(value, ("section", axis), pairs)


def swap_all(values, axis, section):
    received = {d: swap(values[d], axis, d, section) for d in reversed(range(1, len(values)))}
    return [values[0]] + [received[d] for d in range(1, len(values))]


def spread(value, axis, section):
    return swap_all([value] * lax.axis_size(axis), axis, section)


def sum_doubling(value, axis, section):
    distance = 2
    total = value.astype(jnp.float32)
    while distance < lax.axis_size(axis):
        other = swap(value, axis, distance, section)
        total = value.astype(jnp.float32) + other.astype(jnp.float32)
        value = total.astype(jnp.bfloat16)
        distance *= 2
    return total


def sum_pair(sent, kept, axis, section):
    pair = kept.astype(jnp.float32) + swap(sent, axis, 1, section).astype(jnp.float32)
    return pair.astype(jnp.bfloat16)


def half_start(other, half):
    index = lax.bitwise_and(lax.axis_index("head"), 1)
    return (1 - index if other else index) * half


def in_vmem(count):
    return [pl.BlockSpec(memory_space=pltpu.VMEM)] * count


def in_hbm(count):
    return [pl.BlockSpec(memory_space=pltpu.HBM)] * count


def in_smem(count):
    return [pl.BlockSpec(memory_space=pltpu.SMEM)] * count


def params(mebibytes):
    return pltpu.CompilerParams(vmem_limit_bytes=mebibytes * 2**20)


def in_any(count):
    return [pl.BlockSpec(memory_space=pl.ANY)] * count


def ordered(tokens, kernel):
    def run(*refs):
        kernel(*refs[len(tokens) :])

    return run


def fetch_kernel(count, plan, *refs):
    sources, refs = refs[:count], refs[count + 1 :]
    *targets, token, sems = refs
    token[...] = jnp.zeros_like(token)
    copies = [
        pltpu.make_async_copy(source, target, sems.at[i])
        for i, (source, target) in enumerate(plan(sources, targets))
    ]
    for copy in copies:
        copy.start()
    for copy in copies:
        copy.wait()


def fetch(plan, copies, arrays, shapes, after, name):
    return pl.pallas_call(
        functools.partial(fetch_kernel, len(arrays), plan),
        out_shape=[pltpu.VMEM(shape, jnp.bfloat16) for shape in shapes]
        + [jax.ShapeDtypeStruct((8, LANES), jnp.float32)],
        in_specs=in_hbm(len(arrays)) + in_any(1),
        out_specs=in_vmem(len(shapes) + 1),
        scratch_shapes=[pltpu.SemaphoreType.DMA((copies,))],
        compiler_params=params(2),
        name=name,
    )(*arrays, after)


def row_parts(source, first, target, rows, parts):
    size = rows // parts
    return [
        (source.at[pl.ds(first + i * size, size)], target.at[pl.ds(i * size, size)])
        for i in range(parts)
    ]


def fetch_halves(weight, others, after, name):
    half, shape = weight.shape[1] // 2, weight.shape[2:]

    def plan(sources, targets):
        parts = []
        for other, target in zip(others, targets):
            first = pl.multiple_of(half_start(other, half), half)
            parts += row_parts(sources[0].at[0], first, target, half, PARTS)
        return parts

    shapes = [(half, *shape)] * len(others)
    return fetch(plan, PARTS * len(others), [weight], shapes, after, name)


def fetch_quarter(weight, part, after, name):
    half, shape = weight.shape[1] // 2, weight.shape[2:]
    quarter = half // 2

    def plan(sources, targets):
        first = pl.multiple_of(half_start(True, half) + part * quarter, quarter)
        return row_parts(sources[0].at[0], first, targets[0], quarter, PARTS)

    return fetch(plan, PARTS, [weight], [(quarter, *shape)], after, name)


def fetch_output(weight, after):
    depth, half = weight.shape[0], weight.shape[1] // 2

    def plan(sources, targets):
        parts = []
        for other, target in zip((True, False), targets):
            first = pl.multiple_of(half_start(other, half), half)
            parts += row_parts(sources[0].at[:, pl.ds(first, half)], 0, target, depth, PARTS)
        return parts

    return fetch(plan, 2 * PARTS, [weight], [(depth, half)] * 2, after, "fetch_output")


def fetch_down(weight, peers, early, after, name):
    depth, width = weight.shape[1:]
    units, half = depth // peers, width // 2
    distances = down_order(peers)[0 if early else 1]
    others = (None,) if early else (True, False)

    def plan(sources, targets):
        group = lax.axis_index("req")
        parts = []
        for target, other in zip(targets, others):
            columns = target.shape[1]
            first = 0 if other is None else pl.multiple_of(half_start(other, half), half)
            for p, d in enumerate(distances):
                row = pl.multiple_of(lax.bitwise_xor(group, d) * units, LANES)
                parts.append(
                    (
                        sources[0].at[0, pl.ds(row, units), pl.ds(first, columns)],
                        target.at[pl.ds(p * units, units)],
                    )
                )
        return parts

    rows = len(distances) * units
    shapes = [(rows, width if other is None else half) for other in others]
    return fetch(plan, len(distances) * len(others), [weight], shapes, after, name)


def fetch_caches(packed_cache, long_cache, after):
    far_slots = long_cache.shape[2]

    def plan(sources, targets):
        parts = [(sources[0].at[0], targets[0])]
        for j in range(2):
            parts += row_parts(sources[1].at[0, j], 0, targets[1].at[j], far_slots, PARTS)
        return parts

    shapes = [packed_cache.shape[1:], long_cache.shape[1:]]
    return fetch(plan, 2 * PARTS + 1, [packed_cache, long_cache], shapes, after, "fetch_caches")


def down_order(peers):
    return (0, 1), tuple(range(2, peers))


def column_chunks(width):
    edge = COLUMNS // 2
    starts = [0] + list(range(edge, width - edge, COLUMNS)) + [width - edge]
    return [(a, b - a) for a, b in zip(starts, starts[1:] + [width]) if b > a]


def split_parts(value):
    high = value.astype(jnp.bfloat16)
    low = (value - high.astype(jnp.float32)).astype(jnp.bfloat16)
    return high, low


def sum_squares(values):
    floats = values.astype(jnp.float32)
    return jnp.sum(floats * floats, axis=-1, keepdims=True)


def in_lanes(columns):
    rows = columns[0].shape[0]
    lane = lax.broadcasted_iota(jnp.int32, (rows, LANES), 1)
    block = jnp.zeros((rows, LANES), jnp.float32)
    for i, column in enumerate(columns):
        high, low = split_parts(column)
        block = jnp.where(lane == 2 * i, high.astype(jnp.float32), block)
        block = jnp.where(lane == 2 * i + 1, low.astype(jnp.float32), block)
    return block


def from_lanes(block, i):
    return block[:, 2 * i : 2 * i + 1] + block[:, 2 * i + 1 : 2 * i + 2]


def row_scale(squares):
    return lax.rsqrt(squares / MODEL_WIDTH + EPSILON)


def expand_rows(scaled, wide_ref):
    rows, columns = scaled.shape
    chunk = 2 * LANES
    source = lax.broadcasted_iota(jnp.int32, (chunk, 2 * chunk), 0)
    target = lax.broadcasted_iota(jnp.int32, (chunk, 2 * chunk), 1)
    count = columns // chunk
    stacked = jnp.concatenate([scaled[:, c * chunk : (c + 1) * chunk] for c in range(count)], 0)
    for half in range(2):
        select = jnp.where(target == 2 * source + half, 1.0, 0.0).astype(jnp.bfloat16)
        spread = jnp.dot(stacked, select, preferred_element_type=jnp.float32).astype(jnp.bfloat16)
        for c in range(count):
            wide_ref[half * rows : (half + 1) * rows, 2 * c * chunk : 2 * (c + 1) * chunk] = spread[
                c * rows : (c + 1) * rows
            ]


def scale_columns(values, gain):
    return (values.astype(jnp.float32) * gain.astype(jnp.float32)).astype(jnp.bfloat16)


def multiply_halves(others, add, resident, refs):
    count = len(others)
    input_refs, refs = refs[:count], refs[count:]
    (gain_ref, weight_ref), refs = refs[:2], refs[2:]
    if add:
        (partial_ref, squares_ref), refs = refs[:2], refs[2:]
    if resident:
        rest, (wide, total) = refs[:-2], refs[-2:]
        weights = weight_ref
    else:
        rest, (wide, total, weights, sems) = refs[:-4], refs[-4:]
    half = input_refs[0].shape[1]
    starts = [
        0 if other is None else pl.multiple_of(half_start(other, half), half) for other in others
    ]
    chunks = column_chunks(total.shape[1])
    copies = [[] for _ in chunks]
    if not resident:
        for c, (start, width) in enumerate(chunks):
            for p, first in enumerate(starts):
                copy = pltpu.make_async_copy(
                    weight_ref.at[0, pl.ds(first, half), :, pl.ds(start, width)],
                    weights.at[pl.ds(p * half, half), :, pl.ds(start, width)],
                    sems.at[p, c],
                )
                copies[c].append(copy)
    for copy in sum(copies, []):
        copy.start()
    scaled = [
        scale_columns(ref[...], gain_ref[:, pl.ds(first, half)])
        for ref, first in zip(input_refs, starts)
    ]
    expand_rows(jnp.concatenate(scaled, 1), wide)
    squares = sum(sum_squares(ref[...]) for ref in input_refs)
    if add:
        squares = squares + squares_ref[:, 0:1]

    def fill():
        for c, (start, width) in enumerate(chunks):
            for copy in copies[c]:
                copy.wait()
            lanes = slice(start, start + width)
            result = jnp.dot(
                wide[...],
                weights[:, :, lanes].reshape(wide.shape[1], width),
                preferred_element_type=jnp.float32,
            )
            total[:, lanes] = result + partial_ref[:, lanes] if add else result

    return rest, squares, total, fill


def partial_kernel(*refs):
    (partial_out, squares_out), squares, total, fill = multiply_halves((False,), False, True, refs)
    squares_out[...] = jnp.broadcast_to(squares, squares_out.shape)
    fill()
    partial_out[...] = total[...]


def qkv_kernel(peers, others, add, resident, *refs):
    (table_ref, *outs), squares, total, fill = multiply_halves(others, add, resident, refs)
    group = lax.axis_index("req")
    rows = squares.shape[0]
    blocks = rows // peers
    far = peers // 2 * blocks
    width = total.shape[1]
    long_squares = [jnp.broadcast_to(squares[r : r + 1], squares.shape) for r in (0, far)]
    sums = in_lanes([squares] + long_squares)
    high, low = split_parts(table_ref[0:1])
    table = jnp.concatenate(
        [high.astype(jnp.float32), low.astype(jnp.float32), jnp.zeros((blocks - 2, LANES), jnp.float32)], 0
    ).astype(jnp.bfloat16)
    fill()
    heads = QUERY_HEADS // KEY_VALUE_HEADS
    long_queries = [
        jnp.concatenate(
            [
                total[k * rows + r : k * rows + r + 1, h * HEAD_SIZE : (h + 1) * HEAD_SIZE]
                for k in range(2)
                for h in range(heads)
            ],
            0,
        ).astype(jnp.bfloat16)
        for r in (0, far)
    ]
    for d, out in enumerate(outs):
        peer = pl.multiple_of(lax.bitwise_xor(group, d) * blocks, blocks)
        for k in range(2):
            out[:, k * width : (k + 1) * width] = total[pl.ds(k * rows + peer, blocks)].astype(
                jnp.bfloat16
            )
        out[:, 2 * width + LANES : 2 * width + 2 * LANES] = table
        for j in range(2):
            first = 2 * width + (2 + j) * LANES
            out[:, first : first + LANES] = long_queries[j]
    total[0:rows, 0:LANES] = sums
    for d, out in enumerate(outs):
        peer = pl.multiple_of(lax.bitwise_xor(group, d) * blocks, blocks)
        out[:, 2 * width : 2 * width + LANES] = total[pl.ds(peer, blocks), 0:LANES].astype(jnp.bfloat16)


def multiply_quarters(distance, wide, weight_refs, partial_ref, sums, out):
    rows, width = sums.shape[0], out.shape[1] - LANES
    start = pl.multiple_of(lax.bitwise_xor(lax.axis_index("req"), distance) * width, LANES)
    result = partial_ref[:, pl.ds(start, width)]
    depth = wide.shape[1] // len(weight_refs)
    for i, weights in enumerate(weight_refs):
        result = result + jnp.dot(
            wide[:, i * depth : (i + 1) * depth],
            weights[:, :, pl.ds(start, width)].reshape(depth, width),
            preferred_element_type=jnp.float32,
        )
    out[:, 0:width] = result.astype(jnp.bfloat16)
    out[0:rows, width:] = sums
    out[rows:, width:] = sums


def gate_up_first_kernel(distance, input_ref, gain_ref, *refs):
    *weight_refs, partial_ref, squares_ref, out, wide, sums_out = refs
    half = input_ref.shape[1]
    first = pl.multiple_of(half_start(True, half), half)
    expand_rows(scale_columns(input_ref[...], gain_ref[:, pl.ds(first, half)]), wide)
    squares = squares_ref[:, 0:1] + sum_squares(input_ref[...])
    sums = in_lanes([squares]).astype(jnp.bfloat16)
    sums_out[...] = sums
    multiply_quarters(distance, wide, weight_refs, partial_ref, sums, out)


def gate_up_next_kernel(distance, wide, sums_ref, *refs):
    *weight_refs, partial_ref, out = refs
    multiply_quarters(distance, wide, weight_refs, partial_ref, sums_ref[...], out)


def project_pairs(kernel, resident, inputs, gain, weight, partial, extra, out_shapes, name):
    rows, half = inputs[0].shape
    pair, width = weight.shape[-2:]
    depth = len(inputs) * half
    operands = [*inputs, gain, weight, *partial, *extra]
    weight_spec = in_vmem(1) if resident else in_hbm(1)
    specs = in_vmem(len(inputs) + 1) + weight_spec + in_vmem(len(partial) + len(extra))
    scratch = [
        pltpu.VMEM((pair * rows, pair * depth), jnp.bfloat16),
        pltpu.VMEM((pair * rows, width), jnp.float32),
    ]
    if not resident:
        scratch += [
            pltpu.VMEM((depth, pair, width), jnp.bfloat16),
            pltpu.SemaphoreType.DMA((len(inputs), len(column_chunks(width)))),
        ]
    return pl.pallas_call(
        kernel,
        out_shape=out_shapes,
        in_specs=specs,
        out_specs=in_vmem(len(out_shapes)),
        scratch_shapes=scratch,
        compiler_params=params(14 if resident else 24),
        name=name,
    )(*operands)


def project_early(own, gain, weights, tokens, name):
    rows, half = own.shape
    pair, width = weights.shape[-2:]
    shapes = [
        jax.ShapeDtypeStruct((pair * rows, width), jnp.float32),
        jax.ShapeDtypeStruct((rows, LANES), jnp.float32),
    ]
    return pl.pallas_call(
        ordered(tokens, partial_kernel),
        out_shape=shapes,
        in_specs=in_any(len(tokens)) + in_vmem(3),
        out_specs=in_vmem(2),
        scratch_shapes=[
            pltpu.VMEM((pair * rows, pair * half), jnp.bfloat16),
            pltpu.VMEM((pair * rows, width), jnp.float32),
        ],
        compiler_params=params(14),
        name=name,
    )(*tokens, own, gain, weights)


def project_qkv(inputs, gain, weight, fetched, tokens, table, peers):
    blocks = inputs[0].shape[0] // peers
    shapes = [jax.ShapeDtypeStruct((blocks, 2 * weight.shape[3] + 4 * LANES), jnp.bfloat16)] * peers
    if fetched is None:
        kernel = functools.partial(qkv_kernel, peers, (None,), False, False)
        return project_pairs(kernel, False, inputs, gain, weight, [], [table], shapes, "project_qkv")
    own, other = inputs
    partial = project_early(own, gain, fetched[0], tokens, "project_qkv_early")
    kernel = functools.partial(qkv_kernel, peers, (True,), True, True)
    return project_pairs(kernel, True, [other], gain, fetched[1], partial, [table], shapes, "project_qkv")


def exchange_gate_up(section, own, other, gain, fetched, quarters, peers):
    rows, half = own.shape
    shape = jax.ShapeDtypeStruct((2 * rows, quarters[0].shape[2] // peers + LANES), jnp.bfloat16)
    partial, squares = project_early(own, gain, fetched, [], "project_gate_up_early")
    count = len(quarters)
    farthest, wide, sums = pl.pallas_call(
        functools.partial(gate_up_first_kernel, peers - 1),
        out_shape=[
            shape,
            jax.ShapeDtypeStruct((2 * rows, 2 * half), jnp.bfloat16),
            jax.ShapeDtypeStruct((rows, LANES), jnp.bfloat16),
        ],
        in_specs=in_vmem(4 + count),
        out_specs=in_vmem(3),
        compiler_params=params(10),
        name="project_gate_up_first",
    )(other, gain, *quarters, partial, squares)
    received = {peers - 1: swap(farthest, "req", peers - 1, section)}
    tokens = [wide]
    for d in [*range(1, peers - 1), 0]:
        if d == 0:
            tokens.append(received[peers - 1])
        term = pl.pallas_call(
            ordered(tokens, functools.partial(gate_up_next_kernel, d)),
            out_shape=shape,
            in_specs=in_any(len(tokens)) + in_vmem(3 + count),
            out_specs=pl.BlockSpec(memory_space=pltpu.VMEM),
            compiler_params=params(10),
            name="project_gate_up_next",
        )(*tokens, wide, sums, *quarters, partial)
        received[d] = term if d == 0 else swap(term, "req", d, section)
        tokens = [term]
    return [received[d] for d in range(peers)]


def fold_lanes(values, combine):
    blocks = [values[:, i : i + LANES] for i in range(0, values.shape[1], LANES)]
    while len(blocks) > 1:
        pairs = [combine(a, b) for a, b in zip(blocks[::2], blocks[1::2])]
        blocks = pairs + blocks[2 * len(pairs) :]
    return blocks[0]


def attention_kernel(peers, resident, *refs):
    piece_refs, refs = refs[:peers], refs[peers:]
    table_ref, starts, lengths, split, packed_ref, long_ref, out_ref = refs[:7]
    (queries, keys, values, scores, far_scores, far_state, far_sum, merged_rows) = refs[7:15]
    packed, far, packed_sem, far_sems = (packed_ref, long_ref, None, None) if resident else refs[15:]
    group = lax.axis_index("req")
    blocks = out_ref.shape[0]
    heads = QUERY_HEADS // KEY_VALUE_HEADS
    pairs = 2 * heads
    window = scores.shape[2] // 2
    slots = packed.shape[0]
    far_chunks = far.shape[1] // FAR_SLOTS
    scale = 1.0 / math.sqrt(HEAD_SIZE)
    live = [split[0, 0], split[1, 0]]

    def far_copy(j, c):
        return pltpu.make_async_copy(
            long_ref.at[0, j, pl.ds(c * FAR_SLOTS, FAR_SLOTS)],
            far.at[j, pl.ds(c * FAR_SLOTS, FAR_SLOTS)],
            far_sems.at[j, c],
        )

    if not resident:
        packed_copy = pltpu.make_async_copy(packed_ref.at[0], packed, packed_sem)
        packed_copy.start()

    width = HEAD_SIZE * (heads + 2)

    def summed_block(start):
        return sum(piece[:, start : start + LANES].astype(jnp.float32) for piece in piece_refs)

    sums = summed_block(2 * width)
    scale_rows = row_scale(from_lanes(sums, 0))
    tables = [
        piece[:, 2 * width + LANES : 2 * width + 2 * LANES].astype(jnp.float32) for piece in piece_refs
    ]
    tables = [t[0:1] + t[1:2] for t in tables]
    far_tables = [
        sum(
            jnp.where(lax.bitwise_xor(group, d) == j * (peers // 2), t, 0.0)
            for d, t in enumerate(tables)
        )
        for j in range(2)
    ]
    def cosine_sine(table):
        turned = pltpu.roll(table, HEAD_SIZE // 2, 1)
        lower = lax.broadcasted_iota(jnp.int32, table.shape, 1) < HEAD_SIZE // 2
        return jnp.where(lower, table, turned), jnp.where(lower, -turned, table)

    def rotated(block, angles):
        cosine, sine = angles
        return block * cosine + pltpu.roll(block, HEAD_SIZE // 2, 1) * sine

    own_angles = cosine_sine(table_ref[...])
    far_queries = [
        rotated(
            summed_block(2 * width + (2 + j) * LANES) * row_scale(from_lanes(sums, 1 + j)),
            cosine_sine(jnp.broadcast_to(far_tables[j], table_ref.shape)),
        ).astype(jnp.bfloat16)
        for j in range(2)
    ]
    for k in range(2):
        for b in range(heads + 2):
            block = summed_block(k * width + b * HEAD_SIZE) * scale_rows
            if b <= heads:
                block = rotated(block, own_angles)
            block = block.astype(jnp.bfloat16).astype(jnp.float32)
            if b < heads:
                queries[:, k * heads + b, :] = block
            else:
                for h in range(heads):
                    (keys if b == heads else values)[:, k * heads + h, :] = block

    def same_head(rows, columns):
        row = lax.broadcasted_iota(jnp.int32, (rows, columns), 0)
        column = lax.broadcasted_iota(jnp.int32, (rows, columns), 1)
        return (row % pairs // heads) == (column % 2), column // 2 + row // pairs * (columns // 2)

    def contract(a, b):
        return lax.dot_general(a, b, (((1,), (1,)), ((), ())), preferred_element_type=jnp.float32)

    def diagonal(a, b):
        zeros = jnp.zeros_like(a)
        return jnp.concatenate(
            [jnp.concatenate([a, zeros], 1), jnp.concatenate([zeros, b], 1)], 0
        )

    def beside(ref, firsts, count, lanes):
        return jnp.concatenate(
            [ref[pl.ds(first, count), :, lanes].reshape(2 * count, HEAD_SIZE) for first in firsts], 1
        )

    key_lanes, value_lanes = slice(0, HEAD_SIZE), slice(HEAD_SIZE, 2 * HEAD_SIZE)

    if not resident:
        packed_copy.wait()
        for j in range(2):
            for c in range(far_chunks):

                @pl.when(c * FAR_SLOTS < live[j])
                def _():
                    far_copy(j, c).start()

    matching, slot = same_head(pairs, 2 * window)
    first_slots = [jnp.minimum(starts[r], slots - window) for r in range(blocks)]
    for r in range(blocks):
        low = starts[r] - first_slots[r]
        segment = packed[pl.ds(first_slots[r], window), :, key_lanes].reshape(2 * window, HEAD_SIZE)
        found = contract(queries[r].astype(jnp.bfloat16), segment) * scale
        inside = matching & (slot >= low) & (slot < low + lengths[r])
        scores[r] = jnp.where(inside, found, LOWEST)
    own_score = jnp.sum(queries[...] * keys[...], axis=-1, keepdims=True) * scale
    row_max = jnp.maximum(jnp.max(scores[...], axis=-1, keepdims=True), own_score)
    weights = jnp.exp(scores[...] - row_max).astype(jnp.bfloat16)
    own_weight = jnp.exp(own_score - row_max).astype(jnp.bfloat16).astype(jnp.float32)
    totals = jnp.sum(weights.astype(jnp.float32), axis=-1, keepdims=True) + own_weight
    near_peak = row_max[0] + jnp.log(totals[0])
    for r in range(blocks):
        segment = packed[pl.ds(first_slots[r], window), :, value_lanes].reshape(2 * window, HEAD_SIZE)
        summed = jnp.dot(weights[r], segment, preferred_element_type=jnp.float32)
        merged_rows[r] = (summed + own_weight[r] * values[r]) / totals[r]

    matching, slot = same_head(2 * pairs, FAR_SLOTS)
    log_totals = []
    for j in range(2):
        long_rows = diagonal(far_queries[j], far_queries[j])
        far_state[0] = jnp.full((2 * pairs, LANES), LOWEST, jnp.float32)
        far_state[1] = jnp.zeros((2 * pairs, LANES), jnp.float32)
        far_sum[...] = jnp.zeros_like(far_sum)

        def rows_of(c, lanes):
            first = c * FAR_SLOTS
            return beside(far.at[j], (first, first + FAR_SLOTS // 2), FAR_SLOTS // 2, lanes)

        for c in range(far_chunks):

            @pl.when(c * FAR_SLOTS < live[j])
            def _():
                if not resident:
                    far_copy(j, c).wait()
                found = contract(long_rows, rows_of(c, key_lanes)) * scale
                found = jnp.where(matching & (slot < live[j] - c * FAR_SLOTS), found, LOWEST)
                far_scores[c] = found
                far_state[0] = jnp.maximum(far_state[0], fold_lanes(found, jnp.maximum))

        peak = jnp.max(far_state[0], axis=-1, keepdims=True)
        peak = jnp.maximum(peak[:pairs], peak[pairs:])
        peaks = jnp.concatenate([peak, peak], 0)
        for c in range(far_chunks):

            @pl.when(c * FAR_SLOTS < live[j])
            def _():
                weight = jnp.exp(far_scores[c] - peaks).astype(jnp.bfloat16)
                far_state[1] = far_state[1] + fold_lanes(weight.astype(jnp.float32), jnp.add)
                summed = jnp.dot(weight, rows_of(c, value_lanes), preferred_element_type=jnp.float32)
                far_sum[...] = far_sum[...] + (
                    summed[:pairs, :HEAD_SIZE] + summed[pairs:, HEAD_SIZE:]
                )

        total = jnp.sum(far_state[1], axis=-1, keepdims=True)
        total = total[:pairs] + total[pairs:]
        summed = far_sum[...]
        far_peak = peak + jnp.log(total)
        result = summed / total
        owner = group == j * (peers // 2)
        top = jnp.maximum(far_peak, near_peak)
        far_part = jnp.exp(far_peak - top)
        near_part = jnp.exp(near_peak - top)
        both = far_part + near_part
        result = jnp.where(owner, (result * far_part + merged_rows[0] * near_part) / both, result)
        log_total = jnp.where(owner, top + jnp.log(both), far_peak)
        out_ref[:, (pairs + j) * LANES : (pairs + j + 1) * LANES] = result.astype(jnp.bfloat16)
        log_totals.append(log_total)
    out_ref[:, (pairs + 2) * LANES :] = in_lanes(log_totals).astype(jnp.bfloat16)
    for b in range(pairs):
        out_ref[:, b * HEAD_SIZE : (b + 1) * HEAD_SIZE] = merged_rows[:, b, :].astype(jnp.bfloat16)


def attend(pieces, table, starts, lengths, split, packed_cache, long_cache, resident, tokens):
    peers = len(pieces)
    blocks = pieces[0].shape[0]
    heads = QUERY_HEADS // KEY_VALUE_HEADS
    pairs = 2 * heads
    slots = packed_cache.shape[-3]
    far_slots = long_cache.shape[-3]
    scratch = [
        pltpu.VMEM((blocks, pairs, HEAD_SIZE), jnp.float32),
        pltpu.VMEM((blocks, pairs, HEAD_SIZE), jnp.float32),
        pltpu.VMEM((blocks, pairs, HEAD_SIZE), jnp.float32),
        pltpu.VMEM((blocks, pairs, 2 * MOST_SLOTS), jnp.float32),
        pltpu.VMEM((far_slots // FAR_SLOTS, 2 * pairs, FAR_SLOTS), jnp.float32),
        pltpu.VMEM((2, 2 * pairs, LANES), jnp.float32),
        pltpu.VMEM((pairs, HEAD_SIZE), jnp.float32),
        pltpu.VMEM((blocks, pairs, HEAD_SIZE), jnp.float32),
    ]
    if not resident:
        scratch += [
            pltpu.VMEM((slots, 2, 2 * HEAD_SIZE), jnp.bfloat16),
            pltpu.VMEM((2, far_slots, 2, 2 * HEAD_SIZE), jnp.bfloat16),
            pltpu.SemaphoreType.DMA,
            pltpu.SemaphoreType.DMA((2, far_slots // FAR_SLOTS)),
        ]
    return pl.pallas_call(
        ordered(tokens, functools.partial(attention_kernel, peers, resident)),
        out_shape=jax.ShapeDtypeStruct((blocks, (pairs + 3) * HEAD_SIZE), jnp.bfloat16),
        in_specs=in_any(len(tokens))
        + in_vmem(peers + 1)
        + in_smem(3)
        + (in_vmem(2) if resident else in_hbm(2)),
        out_specs=pl.BlockSpec(memory_space=pltpu.VMEM),
        scratch_shapes=scratch,
        compiler_params=params(14 if resident else 34),
        name="attend",
    )(*tokens, *pieces, table, starts, lengths, split, packed_cache, long_cache)


def multiply_columns(rows_of, weights, write):
    for start, width in column_chunks(weights.shape[1]):
        lanes = slice(start, start + width)
        write(lanes, jnp.dot(rows_of[...], weights[:, lanes], preferred_element_type=jnp.float32))


def output_early_kernel(peers, *refs):
    piece_refs, refs = refs[:peers], refs[peers:]
    weights, out_ref, whole = refs
    group = lax.axis_index("req")
    blocks = piece_refs[0].shape[0]
    depth = weights.shape[0]
    pairs = depth // LANES
    for d, piece in enumerate(piece_refs):
        start = pl.multiple_of(lax.bitwise_xor(group, d) * blocks, blocks)
        whole[pl.ds(start, blocks)] = piece[:, 0:depth]
    ends = [piece[:, depth:].astype(jnp.float32) for piece in piece_refs]
    for j in range(2):
        peaks = [from_lanes(end[:, 2 * LANES :], j) for end in ends]
        top = functools.reduce(jnp.maximum, peaks)
        parts = [jnp.exp(peak - top) for peak in peaks]
        merged = sum(end[:, j * LANES : (j + 1) * LANES] * part for end, part in zip(ends, parts))
        merged = merged / sum(parts)
        merged_row = jnp.concatenate([merged[i : i + 1] for i in range(pairs)], 1)
        rows = slice(j * (peers // 2) * blocks, j * (peers // 2) * blocks + blocks)
        row = lax.broadcasted_iota(jnp.int32, (blocks, depth), 0)
        whole[rows] = jnp.where(
            row == 0, merged_row, whole[rows].astype(jnp.float32)
        ).astype(jnp.bfloat16)

    def write(lanes, result):
        out_ref[:, lanes] = result.astype(jnp.bfloat16)

    multiply_columns(whole, weights, write)


def output_late_kernel(whole, weights, out_ref):
    def write(lanes, result):
        out_ref[:, lanes] = result.astype(jnp.bfloat16)

    multiply_columns(whole, weights, write)


def project_output(pieces, weights, token):
    rows = len(pieces) * pieces[0].shape[0]
    depth, half = weights[0].shape
    shape = jax.ShapeDtypeStruct((rows, half), jnp.bfloat16)
    sent, whole = pl.pallas_call(
        ordered([token], functools.partial(output_early_kernel, len(pieces))),
        out_shape=[shape, jax.ShapeDtypeStruct((rows, depth), jnp.bfloat16)],
        in_specs=in_any(1) + in_vmem(len(pieces) + 1),
        out_specs=in_vmem(2),
        compiler_params=params(12),
        name="project_output_sent",
    )(token, *pieces, weights[0])
    kept = pl.pallas_call(
        output_late_kernel,
        out_shape=shape,
        in_specs=in_vmem(2),
        out_specs=pl.BlockSpec(memory_space=pltpu.VMEM),
        compiler_params=params(12),
        name="project_output_kept",
    )(whole, weights[1])
    return sent, kept


def down_kernel(count, other, *refs):
    piece_refs, (weights, *refs) = refs[:count], refs[count:]
    partial_ref = None if other is None else refs.pop(0)
    out_ref, whole = refs
    units = piece_refs[0].shape[1]
    width = weights.shape[1]
    first = 0 if other is None else pl.multiple_of(half_start(other, width), width)
    for p, piece in enumerate(piece_refs):
        whole[:, p * units : (p + 1) * units] = piece[...]

    def write(lanes, result):
        if other is not None:
            start = pl.multiple_of(first + lanes.start, LANES)
            result = result + partial_ref[:, pl.ds(start, lanes.stop - lanes.start)]
        out_ref[:, lanes] = result.astype(out_ref.dtype)

    multiply_columns(whole, weights, write)


def call_down(other, pieces, weights, partial, tokens, name):
    rows = pieces[0].shape[0]
    depth, width = weights.shape
    dtype = jnp.float32 if other is None else jnp.bfloat16
    return pl.pallas_call(
        ordered(tokens, functools.partial(down_kernel, len(pieces), other)),
        out_shape=jax.ShapeDtypeStruct((rows, width), dtype),
        in_specs=in_any(len(tokens)) + in_vmem(len(pieces) + 1 + len(partial)),
        out_specs=pl.BlockSpec(memory_space=pltpu.VMEM),
        scratch_shapes=[pltpu.VMEM((rows, depth), jnp.bfloat16)],
        compiler_params=params(12),
        name=name,
    )(*tokens, *pieces, weights, *partial)


def project_down(pieces, weights, token):
    early, late = down_order(len(pieces))
    partial = call_down(None, [pieces[d] for d in early], weights[0], [], [], "project_down_early")
    rest = [pieces[d] for d in late]
    sent = call_down(True, rest, weights[1], [partial], [token], "project_down_sent")
    kept = call_down(False, rest, weights[2], [partial], [], "project_down_kept")
    return sent, kept


def hidden_kernel(peers, *refs):
    piece_refs, out_ref = refs[:peers], refs[peers]
    rows, width = out_ref.shape
    sums = sum(piece[0:rows, width:].astype(jnp.float32) for piece in piece_refs)
    factor = row_scale(from_lanes(sums, 0))

    def summed(first):
        return sum(piece[first : first + rows, 0:width].astype(jnp.float32) for piece in piece_refs) * factor

    gate, up = summed(0), summed(rows)
    out_ref[...] = (gate / (1.0 + jnp.exp(-gate)) * up).astype(jnp.bfloat16)


def gated_units(pieces, token):
    rows, width = pieces[0].shape[0] // 2, pieces[0].shape[1] - LANES
    return pl.pallas_call(
        ordered([token], functools.partial(hidden_kernel, len(pieces))),
        out_shape=jax.ShapeDtypeStruct((rows, width), jnp.bfloat16),
        in_specs=in_any(1) + in_vmem(len(pieces)),
        out_specs=pl.BlockSpec(memory_space=pltpu.VMEM),
        compiler_params=params(8),
        name="gated_units",
    )(token, *pieces)


def residual_kernel(base, terms, out):
    out[...] = (base[...].astype(jnp.float32) + terms[...]).astype(jnp.bfloat16)


def add_residual(base, terms, token):
    return pl.pallas_call(
        ordered([token], residual_kernel),
        out_shape=jax.ShapeDtypeStruct(base.shape, jnp.bfloat16),
        in_specs=in_any(1) + in_vmem(2),
        out_specs=pl.BlockSpec(memory_space=pltpu.VMEM),
        compiler_params=params(4),
        name="add_residual",
    )(token, base, terms)


def fast_layer(section, inputs, own, fetched, attention_gain, query_key_value_weight, out_weight, feedforward_gain, gate_up, down_weight, packed_cache, long_cache, table, *segments):
    req_count = lax.axis_size("req")
    qkv_fetched, out_fetched, caches, tokens, passed = fetched or (None, None, None, [], None)
    terms = project_qkv(
        inputs, attention_gain, query_key_value_weight, qkv_fetched, tokens, table, req_count
    )
    terms = swap_all(terms, "req", section)
    first_quarter, token = fetch_quarter(gate_up, 0, terms[1], "fetch_gate_up_first")
    if fetched is None:
        *out_fetched, out_token = fetch_output(out_weight, terms[1])
        attended = attend(terms, table, *segments, packed_cache, long_cache, False, [token, out_token])
    else:
        attended = attend(terms, table, *segments, *caches, True, [token, passed])
    pieces = spread(attended, "req", section)
    second_quarter, token = fetch_quarter(gate_up, 1, pieces[1], "fetch_gate_up_second")
    sent, kept = project_output(pieces, out_fetched, token)
    pair = sum_pair(sent, kept, "head", section)
    gate_fetched, token = fetch_halves(gate_up, (False,), pair, "fetch_gate_up")
    residual = add_residual(own, sum_doubling(pair, "head", section), token)
    other_residual = swap(residual, "head", 1, section)
    quarters = [first_quarter, second_quarter]
    terms = exchange_gate_up(
        section, residual, other_residual, feedforward_gain, gate_fetched, quarters, req_count
    )
    down_early, token = fetch_down(down_weight, req_count, True, terms[1], "fetch_down_early")
    hidden = spread(gated_units(terms, token), "req", section)
    *down_late, token = fetch_down(down_weight, req_count, False, hidden[1], "fetch_down_late")
    sent, kept = project_down(hidden, [down_early, *down_late], token)
    lowered = sum_doubling(sum_pair(sent, kept, "head", section), "head", section)
    return (residual.astype(jnp.float32) + lowered).astype(jnp.bfloat16)


def rope_table(lengths):
    req_count, group = lax.axis_size("req"), lax.axis_index("req")
    owner = (group == 0) | (group == req_count // 2)
    long_row = (jnp.arange(lengths.shape[1]) == 0) & owner
    position = lengths[0] + jnp.where(long_row, LONG, 0).astype(jnp.int32)
    half_dim = HEAD_SIZE // 2
    inverse = 1.0 / 10000.0 ** (jnp.arange(half_dim).astype(jnp.float32) * 2.0 / HEAD_SIZE)
    angles = position.astype(jnp.float32)[:, None] * inverse[None, :]
    return jnp.concatenate([jnp.cos(angles), jnp.sin(angles)], 1)


def fast_local(tokens, attention_gain, query_key_value_weight, head_output_weight, feedforward_gain, gate_up, down_weight, packed_cache, long_cache, lengths, long_split):
    out_weight = head_output_weight.reshape(-1, head_output_weight.shape[3])
    query_key_value_weight, out_weight, gate_up, down_weight, packed_cache, long_cache = [
        pltpu.with_memory_space_constraint(array, pltpu.HBM)
        for array in (query_key_value_weight, out_weight, gate_up, down_weight, packed_cache, long_cache)
    ]
    layer_arrays = (
        attention_gain,
        query_key_value_weight,
        out_weight,
        feedforward_gain,
        gate_up,
        down_weight,
        packed_cache,
        long_cache,
        rope_table(lengths),
        jnp.cumsum(lengths[0]) - lengths[0],
        lengths[0],
        long_split,
    )
    half = tokens.shape[1] // 2
    own = lax.dynamic_slice_in_dim(tokens, half_start(False, half), half, 1)
    first = fast_layer(0, [tokens], own, None, *layer_arrays)
    own, other = [swap(first, "head", d, 0, 1) for d in range(2)]
    *qkv_fetched, qkv_token = fetch_halves(query_key_value_weight, (False, True), first, "fetch_qkv")
    *out_fetched, out_token = fetch_output(out_weight, first)
    *caches, caches_token = fetch_caches(packed_cache, long_cache, first)
    first_other = swap(first, "head", 1, 0)
    tokens = [qkv_token, out_token, caches_token]
    fetched = (qkv_fetched, out_fetched, caches, tokens, first_other)
    second = fast_layer(1, [own, other], own, fetched, *layer_arrays)
    second_other = swap(second, "head", 1, 1)
    is_first = lax.axis_index("section") == 0
    own, other = jnp.where(is_first, first, second), jnp.where(is_first, first_other, second_other)
    own_first = half_start(False, half) == 0
    return jnp.where(
        own_first, jnp.concatenate([own, other], 1), jnp.concatenate([other, own], 1)
    )[None]


def is_power_of_two(value):
    return value & (value - 1) == 0


def fits_fast(mesh):
    req_count, head_count = mesh.shape["req"], mesh.shape["head"]
    columns = MODEL_WIDTH // req_count // 2
    return (
        mesh.shape["section"] == 2
        and is_power_of_two(req_count)
        and is_power_of_two(head_count)
        and req_count >= 4
        and head_count >= 2
        and KEY_VALUE_HEADS == 2 * head_count
        and columns % COLUMNS == 0
        and FF % (head_count * COLUMNS) == 0
        and FF % (head_count * req_count * LANES) == 0
    )


def solution(mesh):
    placed = (
        P(None, "req"),
        P("section", "req"),
        P("section", "req", "head", None),
        P("section", "head", None, "req"),
        P("section", "req"),
        P("section", "req", None, "head"),
        P("section", "head", "req"),
        P("section", "req", "head", None),
        P("section", None, "req", "head", None),
        P("req", None),
        P(None, "req"),
    )
    return jax.shard_map(
        fast_local if fits_fast(mesh) else local,
        mesh=mesh,
        in_specs=placed, out_specs=P("section", None, "req"), check_vma=False
    )
```
